128 devices in a mesh: section: 2 (over x_lo), dp: 32 (over y, z, core), tensor: 2 (over x_hi).
Axes of the slice: x: 4 (x_hi: 2, x_lo: 2; x = x_hi * 2 + x_lo), y: 4, z: 4, core: 2. Of those that a mesh axis runs over, the one named last changes fastest.
Arguments:
- tokens_in: bfloat16 [2, 8192, 768], P(None, ('dp', 'tensor')), may hold values from -6 to 6
- cotangent: bfloat16 [2, 8192, 768], P(None, ('dp', 'tensor')), may hold values from -6 to 6
- place: int32 [32], replicated, may hold values from 0 to 31, each once
- w_qkv: bfloat16 [2, 3, 768, 768], P('section', None, 'dp', 'tensor'), may hold values from -0.21875 to 0.21875
- w_out: bfloat16 [2, 768, 768], P('section', 'tensor', 'dp'), may hold values from -1.75 to 1.75
- w_up: bfloat16 [2, 768, 3072], P('section', 'dp', 'tensor'), may hold values from -0.21875 to 0.21875
- w_down: bfloat16 [2, 3072, 768], P('section', 'tensor', 'dp'), may hold values from -0.109375 to 0.109375
- qv_bias: bfloat16 [2, 2, 768], P('section', None, 'tensor'), may hold values from -0.59765625 to 0.59765625
- up_bias: bfloat16 [2, 3072], P('section', 'tensor'), may hold values from -3 to 3
- vectors: bfloat16 [2, 6, 768], P('section'), may hold values from -1.5 to 2
Outputs:
- acts: bfloat16 [2, 2, 8192, 768], P('section', None, ('dp', 'tensor'))
- input_grads: float32 [2, 2, 8192, 768], P('section', None, ('dp', 'tensor'))
- grad_w_qkv: float32 [2, 3, 768, 768], P('section', None, 'dp', 'tensor')
- grad_w_out: float32 [2, 768, 768], P('section', 'tensor', 'dp')
- grad_w_up: float32 [2, 768, 3072], P('section', 'dp', 'tensor')
- grad_w_down: float32 [2, 3072, 768], P('section', 'tensor', 'dp')
- grad_qv_bias: float32 [2, 2, 768], P('section', None, 'tensor')
- grad_up_bias: float32 [2, 3072], P('section', 'tensor')
- grad_vectors: float32 [2, 6, 768], P('section')
The draws below stay inside these ranges and needn't reach their ends.
Inputs may be any that keep to these rules, and one draw needn't show every extreme that they name: A permutation; block d of every micro-batch is part place[d] mod 8 of sequence place[d] div 8.
All inputs are finite; a program needn't handle non-finite values.
Results may differ from the reference program's by a relative error of at most 0.017.
Values may be sent and summed in bfloat16 or wider, within the bound.
A program may use at most 256 MiB of HBM per device.

```python
import jax
import jax.numpy as jnp
from jax import lax

D = 768
HEADS = 12
HEAD_DIM = 64
FF = 3072
TOK_DEV = 256
PIECES = 8
MICRO = 2
LAYERS = 2
BLOCKS = 32
SEQS = 4
TOKENS = 8192


def draw_vectors(key, part):
    key = jax.random.fold_in(key, 7)
    noise_field = jnp.clip(jax.random.normal(key, (LAYERS, 6, D), jnp.float32), -5.0, 5.0)
    row_index = jnp.arange(6)[None, :, None]
    is_gain = (row_index == 0) | (row_index == 3)
    return jnp.where(is_gain, 1.0 + 0.2 * noise_field, 0.3 * noise_field).astype(jnp.bfloat16)


def shard_levels(rng, dims, cuts, least, top_value):
    gain, own = 1.0, jax.random.fold_in(rng, 6)
    for dim, parts in cuts:
        heights = jnp.exp(jax.random.uniform(jax.random.fold_in(own, dim), (parts,), jnp.float32, least / len(cuts), top_value / len(cuts)))
        gain = gain * jnp.repeat(heights, dims[dim] // parts).reshape([-1 if axis == dim else 1 for axis in range(len(dims))])
    return gain


def noise(own_key, shape, scale, most, cuts=(), held_as=jnp.bfloat16):
    entries = scale * jax.random.normal(own_key, shape, jnp.float32)
    if cuts:
        entries = entries * shard_levels(own_key, shape, cuts, -0.22, 0.18)
    return jnp.clip(entries, -most, most).astype(held_as)


def setup_inputs(seed: int = 0) -> dict:
    seeds = jax.random.split(jax.random.key(seed), 11)
    tokens_in = noise(seeds[0], (MICRO, TOKENS, D), 1.0, 6.0, ((1, 64),))
    cotangent = noise(seeds[1], (MICRO, TOKENS, D), 1.0, 6.0, ((1, 64),))
    place = jax.random.permutation(seeds[2], BLOCKS).astype(jnp.int32)
    w_qkv = noise(seeds[3], (LAYERS, 3, D, D), D ** -0.5, 0.21875, ((0, 2), (2, 32), (3, 2)))
    w_out = noise(seeds[4], (LAYERS, D, D), (D // 64) ** -0.5, 1.75, ((0, 2), (1, 2), (2, 32)))
    w_up = noise(seeds[5], (LAYERS, D, FF), D ** -0.5, 0.21875, ((0, 2), (1, 32), (2, 2)))
    w_down = noise(seeds[6], (LAYERS, FF, D), FF ** -0.5, 0.109375, ((0, 2), (1, 2), (2, 32)))
    qv_bias = noise(seeds[7], (LAYERS, 2, D), 0.1, 0.59765625, ((0, 2), (2, 2)))
    up_bias = noise(seeds[8], (LAYERS, FF), 0.5, 3.0, ((0, 2), (1, 2)))
    vectors = draw_vectors(jax.random.fold_in(seeds[10], 71), 0)
    return {"tokens_in": tokens_in, "cotangent": cotangent, "place": place, "w_qkv": w_qkv, "w_out": w_out, "w_up": w_up, "w_down": w_down, "qv_bias": qv_bias, "up_bias": up_bias, "vectors": vectors}


@jax.custom_vjp
def low(v):
    return lax.optimization_barrier(v.astype(jnp.bfloat16)).astype(jnp.float32)

@jax.custom_vjp
def low_back(v):
    return v

def low_keep(v):
    return (low(v), None)

def low_pass(kept, grad):
    return (grad,)

def back_keep(v):
    return (v, None)

def back_low(kept, grad):
    return (low(grad),)
low.defvjp(low_keep, low_pass)
low_back.defvjp(back_keep, back_low)
highest = lax.Precision.HIGHEST
epsilon = 1e-05
masked_value = -1e+30

def matmul(left, right):
    return jnp.dot(left, right, precision=highest, preferred_element_type=jnp.float32)

def normalize(residual, gain_row, shift_row):
    average = lax.optimization_barrier(jnp.mean(residual, axis=-1, keepdims=True))
    centred = residual - average
    spread = lax.optimization_barrier(jnp.mean(centred * centred, axis=-1, keepdims=True))
    return centred * lax.rsqrt(spread + epsilon) * gain_row + shift_row

def attend(triple):
    query_heads, key_heads, value_heads = triple
    place_seq = jnp.arange(query_heads.shape[0])
    scores = low_back(jnp.einsum('qhd,khd->hqk', query_heads, key_heads, precision=highest))
    allowed = (place_seq[:, None] >= place_seq[None, :])[None]
    attention = jax.nn.softmax(jnp.where(allowed, scores, masked_value), axis=-1)
    return jnp.einsum('hqk,khd->qhd', low(attention), value_heads, precision=highest)

def decoder_layer(residual, w_qkv, w_out, w_up, w_down, qv_bias, up_bias, vectors):
    score_scale = HEAD_DIM ** (-0.5)
    normed = low(normalize(residual, vectors[0], vectors[1]))
    query_rows = low(low_back((matmul(normed, w_qkv[0]) + qv_bias[0]) * score_scale))
    key_rows = low(low_back(matmul(normed, w_qkv[1])))
    value_rows = low(low_back(matmul(normed, w_qkv[2]) + qv_bias[1]))
    head_shape = (SEQS, PIECES * TOK_DEV, HEADS, HEAD_DIM)
    mixed_heads = lax.map(jax.checkpoint(attend), (query_rows.reshape(head_shape), key_rows.reshape(head_shape), value_rows.reshape(head_shape)))
    mixed_heads = low(low_back(mixed_heads.reshape(TOKENS, D)))
    hidden = residual + low_back(matmul(mixed_heads, w_out) + vectors[2])
    normed_two = low(normalize(hidden, vectors[3], vectors[4]))
    pre_active = low_back(matmul(normed_two, w_up) + up_bias)
    active = low(jax.nn.gelu(pre_active, approximate=False))
    return hidden + matmul(active, w_down) + vectors[5]

def reference(tokens_in, cotangent, place, w_qkv, w_out, w_up, w_down, qv_bias, up_bias, vectors):
    inverse = jnp.zeros((BLOCKS,), jnp.int32).at[place].set(jnp.arange(BLOCKS, dtype=jnp.int32))

    def to_sequence(rows_in):
        return rows_in.reshape(BLOCKS, TOK_DEV, -1)[inverse].reshape(TOKENS, -1)

    def from_sequence(rows_in):
        return rows_in.reshape(BLOCKS, TOK_DEV, -1)[place].reshape(TOKENS, -1)
    params = [tuple((array[layer_index].astype(jnp.float32) for array in (w_qkv, w_out, w_up, w_down, qv_bias, up_bias, vectors))) for layer_index in range(LAYERS)]
    acts_all = []
    input_all = []
    accrued = None
    for micro_index in range(MICRO):
        entering = to_sequence(tokens_in[micro_index].astype(jnp.float32))
        backers = []
        layer_acts = []
        for layer_index in range(LAYERS):
            leaving, backer = jax.vjp(decoder_layer, entering, *params[layer_index])
            backers.append(backer)
            entering = low(leaving)
            layer_acts.append(from_sequence(entering).astype(jnp.bfloat16))
        carried = to_sequence(cotangent[micro_index].astype(jnp.float32))
        layer_inputs = [None] * LAYERS
        layer_grads = [None] * LAYERS
        for layer_index in reversed(range(LAYERS)):
            results = backers[layer_index](carried)
            layer_inputs[layer_index] = from_sequence(results[0])
            layer_grads[layer_index] = results[1:]
            carried = low(results[0])
        stacked = tuple((jnp.stack([layer_grads[layer_index][which] for layer_index in range(LAYERS)]) for which in range(7)))
        accrued = stacked if accrued is None else tuple((first + second for first, second in zip(accrued, stacked)))
        acts_all.append(jnp.stack(layer_acts))
        input_all.append(jnp.stack(layer_inputs))
    acts = jnp.stack(acts_all, axis=1)
    input_grads = jnp.stack(input_all, axis=1)
    return (acts, input_grads, accrued[0], accrued[1], accrued[2], accrued[3], accrued[4], accrued[5], accrued[6])
```

```python
import jax, jax.numpy as jnp
from jax import lax
from jax.experimental import pallas as pl
from jax.experimental.pallas import tpu as pltpu
from jax.sharding import Mesh, PartitionSpec as P
MESH = pl.DeviceIdType.MESH
ORDERS = ("xyz", "yzx", "zxy")


class Spot:
    def __init__(self):
        self.s, self.y, self.z, self.c, self.t = (lax.axis_index(a) for a in "syzct")
        self.x = self.t * 2 + self.s

    def at(self, axis):
        return {"x": self.x, "y": self.y, "z": self.z}[axis]

    def shifted(self, axis, by):
        return lax.rem(self.at(axis) + (by + 4), 4)

    def device(self, axis, by):
        x, y, z = self.x, self.y, self.z
        moved = self.shifted(axis, by)
        if axis == "x":
            x = moved
        elif axis == "y":
            y = moved
        else:
            z = moved
        return (lax.rem(x, 2), y, z, self.c, lax.div(x, 2))

    def sibling(self):
        return (self.s, self.y, self.z, 1 - self.c, self.t)


class Copies:
    def __init__(self, send_sems, recv_sems):
        self.send_sems, self.recv_sems, self.count = send_sems, recv_sems, 0
        self.sent = []

    def make(self, src, dst, device):
        n = self.count
        self.count += 1
        copy = pltpu.make_async_remote_copy(
            src_ref=src, dst_ref=dst, send_sem=self.send_sems.at[n], recv_sem=self.recv_sems.at[n],
            device_id=device, device_id_type=MESH)
        self.sent.append(copy)
        return copy

    def start(self, src, dst, device):
        copy = self.make(src, dst, device)
        copy.start()
        return copy

    def finish(self):
        for copy in self.sent:
            copy.wait_send()


def greet(spot, with_sibling):
    barrier = pltpu.get_barrier_semaphore()
    peers = [spot.device(axis, by) for axis in "xyz" for by in (1, -1)]
    if with_sibling:
        peers.append(spot.sibling())
    for peer in peers:
        pl.semaphore_signal(barrier, inc=1, device_id=peer, device_id_type=MESH)
    pl.semaphore_wait(barrier, len(peers))


def gather_kernel(w_ref, out_ref, send_sems, recv_sems, own_sems):
    spot = Spot()
    copies = Copies(send_sems, recv_sems)
    half = out_ref.at[spot.c]
    locals_ = []
    for k in range(3):
        local = pltpu.make_async_copy(w_ref.at[k], half.at[k, spot.x, spot.y, spot.z], own_sems.at[k])
        local.start()
        locals_.append(local)
    greet(spot, True)
    for local in locals_:
        local.wait()

    def part(k, order, phase, position, piece=None):
        axis = order[phase]
        index = {}
        for n, name in enumerate(order):
            index[name] = slice(None) if n < phase else spot.at(name)
        index[axis] = position
        rows = slice(None)
        if piece is not None:
            start, size = piece
            if phase == 0:
                rows = pl.ds(start, size)
            else:
                index[order[0]] = pl.ds(start, size)
        return half.at[k, index["x"], index["y"], index["z"], rows]

    def ring(k, order, phase, position, piece, by):
        ref = part(k, order, phase, position, piece)
        return copies.start(ref, ref, spot.device(order[phase], by))

    def push(k, order, phase, position, piece):
        ref = part(k, order, phase, position, piece)
        return copies.start(ref, ref, spot.sibling())

    pushes = []
    for phase in range(3):
        if phase == 0:
            to_right, to_left = [(0, 32), (32, 16)], [(32, 16), (0, 32)]
            pass_right, pass_left = [(0, 32)], [(32, 16)]
        elif phase == 1:
            to_right, to_left = [(0, 2), (2, 2)], [(2, 2), (0, 2)]
            pass_right, pass_left = [(0, 2)], [(2, 2)]
        else:
            to_right, to_left = [(0, 1), (1, 1), (2, 1), (3, 1)], [(2, 1), (3, 1), (0, 1), (1, 1)]
            pass_right, pass_left = [(0, 1), (1, 1)], [(2, 1), (3, 1)]
        first = {}
        for n in range(len(to_right)):
            for k, order in enumerate(ORDERS):
                me = spot.at(order[phase])
                first[k, "r", to_right[n]] = ring(k, order, phase, me, to_right[n], 1)
                first[k, "l", to_left[n]] = ring(k, order, phase, me, to_left[n], -1)
        if phase == 2:
            for k, order in enumerate(ORDERS):
                pushes.append(push(k, order, phase, spot.at(order[phase]), None))
        second = []
        for n in range(len(to_right)):
            for k, order in enumerate(ORDERS):
                axis = order[phase]
                before, after = spot.shifted(axis, -1), spot.shifted(axis, 1)
                first[k, "r", to_right[n]].wait_recv()
                if to_right[n] in pass_right:
                    second.append((k, to_right[n], ring(k, order, phase, before, to_right[n], 1)))
                first[k, "l", to_left[n]].wait_recv()
                if to_left[n] in pass_left:
                    second.append((k, to_left[n], ring(k, order, phase, after, to_left[n], -1)))
                if phase == 2:
                    pushes.append(push(k, order, phase, before, to_right[n]))
                    pushes.append(push(k, order, phase, after, to_left[n]))
        for k, piece, copy in second:
            copy.wait_recv()
            if phase == 2:
                order = ORDERS[k]
                pushes.append(push(k, order, phase, spot.shifted(order[phase], 2), piece))
    for copy in pushes:
        copy.wait_recv()
    copies.finish()


def gather_weights(w):
    return pl.pallas_call(
        gather_kernel,
        out_shape=jax.ShapeDtypeStruct((2, 3, 4, 4, 4, 48, 768), jnp.bfloat16),
        in_specs=[pl.BlockSpec(memory_space=pl.ANY)],
        out_specs=pl.BlockSpec(memory_space=pl.ANY),
        scratch_shapes=[pltpu.SemaphoreType.DMA((160,)), pltpu.SemaphoreType.DMA((160,)), pltpu.SemaphoreType.DMA((3,))],
        compiler_params=pltpu.CompilerParams(collective_id=1, has_side_effects=True),
        name="gather_weights",
    )(w)


def reduce_kernel(g_ref, out_ref, a0, b0, l0, r0, q0, a1, b1, l1, r1, q1, a2, b2, l2, r2, send_sems, recv_sems):
    spot = Spot()
    copies = Copies(send_sems, recv_sems)
    greet(spot, False)
    first_in, second_in = [(a0, b0), (a1, b1), (a2, b2)], [(l0, r0), (l1, r1), (l2, r2)]
    quarters = [q0, q1]

    def source(k, phase, order, position, piece=None):
        axis = order[phase]
        rest = order[phase + 1:]
        if phase == 0:
            index = {axis: position}
            for n, name in enumerate(rest):
                index[name] = slice(None)
            if piece is not None:
                index[max(rest)] = pl.ds(2 * piece, 2)
            return g_ref.at[k, index["x"], index["y"], index["z"]]
        held = quarters[phase - 1].at[k]
        names = [n for n in "xyz" if n in order[phase:]]
        index = []
        for name in names:
            if name == axis:
                index.append(position)
            elif piece is not None and name == rest[0]:
                index.append(pl.ds(2 * piece, 2))
            else:
                index.append(slice(None))
        rows = slice(None)
        if phase == 2 and piece is not None:
            rows = pl.ds(0, 32) if piece == 0 else pl.ds(32, 16)
        return held.at[tuple(index) + (rows,)]

    def slot(buffer, k, phase, order, piece):
        held = buffer.at[k]
        if piece is None:
            return held
        if phase == 2:
            return held.at[pl.ds(0, 32) if piece == 0 else pl.ds(32, 16)]
        rest = order[phase + 1:]
        names = [n for n in "xyz" if n in rest]
        return held.at[tuple(pl.ds(2 * piece, 2) if n == max(rest) else slice(None) for n in names)]

    def each(shape, body):
        lead = shape[:-2]
        if not lead:
            body(())
        elif len(lead) == 1:
            @pl.loop(0, lead[0])
            def _(i):
                body((i,))
        else:
            @pl.loop(0, lead[0])
            def _(i):
                @pl.loop(0, lead[1])
                def _(j):
                    body((i, j))

    for phase in range(3):
        started = []
        for k, gathered in enumerate(ORDERS):
            order = gathered[::-1]
            axis = order[phase]
            right, left = spot.device(axis, 1), spot.device(axis, -1)
            a, b = first_in[phase]
            l, r = second_in[phase]
            far = spot.shifted(axis, 2)
            ca = copies.start(source(k, phase, order, far, 0), a.at[k], right)
            cb = copies.start(source(k, phase, order, far, 1), b.at[k], left)
            started.append([ca, cb])
        for k, gathered in enumerate(ORDERS):
            order = gathered[::-1]
            axis = order[phase]
            right, left = spot.device(axis, 1), spot.device(axis, -1)
            l, r = second_in[phase]
            after, before = spot.shifted(axis, 1), spot.shifted(axis, -1)
            started[k].append(copies.start(source(k, phase, order, after, 1), slot(l, k, phase, order, 1), right))
            started[k].append(copies.start(source(k, phase, order, before, 0), slot(r, k, phase, order, 0), left))
        for k, gathered in enumerate(ORDERS):
            order = gathered[::-1]
            axis = order[phase]
            right, left = spot.device(axis, 1), spot.device(axis, -1)
            a, b = first_in[phase]
            l, r = second_in[phase]
            after, before = spot.shifted(axis, 1), spot.shifted(axis, -1)

            def join(buffer, own):
                def body(i):
                    buffer[i] = (buffer[i].astype(jnp.float32) + own[i].astype(jnp.float32)).astype(jnp.bfloat16)
                each(buffer.shape, body)

            started[k][0].wait_recv()
            join(a.at[k], source(k, phase, order, after, 0))
            started[k].append(copies.start(a.at[k], slot(l, k, phase, order, 0), right))
            started[k][1].wait_recv()
            join(b.at[k], source(k, phase, order, before, 1))
            started[k].append(copies.start(b.at[k], slot(r, k, phase, order, 1), left))
        for k, gathered in enumerate(ORDERS):
            order = gathered[::-1]
            axis = order[phase]
            l, r = second_in[phase]
            for copy in started[k][2:]:
                copy.wait_recv()
            own = source(k, phase, order, spot.at(axis))
            left_in, right_in = l.at[k], r.at[k]
            target = out_ref.at[k] if phase == 2 else quarters[phase].at[k]

            def body(i):
                target[i] = (own[i].astype(jnp.float32) + left_in[i].astype(jnp.float32)
                             + right_in[i].astype(jnp.float32)).astype(target.dtype)
            each(target.shape, body)
    copies.finish()


def reduce_grads(g):
    low = lambda *s: pltpu.VMEM(s, jnp.bfloat16)
    return pl.pallas_call(
        reduce_kernel,
        out_shape=jax.ShapeDtypeStruct((3, 48, 768), jnp.float32),
        in_specs=[pl.BlockSpec(memory_space=pltpu.VMEM)],
        out_specs=pl.BlockSpec(memory_space=pltpu.VMEM),
        scratch_shapes=[
            low(3, 4, 2, 48, 768), low(3, 4, 2, 48, 768), low(3, 4, 4, 48, 768), low(3, 4, 4, 48, 768), low(3, 4, 4, 48, 768),
            low(3, 2, 48, 768), low(3, 2, 48, 768), low(3, 4, 48, 768), low(3, 4, 48, 768), low(3, 4, 48, 768),
            low(3, 32, 768), low(3, 16, 768), low(3, 48, 768), low(3, 48, 768),
            pltpu.SemaphoreType.DMA((60,)), pltpu.SemaphoreType.DMA((60,)),
        ],
        compiler_params=pltpu.CompilerParams(collective_id=2, has_side_effects=True, vmem_limit_bytes=56 * 2**20),
        name="reduce_grads",
    )(g)


def lanes_swapped(tile):
    return pltpu.roll(tile, 64, 1)


def split_pair(ref, column):
    top = ref[0:64, column:column + 128].astype(jnp.float32)
    low = ref[64:128, column:column + 128].astype(jnp.float32)
    left = lax.broadcasted_iota(jnp.int32, (64, 128), 1) < 64
    first = jnp.where(left, top, lanes_swapped(low))
    second = jnp.where(left, lanes_swapped(top), low)
    return first.astype(jnp.bfloat16), second.astype(jnp.bfloat16)


def join_pair(first, second):
    first, second = first.astype(jnp.float32), second.astype(jnp.float32)
    left = lax.broadcasted_iota(jnp.int32, (64, 128), 1) < 64
    top = jnp.where(left, first, lanes_swapped(second))
    low = jnp.where(left, lanes_swapped(first), second)
    return top.astype(jnp.bfloat16), low.astype(jnp.bfloat16)


def pack_rows(block):
    return jnp.concatenate([block[0:64], block[64:128]], axis=1)


class Group:
    def __init__(self):
        self.s, self.y, self.z, self.c, self.t = (lax.axis_index(a) for a in "syzct")
        self.me = self.z * 4 + self.c * 2 + self.t
        self.active = jnp.logical_or(self.c == 0, lax.rem(self.z + self.t, 2) == 0)
        self.head = jnp.where(self.c == 0, self.z * 2 + self.t, 8 + self.z)

    def member(self, index):
        return (self.s, self.y, lax.div(index, 4), lax.rem(lax.div(index, 2), 2), lax.rem(index, 2))

    def holder(self, head):
        late = head - 8
        return jnp.where(head < 8, lax.div(head, 2) * 4 + lax.rem(head, 2), late * 4 + 2 + lax.rem(late, 2))

    def greet(self):
        barrier = pltpu.get_barrier_semaphore()

        @pl.loop(1, 16)
        def _(n):
            pl.semaphore_signal(barrier, inc=1, device_id=self.member(lax.rem(self.me + n, 16)), device_id_type=MESH)
        pl.semaphore_wait(barrier, 15)


def out_to_heads(group, packed, landed, send_sems, recv_sems):
    @pl.loop(0, 12)
    def _(n):
        head = lax.rem(group.me + n, 12)
        target = group.holder(head)

        @pl.when(target != group.me)
        def _():
            pltpu.make_async_remote_copy(
                src_ref=packed.at[head], dst_ref=landed.at[group.me], send_sem=send_sems.at[head],
                recv_sem=recv_sems.at[group.me], device_id=group.member(target), device_id_type=MESH).start()

    @pl.when(group.active)
    def _():
        landed[group.me] = packed[group.head]


def await_member(group, packed, landed, send_sems, recv_sems, index):
    @pl.when(group.me != index)
    def _():
        pltpu.make_async_remote_copy(
            src_ref=packed.at[0], dst_ref=landed.at[index], send_sem=send_sems.at[0],
            recv_sem=recv_sems.at[index], device_id=group.member(index), device_id_type=MESH).wait_recv()


def sent_to_heads(group, packed, landed, send_sems, recv_sems):
    @pl.loop(0, 12)
    def _(head):
        @pl.when(group.holder(head) != group.me)
        def _():
            pltpu.make_async_remote_copy(
                src_ref=packed.at[head], dst_ref=landed.at[group.me], send_sem=send_sems.at[head],
                recv_sem=recv_sems.at[group.me], device_id=group.member(group.holder(head)),
                device_id_type=MESH).wait_send()


def back_to_member(group, packed, landed, send_sems, recv_sems, index):
    @pl.when(group.me != index)
    def _():
        pltpu.make_async_remote_copy(
            src_ref=packed.at[index], dst_ref=landed.at[group.head], send_sem=send_sems.at[index],
            recv_sem=recv_sems.at[group.head], device_id=group.member(index), device_id_type=MESH).start()

    @pl.when(group.me == index)
    def _():
        landed[group.head] = packed[index]


def finish_back(group, packed, landed, send_sems, recv_sems):
    @pl.when(group.active)
    def _():
        @pl.loop(0, 16)
        def _(index):
            @pl.when(group.me != index)
            def _():
                pltpu.make_async_remote_copy(
                    src_ref=packed.at[index], dst_ref=landed.at[group.head], send_sem=send_sems.at[index],
                    recv_sem=recv_sems.at[group.head], device_id=group.member(index),
                    device_id_type=MESH).wait_send()

    @pl.loop(0, 12)
    def _(head):
        holder = group.holder(head)

        @pl.when(holder != group.me)
        def _():
            pltpu.make_async_remote_copy(
                src_ref=packed.at[0], dst_ref=landed.at[head], send_sem=send_sems.at[0],
                recv_sem=recv_sems.at[head], device_id=group.member(holder), device_id_type=MESH).wait_recv()


def dot_right(left, right):
    return lax.dot_general(left, right, (((1,), (1,)), ((), ())), preferred_element_type=jnp.float32)


def dot(left, right):
    return jnp.dot(left, right, preferred_element_type=jnp.float32)


def masked_scores(scores, block):
    key = lax.broadcasted_iota(jnp.int32, scores.shape, 0)
    query = lax.broadcasted_iota(jnp.int32, scores.shape, 1) + block * 256
    return jnp.where(key <= query, scores, -1e30)


def attend_kernel(q_ref, k_ref, v_ref, mixed_ref, heads_ref, total_ref,
                  packed, landed, back, home, value_turned, send_a, recv_a, send_b, recv_b):
    group = Group()
    for n, ref in enumerate((q_ref, k_ref, v_ref)):
        for pair in range(6):
            first, second = split_pair(ref, pair * 128)
            packed[2 * pair, n * 64:n * 64 + 64] = first
            packed[2 * pair + 1, n * 64:n * 64 + 64] = second
    group.greet()
    out_to_heads(group, packed, landed, send_a, recv_a)

    @pl.when(group.active)
    def _():
        for block in range(8):
            for index in (2 * block, 2 * block + 1):
                await_member(group, packed, landed, send_a, recv_a, index)
                for n in range(3):
                    tile = landed[index, n * 64:n * 64 + 64]
                    heads_ref[n, index * 128:index * 128 + 64] = tile[:, 0:64]
                    heads_ref[n, index * 128 + 64:index * 128 + 128] = tile[:, 64:128]
            rows = slice(block * 256, block * 256 + 256)
            value_turned[:, rows] = heads_ref[2, rows].T
            count = block * 256 + 256
            scores = masked_scores(dot_right(heads_ref[1, 0:count], heads_ref[0, rows]), block)
            largest = jnp.max(scores, axis=0, keepdims=True)
            weights = jnp.exp(scores - largest)
            total = jnp.sum(weights, axis=0, keepdims=True)
            total_ref[block:block + 1, :] = largest + jnp.log(total)
            mixed = dot(value_turned[:, 0:count], weights.astype(jnp.bfloat16)) / total
            mixed = mixed.T
            for n, index in enumerate((2 * block, 2 * block + 1)):
                back[index] = pack_rows(mixed[n * 128:n * 128 + 128]).astype(jnp.bfloat16)
                back_to_member(group, back, home, send_b, recv_b, index)

    sent_to_heads(group, packed, landed, send_a, recv_a)
    finish_back(group, back, home, send_b, recv_b)
    for pair in range(6):
        top, low = join_pair(home[2 * pair], home[2 * pair + 1])
        mixed_ref[0:64, pair * 128:pair * 128 + 128] = top
        mixed_ref[64:128, pair * 128:pair * 128 + 128] = low


def attend(q, k, v, which):
    low = lambda *s: pltpu.VMEM(s, jnp.bfloat16)
    vmem = pl.BlockSpec(memory_space=pltpu.VMEM)
    return pl.pallas_call(
        attend_kernel,
        out_shape=(jax.ShapeDtypeStruct((128, 768), jnp.bfloat16), jax.ShapeDtypeStruct((3, 2048, 64), jnp.bfloat16),
                   jax.ShapeDtypeStruct((8, 256), jnp.float32)),
        in_specs=[vmem] * 3,
        out_specs=(vmem, vmem, vmem),
        scratch_shapes=[
            low(12, 192, 128), low(16, 192, 128), low(16, 64, 128), low(12, 64, 128), low(64, 2048),
            pltpu.SemaphoreType.DMA((12,)), pltpu.SemaphoreType.DMA((16,)),
            pltpu.SemaphoreType.DMA((16,)), pltpu.SemaphoreType.DMA((12,)),
        ],
        compiler_params=pltpu.CompilerParams(collective_id=3 + which, has_side_effects=True, vmem_limit_bytes=48 * 2**20),
        name="attend",
    )(q, k, v)


def attend_back_kernel(grad_ref, heads_ref, total_ref, dq_ref, dk_ref, dv_ref,
                       packed, landed, back, home, grad_heads, key_turned, key_sum, value_sum,
                       send_a, recv_a, send_b, recv_b):
    group = Group()
    for pair in range(6):
        first, second = split_pair(grad_ref, pair * 128)
        packed[2 * pair] = first
        packed[2 * pair + 1] = second
    group.greet()
    out_to_heads(group, packed, landed, send_a, recv_a)

    @pl.when(group.active)
    def _():
        key_turned[...] = heads_ref[1].T
        for block in reversed(range(8)):
            for index in (2 * block, 2 * block + 1):
                await_member(group, packed, landed, send_a, recv_a, index)
                tile = landed[index]
                grad_heads[index * 128:index * 128 + 64] = tile[:, 0:64]
                grad_heads[index * 128 + 64:index * 128 + 128] = tile[:, 64:128]
            rows = slice(block * 256, block * 256 + 256)
            count = block * 256 + 256
            query, grad = heads_ref[0, rows], grad_heads[rows]
            scores = masked_scores(dot_right(heads_ref[1, 0:count], query), block)
            weights = jnp.exp(scores - total_ref[block:block + 1, :])
            soft = dot_right(heads_ref[2, 0:count], grad)
            dots = jnp.sum(weights * soft, axis=0, keepdims=True)
            moved = (weights * (soft - dots)).astype(jnp.bfloat16)
            for_key, for_value = dot(moved, query), dot(weights.astype(jnp.bfloat16), grad)
            if block == 7:
                key_sum[...] = for_key
                value_sum[...] = for_value
            else:
                key_sum[0:count] = key_sum[0:count] + for_key
                value_sum[0:count] = value_sum[0:count] + for_value
            for_query = dot(key_turned[:, 0:count], moved).T.astype(jnp.bfloat16).astype(jnp.float32) * 0.125
            for n, index in enumerate((2 * block, 2 * block + 1)):
                part = slice(index * 128, index * 128 + 128)
                back[index, 0:64] = pack_rows(for_query[n * 128:n * 128 + 128]).astype(jnp.bfloat16)
                back[index, 64:128] = pack_rows(key_sum[part]).astype(jnp.bfloat16)
                back[index, 128:192] = pack_rows(value_sum[part]).astype(jnp.bfloat16)
                back_to_member(group, back, home, send_b, recv_b, index)

    sent_to_heads(group, packed, landed, send_a, recv_a)
    finish_back(group, back, home, send_b, recv_b)
    for n, ref in enumerate((dq_ref, dk_ref, dv_ref)):
        for pair in range(6):
            top, low = join_pair(home[2 * pair, n * 64:n * 64 + 64], home[2 * pair + 1, n * 64:n * 64 + 64])
            ref[0:64, pair * 128:pair * 128 + 128] = top
            ref[64:128, pair * 128:pair * 128 + 128] = low


def attend_back(grad, heads, total, which):
    low = lambda *s: pltpu.VMEM(s, jnp.bfloat16)
    vmem = pl.BlockSpec(memory_space=pltpu.VMEM)
    return pl.pallas_call(
        attend_back_kernel,
        out_shape=(jax.ShapeDtypeStruct((128, 768), jnp.bfloat16),) * 3,
        in_specs=[vmem] * 3,
        out_specs=(vmem,) * 3,
        scratch_shapes=[
            low(12, 64, 128), low(16, 64, 128), low(16, 192, 128), low(12, 192, 128), low(2048, 64), low(64, 2048),
            pltpu.VMEM((2048, 64), jnp.float32), pltpu.VMEM((2048, 64), jnp.float32),
            pltpu.SemaphoreType.DMA((12,)), pltpu.SemaphoreType.DMA((16,)),
            pltpu.SemaphoreType.DMA((16,)), pltpu.SemaphoreType.DMA((12,)),
        ],
        compiler_params=pltpu.CompilerParams(collective_id=5 + which, has_side_effects=True, vmem_limit_bytes=48 * 2**20),
        name="attend_back",
    )(grad, heads, total)


def move_kernel(order_ref, x_ref, out_ref, middle, turned, send_a, recv_a, send_b, recv_b):
    s, y, z, c, t = (lax.axis_index(a) for a in "syzct")
    me = y * 8 + z * 2 + c

    def member(index):
        return (s, lax.div(index, 8), lax.rem(lax.div(index, 2), 4), lax.rem(index, 2), t)

    barrier = pltpu.get_barrier_semaphore()

    @pl.loop(1, 32)
    def _(n):
        pl.semaphore_signal(barrier, inc=1, device_id=member(lax.rem(me + n, 32)), device_id_type=MESH)
    pl.semaphore_wait(barrier, 31)

    def exchange(source, target, send_sems, recv_sems):
        def copy(n):
            to = lax.rem(me + n, 32)
            return pltpu.make_async_remote_copy(
                src_ref=source.at[to], dst_ref=target.at[me], send_sem=send_sems.at[n], recv_sem=recv_sems.at[n],
                device_id=member(to), device_id_type=MESH)

        @pl.loop(1, 32)
        def _(n):
            copy(n).start()
        target[me] = source[me]

        @pl.loop(1, 32)
        def _(n):
            came = lax.rem(me + 32 - n, 32)
            pltpu.make_async_remote_copy(
                src_ref=source.at[came], dst_ref=target.at[came], send_sem=send_sems.at[n], recv_sem=recv_sems.at[n],
                device_id=member(came), device_id_type=MESH).wait_recv()
        return copy

    first = exchange(x_ref, middle, send_a, recv_a)

    @pl.loop(0, 32)
    def _(n):
        turned[n] = middle[order_ref[n]]
    second = exchange(turned, out_ref, send_b, recv_b)

    @pl.loop(1, 32)
    def _(n):
        first(n).wait_send()
        second(n).wait_send()


def move_blocks(order, x, which):
    vmem = pl.BlockSpec(memory_space=pltpu.VMEM)
    sems = [pltpu.SemaphoreType.DMA((32,))] * 4
    return pl.pallas_call(
        move_kernel,
        out_shape=jax.ShapeDtypeStruct(x.shape, x.dtype),
        in_specs=[pl.BlockSpec(memory_space=pltpu.SMEM), vmem],
        out_specs=vmem,
        scratch_shapes=[pltpu.VMEM(x.shape, x.dtype), pltpu.VMEM(x.shape, x.dtype)] + sems,
        compiler_params=pltpu.CompilerParams(collective_id=which, has_side_effects=True),
        name="move_blocks",
    )(order, x)


def deltas_kernel(left_a, left_b, right_ref, out_ref):
    def product(left):
        return lax.dot_general(left, right_ref[0, 0, 0], (((0,), (0,)), ((), ())), preferred_element_type=jnp.float32)
    which = pl.program_id(1)
    first = product(left_a[0, 0])
    out_ref[0, 0] = first.astype(jnp.bfloat16)

    @pl.when(which == 1)
    def _():
        out_ref[0, 0, :, 384:768] = product(left_b[0, 0])[:, 384:768].astype(jnp.bfloat16)


def weight_deltas(left, right):
    def left_a(layer, part, half):
        return (layer, jnp.where(part == 2, 3, part), 0, 0)

    def left_b(layer, part, half):
        return (layer, jnp.where(part == 2, 3, part * 2), 0, 0)
    return pl.pallas_call(
        deltas_kernel,
        grid=(2, 3, 2),
        out_shape=jax.ShapeDtypeStruct((3, 4, 768, 768), jnp.bfloat16),
        in_specs=[
            pl.BlockSpec((1, 1, 256, 768), left_a), pl.BlockSpec((1, 1, 256, 768), left_b),
            pl.BlockSpec((1, 1, 1, 256, 768), lambda layer, part, half: (layer, part, half, 0, 0)),
        ],
        out_specs=pl.BlockSpec((1, 1, 768, 768), lambda layer, part, half: (part, half * 2 + layer, 0, 0)),
        compiler_params=pltpu.CompilerParams(vmem_limit_bytes=32 * 2**20),
        name="weight_deltas",
    )(left, left, right)


epsilon = 1e-05


def normalize(residual, gain_row, shift_row):
    average = jnp.mean(residual, axis=-1, keepdims=True)
    centred = residual - average
    spread = jnp.mean(centred * centred, axis=-1, keepdims=True)
    return centred * lax.rsqrt(spread + epsilon) * gain_row + shift_row


def smooth_gate(values):
    return jax.nn.gelu(values, approximate=False)


def swap(value, axis):
    return lax.ppermute(value, axis, [(0, 1), (1, 0)])


def low(value):
    return value.astype(jnp.bfloat16)


def layer_forward(entering, weights, bias_qv, bias_up, rows, layer):
    pair_qk, pair_vo, up_a, up_b, down_a, down_b = weights
    normed = low(normalize(entering, rows[0], rows[1]))
    qk = [dot(normed, pair_qk[t]) for t in range(2)]
    query = jnp.concatenate([qk[t][:, :384] for t in range(2)], axis=1)
    key = low(jnp.concatenate([qk[t][:, 384:] for t in range(2)], axis=1))
    value = jnp.concatenate([dot(normed, pair_vo[t][:, :384]) for t in range(2)], axis=1)
    query = low((query + bias_qv[0]) * 0.125)
    value = low(value + bias_qv[1])
    mixed, heads, total = attend(query, key, value, layer)
    hidden = entering + rows[2] + sum(
        dot_right(mixed[:, t * 384:t * 384 + 384], pair_vo[t][:, 384:]) for t in range(2))
    normed_two = low(normalize(hidden, rows[3], rows[4]))
    pre = [[dot(normed_two, up[t]) + bias_up[t, n * 768:n * 768 + 768] for n, up in enumerate((up_a, up_b))] for t in range(2)]
    active = [[low(smooth_gate(p)) for p in two] for two in pre]
    leaving = hidden + rows[5] + sum(
        dot_right(active[t][n], down[t]) for t in range(2) for n, down in enumerate((down_a, down_b)))
    return leaving, (entering, normed, mixed, heads, total, hidden, normed_two, pre, active)


def layer_backward(arriving, kept, weights, rows, layer):
    pair_qk, pair_vo, up_a, up_b, down_a, down_b = weights
    entering, normed, mixed, heads, total, hidden, normed_two, pre, active = kept
    carried = arriving.astype(jnp.float32)
    grad_pre = [[None, None], [None, None]]
    for t in range(2):
        for n, down in enumerate((down_a, down_b)):
            grad_active = dot(arriving, down[t])
            grad_pre[t][n] = low(jax.vjp(smooth_gate, pre[t][n])[1](grad_active)[0])
    grad_normed_two = sum(
        dot_right(grad_pre[t][n], up[t]) for t in range(2) for n, up in enumerate((up_a, up_b)))
    through_two, gain_two, shift_two = jax.vjp(normalize, hidden, rows[3], rows[4])[1](grad_normed_two)
    grad_hidden = carried + through_two
    hidden_low = low(grad_hidden)
    grad_mixed = low(jnp.concatenate([dot(hidden_low, pair_vo[t][:, 384:]) for t in range(2)], axis=1))
    grad_q, grad_k, grad_v = attend_back(grad_mixed, heads, total, layer)
    grad_normed = 0.0
    for t in range(2):
        cut = slice(t * 384, t * 384 + 384)
        grad_normed += dot_right(jnp.concatenate([grad_q[:, cut], grad_k[:, cut]], axis=1), pair_qk[t])
        grad_normed += dot_right(grad_v[:, cut], pair_vo[t][:, :384])
    through_one, gain_one, shift_one = jax.vjp(normalize, entering, rows[0], rows[1])[1](grad_normed)
    grad_input = grad_hidden + through_one

    def column_sum(value):
        return jnp.sum(value.astype(jnp.float32), axis=0)
    vectors = jnp.concatenate([
        gain_one, shift_one, column_sum(hidden_low), gain_two, shift_two, column_sum(carried),
        column_sum(grad_q), column_sum(grad_v),
    ] + [column_sum(grad_pre[t][n]) for t in range(2) for n in range(2)])
    return grad_input, vectors, (normed, hidden_low, normed_two, arriving, grad_q, grad_k, grad_v, mixed, grad_pre, active)


def delta_operands(parts, core):
    normed, hidden_low, normed_two, arriving, grad_q, grad_k, grad_v, mixed, grad_pre, active = parts

    def operands(core):
        pick = lambda a, b: jnp.where(core == 0, a, b)
        left = jnp.stack([pick(normed, normed_two), pick(normed, arriving), pick(hidden_low, arriving), pick(normed_two, arriving)])
        right = []
        cuts = [slice(t * 384, t * 384 + 384) for t in range(2)]
        right.append(jnp.stack([pick(jnp.concatenate([grad_q[:, cuts[t]], grad_k[:, cuts[t]]], axis=1), grad_pre[t][1]) for t in range(2)]))
        right.append(jnp.stack([pick(jnp.concatenate([grad_v[:, cuts[t]], mixed[:, cuts[t]]], axis=1), active[t][0]) for t in range(2)]))
        right.append(jnp.stack([pick(grad_pre[t][0], active[t][1]) for t in range(2)]))
        return left, jnp.stack(right)
    own = operands(core)
    other = swap(operands(1 - core), "c")
    return tuple(jnp.concatenate([a, b], axis=-2) for a, b in zip(own, other))


def on_device(tokens_in, cotangent, place, w_qkv, w_out, w_up, w_down, qv_bias, up_bias, vectors):
    section = lax.axis_index("s")
    core = lax.axis_index("c")
    half = lax.axis_index("t")
    inverse = jnp.sum(
        jnp.where(place[None, :] == jnp.arange(32, dtype=jnp.int32)[:, None], jnp.arange(32, dtype=jnp.int32)[None, :], 0),
        axis=1)

    shard = jnp.stack([
        jnp.concatenate([w_qkv[0, 0], w_qkv[0, 1]], axis=1), jnp.concatenate([w_qkv[0, 2], w_out[0].T], axis=1),
        w_up[0, :, :768], w_up[0, :, 768:], w_down[0, :768].T, w_down[0, 768:].T])
    own = jnp.where(core == 0, shard[:3], shard[3:])
    got = swap(jnp.where(core == 0, shard[3:], shard[:3]), "c")
    both = jnp.where(core == 0, jnp.concatenate([own, got], axis=1), jnp.concatenate([got, own], axis=1))
    gathered = gather_weights(both).reshape(6, 4, 768, 768)
    weights = [[[gathered[part, t * 2 + layer] for t in range(2)] for part in range(6)] for layer in range(2)]

    small = jnp.concatenate([
        vectors[0].astype(jnp.float32).reshape(-1),
        jnp.zeros((2, 2, 384), jnp.float32).at[:, half].set(qv_bias[0].reshape(2, 384).astype(jnp.float32)).reshape(-1) * 1.0,
        jnp.zeros((2, 1536), jnp.float32).at[half].set(up_bias[0].astype(jnp.float32)).reshape(-1),
    ])
    split = jnp.arange(4608 + 1536 + 3072) >= 4608
    partner = swap(small, "t")
    small = jnp.where(split, small + partner, small)
    beside = swap(small, "s")
    small = jnp.where(section == 0, jnp.stack([small, beside]), jnp.stack([beside, small]))
    rows = small[:, :4608].reshape(2, 6, 768)
    bias_qv = small[:, 4608:6144].reshape(2, 2, 768)
    bias_up = small[:, 6144:].reshape(2, 2, 1536)

    mine = jnp.stack([jnp.where(section == 0, a[0], a[1]) for a in (tokens_in, cotangent)])
    mine = mine.reshape(2, 32, 4, 768).transpose(1, 0, 2, 3).reshape(32, 48, 128)
    mine = move_blocks(inverse, mine, 7)
    mine = mine.reshape(32, 2, 4, 768).transpose(1, 0, 2, 3).reshape(2, 128, 768)

    acts, kept = [], []
    entering = mine[0]
    for layer in range(2):
        leaving, state = layer_forward(entering.astype(jnp.float32), weights[layer], bias_qv[layer], bias_up[layer], rows[layer], layer)
        entering = low(leaving)
        acts.append(entering)
        kept.append(state)
    arriving = mine[1]
    input_grads, sums, operands = [None] * 2, [None] * 2, [None] * 2
    for layer in (1, 0):
        grad_input, sums[layer], parts = layer_backward(arriving, kept[layer], weights[layer], rows[layer], layer)
        operands[layer] = delta_operands(parts, core)
        arriving = low(grad_input)
        input_grads[layer] = arriving
    left, right = (jnp.stack(both) for both in zip(*operands))
    deltas = weight_deltas(left, right).reshape(3, 4, 4, 4, 48, 768)
    summed = reduce_grads(deltas)
    own_rows = lax.dynamic_slice_in_dim(summed, core * 24, 24, 1)
    got = swap(lax.dynamic_slice_in_dim(summed, (1 - core) * 24, 24, 1), "c")
    full = jnp.where(core == 0, jnp.concatenate([own_rows, got]), jnp.concatenate([got, own_rows]))
    grad_qkv = jnp.stack([full[0, :, :384], full[0, :, 384:], full[1, :, :384]])[None]
    grad_out = full[1, :, 384:].T[None]
    grad_up = jnp.concatenate([full[2], full[3]], axis=1)[None]
    grad_down = jnp.concatenate([full[4].T, full[5].T], axis=0)[None]

    total = lax.psum(jnp.stack(sums), ("s", "y", "z", "c", "t"))
    total = jnp.where(section == 0, total[0], total[1])
    grad_vectors = total[:4608].reshape(1, 6, 768)
    grad_qv = lax.dynamic_slice_in_dim(total[4608:6144].reshape(2, 768), half * 384, 384, 1)[None]
    grad_up_bias = lax.dynamic_slice_in_dim(total[6144:], half * 1536, 1536)[None]

    held = jnp.stack([jnp.stack([acts[layer], input_grads[layer]]) for layer in range(2)])
    stays = jnp.where(section == 0, held[0], held[1])
    came = swap(jnp.where(section == 0, held[1], held[0]), "s")
    rows_out = jnp.where(section == 0, jnp.stack([stays, came]), jnp.stack([came, stays]))
    rows_out = rows_out.reshape(4, 32, 4, 768).transpose(1, 0, 2, 3).reshape(32, 96, 128)
    rows_out = move_blocks(place, rows_out, 8)
    rows_out = rows_out.reshape(32, 4, 4, 768).transpose(1, 0, 2, 3).reshape(2, 2, 128, 768)
    acts_out = rows_out[:, 0][None]
    grads_out = rows_out[:, 1].astype(jnp.float32)[None]
    return acts_out, grads_out, grad_qkv, grad_out, grad_up, grad_down, grad_qv, grad_up_bias, grad_vectors


def solution(mesh):
    fine = Mesh(mesh.devices.reshape(2, 4, 4, 2, 2), ("s", "y", "z", "c", "t"))
    dp = ("y", "z", "c")
    blocks = P(None, dp + ("t",), None)
    weights = (P("s", None, dp, "t"), P("s", "t", dp), P("s", dp, "t"), P("s", "t", dp))
    small = (P("s", None, "t"), P("s", "t"), P("s", None, None))
    rows = P("s", None, dp + ("t",), None)
    return jax.shard_map(
        on_device, mesh=fine,
        in_specs=(blocks, blocks, P()) + weights + small,
        out_specs=(rows, rows) + weights + small,
        check_vma=False)
```

```python
import jax, jax.numpy as jnp
from jax import lax
from jax.experimental import pallas as pl
from jax.experimental.pallas import tpu as pltpu
from jax.sharding import Mesh, PartitionSpec as P
MESH = pl.DeviceIdType.MESH
ORDERS = ("xyz", "yzx", "zxy")


class Spot:
    def __init__(self):
        self.s, self.y, self.z, self.c, self.t = (lax.axis_index(a) for a in "syzct")
        self.x = self.t * 2 + self.s

    def at(self, axis):
        return {"x": self.x, "y": self.y, "z": self.z}[axis]

    def shifted(self, axis, by):
        return lax.rem(self.at(axis) + (by + 4), 4)

    def device(self, axis, by):
        x, y, z = self.x, self.y, self.z
        moved = self.shifted(axis, by)
        if axis == "x":
            x = moved
        elif axis == "y":
            y = moved
        else:
            z = moved
        return (lax.rem(x, 2), y, z, self.c, lax.div(x, 2))

    def sibling(self):
        return (self.s, self.y, self.z, 1 - self.c, self.t)


class Copies:
    def __init__(self, send_sems, recv_sems):
        self.send_sems, self.recv_sems, self.count = send_sems, recv_sems, 0
        self.sent = []

    def make(self, src, dst, device):
        n = self.count
        self.count += 1
        copy = pltpu.make_async_remote_copy(
            src_ref=src, dst_ref=dst, send_sem=self.send_sems.at[n], recv_sem=self.recv_sems.at[n],
            device_id=device, device_id_type=MESH)
        self.sent.append(copy)
        return copy

    def start(self, src, dst, device):
        copy = self.make(src, dst, device)
        copy.start()
        return copy

    def finish(self):
        for copy in self.sent:
            copy.wait_send()


class Move:
    def __init__(self, spot, order_ref, x_ref, out_ref, middle, turned, send_a, recv_a, send_b, recv_b):
        self.spot, self.order, self.turned, self.middle = spot, order_ref, turned, middle
        self.me = spot.y * 8 + spot.z * 2 + spot.c
        self.first = (x_ref, middle, send_a, recv_a)
        self.second = (turned, out_ref, send_b, recv_b)

    def member(self, index):
        return (self.spot.s, lax.div(index, 8), lax.rem(lax.div(index, 2), 4), lax.rem(index, 2), self.spot.t)

    def copy(self, which, n):
        source, target, send_sems, recv_sems = which
        to = lax.rem(self.me + n, 32)
        return pltpu.make_async_remote_copy(
            src_ref=source.at[to], dst_ref=target.at[self.me], send_sem=send_sems.at[n], recv_sem=recv_sems.at[n],
            device_id=self.member(to), device_id_type=MESH)

    def start(self, which):
        @pl.loop(1, 32)
        def _(n):
            self.copy(which, n).start()
        source, target = which[:2]
        target[self.me] = source[self.me]

    def arrive(self, which):
        source, target, send_sems, recv_sems = which

        @pl.loop(1, 32)
        def _(n):
            came = lax.rem(self.me + 32 - n, 32)
            pltpu.make_async_remote_copy(
                src_ref=source.at[came], dst_ref=target.at[came], send_sem=send_sems.at[n], recv_sem=recv_sems.at[n],
                device_id=self.member(came), device_id_type=MESH).wait_recv()

    def begin(self):
        self.start(self.first)

    def turn(self):
        self.arrive(self.first)

        @pl.loop(0, 32)
        def _(n):
            self.turned[n] = self.middle[self.order[n]]
        self.start(self.second)

    def end(self):
        self.arrive(self.second)

        @pl.loop(1, 32)
        def _(n):
            self.copy(self.first, n).wait_send()
            self.copy(self.second, n).wait_send()


def greet(spot, move, far):
    barrier = pltpu.get_barrier_semaphore()
    steps = (1, -1, 2) if far else (1, -1)
    for by in steps:
        pl.semaphore_signal(barrier, inc=1, device_id=spot.device("x", by), device_id_type=MESH)

    @pl.loop(1, 32)
    def _(n):
        pl.semaphore_signal(barrier, inc=1, device_id=move.member(lax.rem(move.me + n, 32)), device_id_type=MESH)
    pl.semaphore_wait(barrier, 31 + len(steps))


def move_scratch(shape):
    return [pltpu.VMEM(shape, jnp.bfloat16)] * 2 + [pltpu.SemaphoreType.DMA((32,))] * 4


def gather_kernel(order_ref, x_ref, w_ref, out_ref, moved_ref, send_sems, recv_sems, own_sems, *move_refs):
    spot = Spot()
    move = Move(spot, order_ref, x_ref, moved_ref, *move_refs)
    copies = Copies(send_sems, recv_sems)
    half = out_ref.at[spot.c]
    locals_ = []
    for k in range(3):
        local = pltpu.make_async_copy(w_ref.at[k], half.at[k, spot.x, spot.y, spot.z], own_sems.at[k])
        local.start()
        locals_.append(local)
    greet(spot, move, False)
    for local in locals_:
        local.wait()
    move.begin()

    def part(k, order, phase, position, piece=None):
        axis = order[phase]
        index = {}
        for n, name in enumerate(order):
            index[name] = slice(None) if n < phase else spot.at(name)
        index[axis] = position
        rows = slice(None)
        if piece is not None:
            start, size = piece
            if phase == 0:
                rows = pl.ds(start, size)
            else:
                index[order[0]] = pl.ds(start, size)
        return half.at[k, index["x"], index["y"], index["z"], rows]

    def ring(k, order, phase, position, piece, by):
        ref = part(k, order, phase, position, piece)
        return copies.start(ref, ref, spot.device(order[phase], by))

    def push(k, order, phase, position, piece):
        ref = part(k, order, phase, position, piece)
        return copies.start(ref, ref, spot.sibling())

    pushes = []
    for phase in range(3):
        if phase == 0:
            to_right, to_left = [(0, 32), (32, 16)], [(32, 16), (0, 32)]
            pass_right, pass_left = [(0, 32)], [(32, 16)]
        elif phase == 1:
            to_right, to_left = [(0, 2), (2, 2)], [(2, 2), (0, 2)]
            pass_right, pass_left = [(0, 2)], [(2, 2)]
        else:
            to_right, to_left = [(0, 1), (1, 1), (2, 1), (3, 1)], [(2, 1), (3, 1), (0, 1), (1, 1)]
            pass_right, pass_left = [(0, 1), (1, 1)], [(2, 1), (3, 1)]
        first = {}
        for n in range(len(to_right)):
            for k, order in enumerate(ORDERS):
                me = spot.at(order[phase])
                first[k, "r", to_right[n]] = ring(k, order, phase, me, to_right[n], 1)
                first[k, "l", to_left[n]] = ring(k, order, phase, me, to_left[n], -1)
        if phase == 1:
            move.turn()
        if phase == 2:
            for k, order in enumerate(ORDERS):
                pushes.append(push(k, order, phase, spot.at(order[phase]), None))
        second = []
        for n in range(len(to_right)):
            for k, order in enumerate(ORDERS):
                axis = order[phase]
                before, after = spot.shifted(axis, -1), spot.shifted(axis, 1)
                first[k, "r", to_right[n]].wait_recv()
                if to_right[n] in pass_right:
                    second.append((k, to_right[n], ring(k, order, phase, before, to_right[n], 1)))
                first[k, "l", to_left[n]].wait_recv()
                if to_left[n] in pass_left:
                    second.append((k, to_left[n], ring(k, order, phase, after, to_left[n], -1)))
                if phase == 2:
                    pushes.append(push(k, order, phase, before, to_right[n]))
                    pushes.append(push(k, order, phase, after, to_left[n]))
        for k, piece, copy in second:
            copy.wait_recv()
            if phase == 2:
                order = ORDERS[k]
                pushes.append(push(k, order, phase, spot.shifted(order[phase], 2), piece))
    for copy in pushes:
        copy.wait_recv()
    copies.finish()
    move.end()


def gather_weights(order, x, w):
    vmem = pl.BlockSpec(memory_space=pltpu.VMEM)
    return pl.pallas_call(
        gather_kernel,
        out_shape=(jax.ShapeDtypeStruct((2, 3, 4, 4, 4, 48, 768), jnp.bfloat16), jax.ShapeDtypeStruct(x.shape, x.dtype)),
        in_specs=[pl.BlockSpec(memory_space=pltpu.SMEM), vmem, pl.BlockSpec(memory_space=pl.ANY)],
        out_specs=(pl.BlockSpec(memory_space=pl.ANY), vmem),
        scratch_shapes=[pltpu.SemaphoreType.DMA((160,)), pltpu.SemaphoreType.DMA((160,)), pltpu.SemaphoreType.DMA((3,))]
        + move_scratch(x.shape),
        compiler_params=pltpu.CompilerParams(collective_id=1, has_side_effects=True),
        name="gather_weights",
    )(order, x, w)


def reduce_kernel(order_ref, x_ref, sums_ref, left_ref, right_ref, out_ref, moved_ref, total_ref,
                  g_ref, a0, b0, l0, r0, q0, a1, b1, l1, r1, q1, a2, b2, l2, r2, beside, slots, send_sems, recv_sems, *move_refs):
    spot = Spot()
    copies = Copies(send_sems, recv_sems)
    move = Move(spot, order_ref, x_ref, moved_ref, *move_refs)
    greet(spot, move, True)
    move.begin()
    vector_copies = [copies.start(sums_ref, beside, spot.sibling())]

    def spread(axis, n):
        me = spot.at(axis)
        return [copies.start(slots.at[n, me], slots.at[n, me], spot.device(axis, by)) for by in (1, -1, 2)]

    def gathered_sum(n):
        for copy in vector_copies.pop():
            copy.wait_recv()
        return (slots[n, 0] + slots[n, 1]) + (slots[n, 2] + slots[n, 3])

    def make_part(k):
        @pl.loop(0, 4)
        def _(x):
            layer, half = lax.rem(x, 2), lax.div(x, 2)

            def product(which, columns):
                return lax.dot_general(
                    left_ref[layer, which], right_ref[layer, k, half, :, columns], (((0,), (0,)), ((), ())),
                    preferred_element_type=jnp.float32).astype(jnp.bfloat16).reshape(4, 4, 48, -1)
            if k == 1:
                g_ref[k, x, :, :, :, 0:384] = product(1, slice(0, 384))
                g_ref[k, x, :, :, :, 384:768] = product(2, slice(384, 768))
            else:
                g_ref[k, x] = product(3 if k == 2 else 0, slice(0, 768))
    first_in, second_in = [(a0, b0), (a1, b1), (a2, b2)], [(l0, r0), (l1, r1), (l2, r2)]
    quarters = [q0, q1]

    def source(k, phase, order, position, piece=None):
        axis = order[phase]
        rest = order[phase + 1:]
        if phase == 0:
            index = {axis: position}
            for n, name in enumerate(rest):
                index[name] = slice(None)
            if piece is not None:
                index[max(rest)] = pl.ds(2 * piece, 2)
            return g_ref.at[k, index["x"], index["y"], index["z"]]
        held = quarters[phase - 1].at[k]
        names = [n for n in "xyz" if n in order[phase:]]
        index = []
        for name in names:
            if name == axis:
                index.append(position)
            elif piece is not None and name == rest[0]:
                index.append(pl.ds(2 * piece, 2))
            else:
                index.append(slice(None))
        rows = slice(None)
        if phase == 2 and piece is not None:
            rows = pl.ds(0, 32) if piece == 0 else pl.ds(32, 16)
        return held.at[tuple(index) + (rows,)]

    def slot(buffer, k, phase, order, piece):
        held = buffer.at[k]
        if piece is None:
            return held
        if phase == 2:
            return held.at[pl.ds(0, 32) if piece == 0 else pl.ds(32, 16)]
        rest = order[phase + 1:]
        names = [n for n in "xyz" if n in rest]
        return held.at[tuple(pl.ds(2 * piece, 2) if n == max(rest) else slice(None) for n in names)]

    def each(shape, body):
        lead = shape[:-2]
        if not lead:
            body(())
        elif len(lead) == 1:
            @pl.loop(0, lead[0])
            def _(i):
                body((i,))
        else:
            @pl.loop(0, lead[0])
            def _(i):
                @pl.loop(0, lead[1])
                def _(j):
                    body((i, j))

    for phase in range(3):
        started = []
        for k, gathered in enumerate(ORDERS):
            if phase == 0:
                make_part(k)
            order = gathered[::-1]
            axis = order[phase]
            right, left = spot.device(axis, 1), spot.device(axis, -1)
            a, b = first_in[phase]
            l, r = second_in[phase]
            far = spot.shifted(axis, 2)
            ca = copies.start(source(k, phase, order, far, 0), a.at[k], right)
            cb = copies.start(source(k, phase, order, far, 1), b.at[k], left)
            started.append([ca, cb])
        for k, gathered in enumerate(ORDERS):
            order = gathered[::-1]
            axis = order[phase]
            right, left = spot.device(axis, 1), spot.device(axis, -1)
            l, r = second_in[phase]
            after, before = spot.shifted(axis, 1), spot.shifted(axis, -1)
            started[k].append(copies.start(source(k, phase, order, after, 1), slot(l, k, phase, order, 1), right))
            started[k].append(copies.start(source(k, phase, order, before, 0), slot(r, k, phase, order, 0), left))
        for k, gathered in enumerate(ORDERS):
            order = gathered[::-1]
            axis = order[phase]
            right, left = spot.device(axis, 1), spot.device(axis, -1)
            a, b = first_in[phase]
            l, r = second_in[phase]
            after, before = spot.shifted(axis, 1), spot.shifted(axis, -1)

            def join(buffer, own):
                def body(i):
                    buffer[i] = (buffer[i].astype(jnp.float32) + own[i].astype(jnp.float32)).astype(jnp.bfloat16)
                each(buffer.shape, body)

            started[k][0].wait_recv()
            join(a.at[k], source(k, phase, order, after, 0))
            started[k].append(copies.start(a.at[k], slot(l, k, phase, order, 0), right))
            started[k][1].wait_recv()
            join(b.at[k], source(k, phase, order, before, 1))
            started[k].append(copies.start(b.at[k], slot(r, k, phase, order, 1), left))
        if phase == 0:
            vector_copies.pop().wait_recv()
            slots[0, spot.x] = sums_ref[...] + beside[...]
            vector_copies.append(spread("x", 0))
            move.turn()
        else:
            slots[phase, spot.at("xyz"[phase])] = gathered_sum(phase - 1)
            vector_copies.append(spread("xyz"[phase], phase))
        for k, gathered in enumerate(ORDERS):
            order = gathered[::-1]
            axis = order[phase]
            l, r = second_in[phase]
            for copy in started[k][2:]:
                copy.wait_recv()
            own = source(k, phase, order, spot.at(axis))
            left_in, right_in = l.at[k], r.at[k]
            target = out_ref.at[k] if phase == 2 else quarters[phase].at[k]

            def body(i):
                target[i] = (own[i].astype(jnp.float32) + left_in[i].astype(jnp.float32)
                             + right_in[i].astype(jnp.float32)).astype(target.dtype)
            each(target.shape, body)
    total_ref[...] = gathered_sum(2)
    copies.finish()
    move.end()


def reduce_grads(order, x, sums, left, right):
    low = lambda *s: pltpu.VMEM(s, jnp.bfloat16)
    vmem = pl.BlockSpec(memory_space=pltpu.VMEM)
    return pl.pallas_call(
        reduce_kernel,
        out_shape=(jax.ShapeDtypeStruct((3, 48, 768), jnp.float32), jax.ShapeDtypeStruct(x.shape, x.dtype),
                   jax.ShapeDtypeStruct(sums.shape, sums.dtype)),
        in_specs=[pl.BlockSpec(memory_space=pltpu.SMEM)] + [vmem] * 4,
        out_specs=(vmem,) * 3,
        scratch_shapes=[
            low(3, 4, 4, 4, 48, 768),
            low(3, 4, 2, 48, 768), low(3, 4, 2, 48, 768), low(3, 4, 4, 48, 768), low(3, 4, 4, 48, 768), low(3, 4, 4, 48, 768),
            low(3, 2, 48, 768), low(3, 2, 48, 768), low(3, 4, 48, 768), low(3, 4, 48, 768), low(3, 4, 48, 768),
            low(3, 32, 768), low(3, 16, 768), low(3, 48, 768), low(3, 48, 768),
            pltpu.VMEM(sums.shape, jnp.float32), pltpu.VMEM((3, 4) + sums.shape, jnp.float32),
            pltpu.SemaphoreType.DMA((80,)), pltpu.SemaphoreType.DMA((80,)),
        ] + move_scratch(x.shape),
        compiler_params=pltpu.CompilerParams(collective_id=2, has_side_effects=True, vmem_limit_bytes=56 * 2**20),
        name="reduce_grads",
    )(order, x, sums, left, right)


def lanes_swapped(tile):
    return pltpu.roll(tile, 64, 1)


def split_pair(ref, column):
    top = ref[0:64, column:column + 128].astype(jnp.float32)
    low = ref[64:128, column:column + 128].astype(jnp.float32)
    left = lax.broadcasted_iota(jnp.int32, (64, 128), 1) < 64
    first = jnp.where(left, top, lanes_swapped(low))
    second = jnp.where(left, lanes_swapped(top), low)
    return first.astype(jnp.bfloat16), second.astype(jnp.bfloat16)


def join_pair(first, second):
    first, second = first.astype(jnp.float32), second.astype(jnp.float32)
    left = lax.broadcasted_iota(jnp.int32, (64, 128), 1) < 64
    top = jnp.where(left, first, lanes_swapped(second))
    low = jnp.where(left, lanes_swapped(first), second)
    return top.astype(jnp.bfloat16), low.astype(jnp.bfloat16)


def pack_rows(block):
    return jnp.concatenate([block[0:64], block[64:128]], axis=1)


class Group:
    def __init__(self):
        self.s, self.y, self.z, self.c, self.t = (lax.axis_index(a) for a in "syzct")
        self.micro = lax.rem(self.s + self.t, 2)
        y, z = lax.rem(self.y, 2), lax.rem(self.z, 2)
        self.me = y * 8 + z * 4 + self.c * 2 + self.t
        self.active = jnp.logical_or(self.c == 0, lax.rem(y + z + self.t, 2) == 0)
        self.head = jnp.where(self.c == 0, y * 4 + z * 2 + self.t, 8 + y * 2 + z)

    def member(self, index):
        t = lax.rem(index, 2)
        y = lax.div(self.y, 2) * 2 + lax.div(index, 8)
        z = lax.div(self.z, 2) * 2 + lax.rem(lax.div(index, 4), 2)
        return (lax.rem(self.micro + t, 2), y, z, lax.rem(lax.div(index, 2), 2), t)

    def holder(self, head):
        late = head - 8
        y, z = lax.div(late, 2), lax.rem(late, 2)
        return jnp.where(
            head < 8, lax.div(head, 4) * 8 + lax.rem(lax.div(head, 2), 2) * 4 + lax.rem(head, 2),
            y * 8 + z * 4 + 2 + lax.rem(y + z, 2))

    def greet(self):
        barrier = pltpu.get_barrier_semaphore()

        @pl.loop(1, 16)
        def _(n):
            pl.semaphore_signal(barrier, inc=1, device_id=self.member(lax.rem(self.me + n, 16)), device_id_type=MESH)
        pl.semaphore_wait(barrier, 15)


def out_to_heads(group, packed, landed, send_sems, recv_sems):
    @pl.loop(0, 12)
    def _(n):
        head = lax.rem(group.me + n, 12)
        target = group.holder(head)

        @pl.when(target != group.me)
        def _():
            pltpu.make_async_remote_copy(
                src_ref=packed.at[head], dst_ref=landed.at[group.me], send_sem=send_sems.at[head],
                recv_sem=recv_sems.at[group.me], device_id=group.member(target), device_id_type=MESH).start()

    @pl.when(group.active)
    def _():
        landed[group.me] = packed[group.head]


def await_member(group, packed, landed, send_sems, recv_sems, index):
    @pl.when(group.me != index)
    def _():
        pltpu.make_async_remote_copy(
            src_ref=packed.at[0], dst_ref=landed.at[index], send_sem=send_sems.at[0],
            recv_sem=recv_sems.at[index], device_id=group.member(index), device_id_type=MESH).wait_recv()


def sent_to_heads(group, packed, landed, send_sems, recv_sems):
    @pl.loop(0, 12)
    def _(head):
        @pl.when(group.holder(head) != group.me)
        def _():
            pltpu.make_async_remote_copy(
                src_ref=packed.at[head], dst_ref=landed.at[group.me], send_sem=send_sems.at[head],
                recv_sem=recv_sems.at[group.me], device_id=group.member(group.holder(head)),
                device_id_type=MESH).wait_send()


def back_to_member(group, packed, landed, send_sems, recv_sems, index):
    @pl.when(group.me != index)
    def _():
        pltpu.make_async_remote_copy(
            src_ref=packed.at[index], dst_ref=landed.at[group.head], send_sem=send_sems.at[index],
            recv_sem=recv_sems.at[group.head], device_id=group.member(index), device_id_type=MESH).start()

    @pl.when(group.me == index)
    def _():
        landed[group.head] = packed[index]


def finish_back(group, packed, landed, send_sems, recv_sems):
    @pl.when(group.active)
    def _():
        @pl.loop(0, 16)
        def _(index):
            @pl.when(group.me != index)
            def _():
                pltpu.make_async_remote_copy(
                    src_ref=packed.at[index], dst_ref=landed.at[group.head], send_sem=send_sems.at[index],
                    recv_sem=recv_sems.at[group.head], device_id=group.member(index),
                    device_id_type=MESH).wait_send()

    @pl.loop(0, 12)
    def _(head):
        holder = group.holder(head)

        @pl.when(holder != group.me)
        def _():
            pltpu.make_async_remote_copy(
                src_ref=packed.at[0], dst_ref=landed.at[head], send_sem=send_sems.at[0],
                recv_sem=recv_sems.at[head], device_id=group.member(holder), device_id_type=MESH).wait_recv()


def dot_right(left, right):
    return lax.dot_general(left, right, (((1,), (1,)), ((), ())), preferred_element_type=jnp.float32)


def dot(left, right):
    return jnp.dot(left, right, preferred_element_type=jnp.float32)


def masked_scores(scores, block):
    key = lax.broadcasted_iota(jnp.int32, scores.shape, 0)
    query = lax.broadcasted_iota(jnp.int32, scores.shape, 1) + block * 256
    return jnp.where(key <= query, scores, -1e30)


def attend_kernel(q_ref, k_ref, v_ref, mixed_ref, heads_ref, total_ref,
                  packed, landed, back, home, value_turned, send_a, recv_a, send_b, recv_b):
    group = Group()
    for n, ref in enumerate((q_ref, k_ref, v_ref)):
        for pair in range(6):
            first, second = split_pair(ref, pair * 128)
            packed[2 * pair, n * 64:n * 64 + 64] = first
            packed[2 * pair + 1, n * 64:n * 64 + 64] = second
    group.greet()
    out_to_heads(group, packed, landed, send_a, recv_a)

    @pl.when(group.active)
    def _():
        for block in range(8):
            for index in (2 * block, 2 * block + 1):
                await_member(group, packed, landed, send_a, recv_a, index)
                for n in range(3):
                    tile = landed[index, n * 64:n * 64 + 64]
                    heads_ref[n, index * 128:index * 128 + 64] = tile[:, 0:64]
                    heads_ref[n, index * 128 + 64:index * 128 + 128] = tile[:, 64:128]
            rows = slice(block * 256, block * 256 + 256)
            value_turned[:, rows] = heads_ref[2, rows].T
            count = block * 256 + 256
            scores = masked_scores(dot_right(heads_ref[1, 0:count], heads_ref[0, rows]), block)
            largest = jnp.max(scores, axis=0, keepdims=True)
            weights = jnp.exp(scores - largest)
            total = jnp.sum(weights, axis=0, keepdims=True)
            total_ref[block:block + 1, :] = largest + jnp.log(total)
            mixed = dot(value_turned[:, 0:count], weights.astype(jnp.bfloat16)) / total
            mixed = mixed.T
            for n, index in enumerate((2 * block, 2 * block + 1)):
                back[index] = pack_rows(mixed[n * 128:n * 128 + 128]).astype(jnp.bfloat16)
                back_to_member(group, back, home, send_b, recv_b, index)

    sent_to_heads(group, packed, landed, send_a, recv_a)
    finish_back(group, back, home, send_b, recv_b)
    for pair in range(6):
        top, low = join_pair(home[2 * pair], home[2 * pair + 1])
        mixed_ref[0:64, pair * 128:pair * 128 + 128] = top
        mixed_ref[64:128, pair * 128:pair * 128 + 128] = low


def attend(q, k, v, which):
    low = lambda *s: pltpu.VMEM(s, jnp.bfloat16)
    vmem = pl.BlockSpec(memory_space=pltpu.VMEM)
    return pl.pallas_call(
        attend_kernel,
        out_shape=(jax.ShapeDtypeStruct((128, 768), jnp.bfloat16), jax.ShapeDtypeStruct((3, 2048, 64), jnp.bfloat16),
                   jax.ShapeDtypeStruct((8, 256), jnp.float32)),
        in_specs=[vmem] * 3,
        out_specs=(vmem, vmem, vmem),
        scratch_shapes=[
            low(12, 192, 128), low(16, 192, 128), low(16, 64, 128), low(12, 64, 128), low(64, 2048),
            pltpu.SemaphoreType.DMA((12,)), pltpu.SemaphoreType.DMA((16,)),
            pltpu.SemaphoreType.DMA((16,)), pltpu.SemaphoreType.DMA((12,)),
        ],
        compiler_params=pltpu.CompilerParams(collective_id=3 + which, has_side_effects=True, vmem_limit_bytes=48 * 2**20),
        name="attend",
    )(q, k, v)


def attend_back_kernel(grad_ref, heads_ref, total_ref, dq_ref, dk_ref, dv_ref,
                       packed, landed, back, home, grad_heads, key_turned, key_sum, value_sum,
                       send_a, recv_a, send_b, recv_b):
    group = Group()
    for pair in range(6):
        first, second = split_pair(grad_ref, pair * 128)
        packed[2 * pair] = first
        packed[2 * pair + 1] = second
    group.greet()
    out_to_heads(group, packed, landed, send_a, recv_a)

    @pl.when(group.active)
    def _():
        key_turned[...] = heads_ref[1].T
        for block in reversed(range(8)):
            for index in (2 * block, 2 * block + 1):
                await_member(group, packed, landed, send_a, recv_a, index)
                tile = landed[index]
                grad_heads[index * 128:index * 128 + 64] = tile[:, 0:64]
                grad_heads[index * 128 + 64:index * 128 + 128] = tile[:, 64:128]
            rows = slice(block * 256, block * 256 + 256)
            count = block * 256 + 256
            query, grad = heads_ref[0, rows], grad_heads[rows]
            scores = masked_scores(dot_right(heads_ref[1, 0:count], query), block)
            weights = jnp.exp(scores - total_ref[block:block + 1, :])
            soft = dot_right(heads_ref[2, 0:count], grad)
            dots = jnp.sum(weights * soft, axis=0, keepdims=True)
            moved = (weights * (soft - dots)).astype(jnp.bfloat16)
            for_key, for_value = dot(moved, query), dot(weights.astype(jnp.bfloat16), grad)
            if block == 7:
                key_sum[...] = for_key
                value_sum[...] = for_value
            else:
                key_sum[0:count] = key_sum[0:count] + for_key
                value_sum[0:count] = value_sum[0:count] + for_value
            for_query = dot(key_turned[:, 0:count], moved).T.astype(jnp.bfloat16).astype(jnp.float32) * 0.125
            for n, index in enumerate((2 * block, 2 * block + 1)):
                part = slice(index * 128, index * 128 + 128)
                back[index, 0:64] = pack_rows(for_query[n * 128:n * 128 + 128]).astype(jnp.bfloat16)
                back[index, 64:128] = pack_rows(key_sum[part]).astype(jnp.bfloat16)
                back[index, 128:192] = pack_rows(value_sum[part]).astype(jnp.bfloat16)
                back_to_member(group, back, home, send_b, recv_b, index)

    sent_to_heads(group, packed, landed, send_a, recv_a)
    finish_back(group, back, home, send_b, recv_b)
    for n, ref in enumerate((dq_ref, dk_ref, dv_ref)):
        for pair in range(6):
            top, low = join_pair(home[2 * pair, n * 64:n * 64 + 64], home[2 * pair + 1, n * 64:n * 64 + 64])
            ref[0:64, pair * 128:pair * 128 + 128] = top
            ref[64:128, pair * 128:pair * 128 + 128] = low


def attend_back(grad, heads, total, which):
    low = lambda *s: pltpu.VMEM(s, jnp.bfloat16)
    vmem = pl.BlockSpec(memory_space=pltpu.VMEM)
    return pl.pallas_call(
        attend_back_kernel,
        out_shape=(jax.ShapeDtypeStruct((128, 768), jnp.bfloat16),) * 3,
        in_specs=[vmem] * 3,
        out_specs=(vmem,) * 3,
        scratch_shapes=[
            low(12, 64, 128), low(16, 64, 128), low(16, 192, 128), low(12, 192, 128), low(2048, 64), low(64, 2048),
            pltpu.VMEM((2048, 64), jnp.float32), pltpu.VMEM((2048, 64), jnp.float32),
            pltpu.SemaphoreType.DMA((12,)), pltpu.SemaphoreType.DMA((16,)),
            pltpu.SemaphoreType.DMA((16,)), pltpu.SemaphoreType.DMA((12,)),
        ],
        compiler_params=pltpu.CompilerParams(collective_id=5 + which, has_side_effects=True, vmem_limit_bytes=48 * 2**20),
        name="attend_back",
    )(grad, heads, total)


epsilon = 1e-05


def normalize(residual, gain_row, shift_row):
    average = jnp.mean(residual, axis=-1, keepdims=True)
    centred = residual - average
    spread = jnp.mean(centred * centred, axis=-1, keepdims=True)
    return centred * lax.rsqrt(spread + epsilon) * gain_row + shift_row


def smooth_gate(values):
    return jax.nn.gelu(values, approximate=False)


def swap(value, axis):
    return lax.ppermute(value, axis, [(0, 1), (1, 0)])


def low(value):
    return value.astype(jnp.bfloat16)


def look_up(table, index):
    found = index[:, None] == jnp.arange(table.shape[0], dtype=jnp.int32)[None, :]
    return jnp.sum(jnp.where(found, table[None, :], 0), axis=1)


def layer_forward(entering, weights, bias_qv, bias_up, rows, layer):
    pair_qk, pair_vo, up_a, up_b, down_a, down_b = weights
    normed = low(normalize(entering, rows[0], rows[1]))
    qk = [dot(normed, pair_qk[t]) for t in range(2)]
    query = jnp.concatenate([qk[t][:, :384] for t in range(2)], axis=1)
    key = low(jnp.concatenate([qk[t][:, 384:] for t in range(2)], axis=1))
    value = jnp.concatenate([dot(normed, pair_vo[t][:, :384]) for t in range(2)], axis=1)
    query = low((query + bias_qv[0]) * 0.125)
    value = low(value + bias_qv[1])
    mixed, heads, total = attend(query, key, value, layer)
    hidden = entering + rows[2] + sum(
        dot_right(mixed[:, t * 384:t * 384 + 384], pair_vo[t][:, 384:]) for t in range(2))
    normed_two = low(normalize(hidden, rows[3], rows[4]))
    pre = [[dot(normed_two, up[t]) + bias_up[t, n * 768:n * 768 + 768] for n, up in enumerate((up_a, up_b))] for t in range(2)]
    active = [[low(smooth_gate(p)) for p in two] for two in pre]
    leaving = hidden + rows[5] + sum(
        dot_right(active[t][n], down[t]) for t in range(2) for n, down in enumerate((down_a, down_b)))
    return leaving, (entering, normed, mixed, heads, total, hidden, normed_two, pre, active)


def layer_backward(arriving, kept, weights, rows, layer):
    pair_qk, pair_vo, up_a, up_b, down_a, down_b = weights
    entering, normed, mixed, heads, total, hidden, normed_two, pre, active = kept
    carried = arriving.astype(jnp.float32)
    grad_pre = [[None, None], [None, None]]
    for t in range(2):
        for n, down in enumerate((down_a, down_b)):
            grad_active = dot(arriving, down[t])
            grad_pre[t][n] = low(jax.vjp(smooth_gate, pre[t][n])[1](grad_active)[0])
    grad_normed_two = sum(
        dot_right(grad_pre[t][n], up[t]) for t in range(2) for n, up in enumerate((up_a, up_b)))
    through_two, gain_two, shift_two = jax.vjp(normalize, hidden, rows[3], rows[4])[1](grad_normed_two)
    grad_hidden = carried + through_two
    hidden_low = low(grad_hidden)
    grad_mixed = low(jnp.concatenate([dot(hidden_low, pair_vo[t][:, 384:]) for t in range(2)], axis=1))
    grad_q, grad_k, grad_v = attend_back(grad_mixed, heads, total, layer)
    grad_normed = 0.0
    for t in range(2):
        cut = slice(t * 384, t * 384 + 384)
        grad_normed += dot_right(jnp.concatenate([grad_q[:, cut], grad_k[:, cut]], axis=1), pair_qk[t])
        grad_normed += dot_right(grad_v[:, cut], pair_vo[t][:, :384])
    through_one, gain_one, shift_one = jax.vjp(normalize, entering, rows[0], rows[1])[1](grad_normed)
    grad_input = grad_hidden + through_one

    def column_sum(value):
        return jnp.sum(value.astype(jnp.float32), axis=0)
    vectors = jnp.concatenate([
        gain_one, shift_one, column_sum(hidden_low), gain_two, shift_two, column_sum(carried),
        column_sum(grad_q), column_sum(grad_v),
    ] + [column_sum(grad_pre[t][n]) for t in range(2) for n in range(2)])
    return grad_input, vectors, (normed, hidden_low, normed_two, arriving, grad_q, grad_k, grad_v, mixed, grad_pre, active)


def delta_operands(parts, core):
    normed, hidden_low, normed_two, arriving, grad_q, grad_k, grad_v, mixed, grad_pre, active = parts

    def operands(core):
        pick = lambda a, b: jnp.where(core == 0, a, b)
        left = jnp.stack([pick(normed, normed_two), pick(normed, arriving), pick(hidden_low, arriving), pick(normed_two, arriving)])
        right = []
        cuts = [slice(t * 384, t * 384 + 384) for t in range(2)]
        right.append(jnp.stack([pick(jnp.concatenate([grad_q[:, cuts[t]], grad_k[:, cuts[t]]], axis=1), grad_pre[t][1]) for t in range(2)]))
        right.append(jnp.stack([pick(jnp.concatenate([grad_v[:, cuts[t]], mixed[:, cuts[t]]], axis=1), active[t][0]) for t in range(2)]))
        right.append(jnp.stack([pick(grad_pre[t][0], active[t][1]) for t in range(2)]))
        return left, jnp.stack(right)
    own = operands(core)
    other = swap(operands(1 - core), "c")
    return tuple(jnp.concatenate([a, b], axis=-2) for a, b in zip(own, other))


def on_device(tokens_in, cotangent, place, w_qkv, w_out, w_up, w_down, qv_bias, up_bias, vectors):
    section = lax.axis_index("s")
    core = lax.axis_index("c")
    half = lax.axis_index("t")
    inverse = jnp.sum(
        jnp.where(place[None, :] == jnp.arange(32, dtype=jnp.int32)[:, None], jnp.arange(32, dtype=jnp.int32)[None, :], 0),
        axis=1)

    shard = jnp.stack([
        jnp.concatenate([w_qkv[0, 0], w_qkv[0, 1]], axis=1), jnp.concatenate([w_qkv[0, 2], w_out[0].T], axis=1),
        w_up[0, :, :768], w_up[0, :, 768:], w_down[0, :768].T, w_down[0, 768:].T])
    own = jnp.where(core == 0, shard[:3], shard[3:])
    got = swap(jnp.where(core == 0, shard[3:], shard[:3]), "c")
    both = jnp.where(core == 0, jnp.concatenate([own, got], axis=1), jnp.concatenate([got, own], axis=1))
    micro = lax.rem(section + half, 2)
    device = jnp.arange(32, dtype=jnp.int32)
    y, z = device // 8, device // 2 % 4
    seat = ((y // 2) * 2 + z // 2) * 8 + (y % 2) * 4 + (z % 2) * 2 + device % 2
    mine = jnp.stack([jnp.where(micro == 0, a[0], a[1]) for a in (tokens_in, cotangent)])
    mine = mine.reshape(2, 32, 4, 768).transpose(1, 0, 2, 3).reshape(32, 48, 128)
    gathered, mine = gather_weights(look_up(inverse, seat), mine, both)
    mine = mine.reshape(32, 2, 4, 768).transpose(1, 0, 2, 3).reshape(2, 128, 768)
    gathered = gathered.reshape(6, 4, 768, 768)
    weights = [[[gathered[part, t * 2 + layer] for t in range(2)] for part in range(6)] for layer in range(2)]

    small = jnp.concatenate([
        vectors[0].astype(jnp.float32).reshape(-1),
        jnp.zeros((2, 2, 384), jnp.float32).at[:, half].set(qv_bias[0].reshape(2, 384).astype(jnp.float32)).reshape(-1) * 1.0,
        jnp.zeros((2, 1536), jnp.float32).at[half].set(up_bias[0].astype(jnp.float32)).reshape(-1),
    ])
    split = jnp.arange(4608 + 1536 + 3072) >= 4608
    partner = swap(small, "t")
    small = jnp.where(split, small + partner, small)
    beside = swap(small, "s")
    small = jnp.where(section == 0, jnp.stack([small, beside]), jnp.stack([beside, small]))
    rows = small[:, :4608].reshape(2, 6, 768)
    bias_qv = small[:, 4608:6144].reshape(2, 2, 768)
    bias_up = small[:, 6144:].reshape(2, 2, 1536)

    acts, kept = [], []
    entering = mine[0]
    for layer in range(2):
        leaving, state = layer_forward(entering.astype(jnp.float32), weights[layer], bias_qv[layer], bias_up[layer], rows[layer], layer)
        entering = low(leaving)
        acts.append(entering)
        kept.append(state)
    acts_kept = jnp.where(section == 0, acts[0], acts[1])
    acts_came = swap(jnp.where(section == 0, acts[1], acts[0]), "s")
    arriving = mine[1]
    input_grads, sums, operands = [None] * 2, [None] * 2, [None] * 2
    for layer in (1, 0):
        grad_input, sums[layer], parts = layer_backward(arriving, kept[layer], weights[layer], rows[layer], layer)
        operands[layer] = delta_operands(parts, core)
        arriving = low(grad_input)
        input_grads[layer] = arriving
    left, right = (jnp.stack(both) for both in zip(*operands))
    grads_kept = jnp.where(section == 0, input_grads[0], input_grads[1])
    grads_came = swap(jnp.where(section == 0, input_grads[1], input_grads[0]), "s")
    kept_rows, came_rows = jnp.stack([acts_kept, grads_kept]), jnp.stack([acts_came, grads_came])
    rows_out = jnp.where(micro == 0, jnp.stack([kept_rows, came_rows]), jnp.stack([came_rows, kept_rows]))
    rows_out = rows_out.reshape(4, 32, 4, 768).transpose(1, 0, 2, 3).reshape(32, 96, 128)
    seq, part = place // 8, place % 8
    holder = (seq // 2 * 2 + part // 4) * 8 + (seq % 2 * 2 + part // 2 % 2) * 2 + part % 2
    summed, rows_out, total = reduce_grads(holder, rows_out, jnp.stack(sums).reshape(144, 128), left, right)
    rows_out = rows_out.reshape(32, 4, 4, 768).transpose(1, 0, 2, 3).reshape(2, 2, 128, 768)
    acts_out = rows_out[:, 0][None]
    grads_out = rows_out[:, 1].astype(jnp.float32)[None]
    own_rows = lax.dynamic_slice_in_dim(summed, core * 24, 24, 1)
    got = swap(lax.dynamic_slice_in_dim(summed, (1 - core) * 24, 24, 1), "c")
    full = jnp.where(core == 0, jnp.concatenate([own_rows, got]), jnp.concatenate([got, own_rows]))
    grad_qkv = jnp.stack([full[0, :, :384], full[0, :, 384:], full[1, :, :384]])[None]
    grad_out = full[1, :, 384:].T[None]
    grad_up = jnp.concatenate([full[2], full[3]], axis=1)[None]
    grad_down = jnp.concatenate([full[4].T, full[5].T], axis=0)[None]

    total = total.reshape(2, 9216)
    total = jnp.where(section == 0, total[0], total[1])
    grad_vectors = total[:4608].reshape(1, 6, 768)
    grad_qv = lax.dynamic_slice_in_dim(total[4608:6144].reshape(2, 768), half * 384, 384, 1)[None]
    grad_up_bias = lax.dynamic_slice_in_dim(total[6144:], half * 1536, 1536)[None]

    return acts_out, grads_out, grad_qkv, grad_out, grad_up, grad_down, grad_qv, grad_up_bias, grad_vectors


def solution(mesh):
    fine = Mesh(mesh.devices.reshape(2, 4, 4, 2, 2), ("s", "y", "z", "c", "t"))
    dp = ("y", "z", "c")
    blocks = P(None, dp + ("t",), None)
    weights = (P("s", None, dp, "t"), P("s", "t", dp), P("s", dp, "t"), P("s", "t", dp))
    small = (P("s", None, "t"), P("s", "t"), P("s", None, None))
    rows = P("s", None, dp + ("t",), None)
    return jax.shard_map(
        on_device, mesh=fine,
        in_specs=(blocks, blocks, P()) + weights + small,
        out_specs=(rows, rows) + weights + small,
        check_vma=False)
```

```python
import functools

import jax
import jax.numpy as jnp
from jax import lax
from jax.experimental import pallas as pl
from jax.experimental.pallas import tpu as pltpu
from jax.sharding import Mesh, PartitionSpec as P
MESH = pl.DeviceIdType.MESH
ORDERS = ("xyz", "yzx", "zxy")
EARLY, LATE = slice(0, 384), slice(384, 768)


class Spot:
    def __init__(self):
        self.s, self.y, self.z, self.c, self.t = (lax.axis_index(a) for a in "syzct")
        self.x = self.t * 2 + self.s

    def at(self, axis):
        return {"x": self.x, "y": self.y, "z": self.z}[axis]

    def shifted(self, axis, by):
        return lax.rem(self.at(axis) + (by + 4), 4)

    def device(self, axis, by):
        x, y, z = self.x, self.y, self.z
        moved = self.shifted(axis, by)
        if axis == "x":
            x = moved
        elif axis == "y":
            y = moved
        else:
            z = moved
        return (lax.rem(x, 2), y, z, self.c, lax.div(x, 2))

    def sibling(self):
        return (self.s, self.y, self.z, 1 - self.c, self.t)


class Copies:
    def __init__(self, send_sems, recv_sems):
        self.send_sems, self.recv_sems, self.count = send_sems, recv_sems, 0
        self.sent = []

    def make(self, src, dst, device):
        n = self.count
        self.count += 1
        copy = pltpu.make_async_remote_copy(
            src_ref=src, dst_ref=dst, send_sem=self.send_sems.at[n], recv_sem=self.recv_sems.at[n],
            device_id=device, device_id_type=MESH)
        self.sent.append(copy)
        return copy

    def start(self, src, dst, device):
        copy = self.make(src, dst, device)
        copy.start()
        return copy

    def finish(self):
        for copy in self.sent:
            copy.wait_send()


class Move:
    def __init__(self, spot, order_ref, x_ref, out_ref, middle, turned, send_a, recv_a, send_b, recv_b):
        self.spot, self.order, self.turned, self.middle = spot, order_ref, turned, middle
        self.me = spot.y * 8 + spot.z * 2 + spot.c
        self.first = (x_ref, middle, send_a, recv_a)
        self.second = (turned, out_ref, send_b, recv_b)

    def member(self, index):
        return (self.spot.s, lax.div(index, 8), lax.rem(lax.div(index, 2), 4), lax.rem(index, 2), self.spot.t)

    def copy(self, which, n):
        source, target, send_sems, recv_sems = which
        to = lax.rem(self.me + n, 32)
        return pltpu.make_async_remote_copy(
            src_ref=source.at[to], dst_ref=target.at[self.me], send_sem=send_sems.at[n], recv_sem=recv_sems.at[n],
            device_id=self.member(to), device_id_type=MESH)

    def start(self, which):
        @pl.loop(1, 32)
        def _(n):
            self.copy(which, n).start()
        source, target = which[:2]
        target[self.me] = source[self.me]

    def arrive(self, which):
        source, target, send_sems, recv_sems = which

        @pl.loop(1, 32)
        def _(n):
            came = lax.rem(self.me + 32 - n, 32)
            pltpu.make_async_remote_copy(
                src_ref=source.at[came], dst_ref=target.at[came], send_sem=send_sems.at[n], recv_sem=recv_sems.at[n],
                device_id=self.member(came), device_id_type=MESH).wait_recv()

    def begin(self):
        self.start(self.first)

    def turn(self):
        self.arrive(self.first)

        @pl.loop(0, 32)
        def _(n):
            self.turned[n] = self.middle[self.order[n]]
        self.start(self.second)

    def end(self):
        self.arrive(self.second)

        @pl.loop(1, 32)
        def _(n):
            self.copy(self.first, n).wait_send()
            self.copy(self.second, n).wait_send()


def greet(spot, move, far):
    barrier = pltpu.get_barrier_semaphore()
    steps = (1, -1, 2) if far else (1, -1)
    for by in steps:
        pl.semaphore_signal(barrier, inc=1, device_id=spot.device("x", by), device_id_type=MESH)

    @pl.loop(1, 32)
    def _(n):
        pl.semaphore_signal(barrier, inc=1, device_id=move.member(lax.rem(move.me + n, 32)), device_id_type=MESH)
    pl.semaphore_wait(barrier, 31 + len(steps))


def move_scratch(shape):
    return [pltpu.VMEM(shape, jnp.bfloat16)] * 2 + [pltpu.SemaphoreType.DMA((32,))] * 4


def gather_kernel(order_ref, x_ref, w_ref, out_ref, moved_ref, send_sems, recv_sems, own_sems, *move_refs):
    spot = Spot()
    move = Move(spot, order_ref, x_ref, moved_ref, *move_refs)
    copies = Copies(send_sems, recv_sems)
    half = out_ref.at[spot.c]
    locals_ = []
    for k in range(3):
        local = pltpu.make_async_copy(w_ref.at[k], half.at[k, spot.x, spot.y, spot.z], own_sems.at[k])
        local.start()
        locals_.append(local)
    greet(spot, move, False)
    for local in locals_:
        local.wait()
    move.begin()

    def part(k, order, phase, position, piece=None):
        axis = order[phase]
        index = {}
        for n, name in enumerate(order):
            index[name] = slice(None) if n < phase else spot.at(name)
        index[axis] = position
        rows = slice(None)
        if piece is not None:
            start, size = piece
            if phase == 0:
                rows = pl.ds(start, size)
            else:
                index[order[0]] = pl.ds(start, size)
        return half.at[k, index["x"], index["y"], index["z"], rows]

    def ring(k, order, phase, position, piece, by):
        ref = part(k, order, phase, position, piece)
        return copies.start(ref, ref, spot.device(order[phase], by))

    def push(k, order, phase, position, piece):
        ref = part(k, order, phase, position, piece)
        return copies.start(ref, ref, spot.sibling())

    pushes = []
    for phase in range(3):
        if phase == 0:
            to_right, to_left = [(0, 32), (32, 16)], [(32, 16), (0, 32)]
            pass_right, pass_left = [(0, 32)], [(32, 16)]
        elif phase == 1:
            to_right, to_left = [(0, 2), (2, 2)], [(2, 2), (0, 2)]
            pass_right, pass_left = [(0, 2)], [(2, 2)]
        else:
            to_right, to_left = [(0, 1), (1, 1), (2, 1), (3, 1)], [(2, 1), (3, 1), (0, 1), (1, 1)]
            pass_right, pass_left = [(0, 1), (1, 1)], [(2, 1), (3, 1)]
        first = {}
        for n in range(len(to_right)):
            for k, order in enumerate(ORDERS):
                me = spot.at(order[phase])
                first[k, "r", to_right[n]] = ring(k, order, phase, me, to_right[n], 1)
                first[k, "l", to_left[n]] = ring(k, order, phase, me, to_left[n], -1)
        if phase == 1:
            move.turn()
        if phase == 2:
            for k, order in enumerate(ORDERS):
                pushes.append(push(k, order, phase, spot.at(order[phase]), None))
        second = []
        for n in range(len(to_right)):
            for k, order in enumerate(ORDERS):
                axis = order[phase]
                before, after = spot.shifted(axis, -1), spot.shifted(axis, 1)
                first[k, "r", to_right[n]].wait_recv()
                if to_right[n] in pass_right:
                    second.append((k, to_right[n], ring(k, order, phase, before, to_right[n], 1)))
                first[k, "l", to_left[n]].wait_recv()
                if to_left[n] in pass_left:
                    second.append((k, to_left[n], ring(k, order, phase, after, to_left[n], -1)))
                if phase == 2:
                    pushes.append(push(k, order, phase, before, to_right[n]))
                    pushes.append(push(k, order, phase, after, to_left[n]))
        for k, piece, copy in second:
            copy.wait_recv()
            if phase == 2:
                order = ORDERS[k]
                pushes.append(push(k, order, phase, spot.shifted(order[phase], 2), piece))
    for copy in pushes:
        copy.wait_recv()
    copies.finish()
    move.end()


def gather_weights(order, x, w):
    vmem = pl.BlockSpec(memory_space=pltpu.VMEM)
    return pl.pallas_call(
        gather_kernel,
        out_shape=(jax.ShapeDtypeStruct((2, 3, 4, 4, 4, 48, 768), jnp.bfloat16), jax.ShapeDtypeStruct(x.shape, x.dtype)),
        in_specs=[pl.BlockSpec(memory_space=pltpu.SMEM), vmem, pl.BlockSpec(memory_space=pl.ANY)],
        out_specs=(pl.BlockSpec(memory_space=pl.ANY), vmem),
        scratch_shapes=[pltpu.SemaphoreType.DMA((160,)), pltpu.SemaphoreType.DMA((160,)), pltpu.SemaphoreType.DMA((3,))]
        + move_scratch(x.shape),
        compiler_params=pltpu.CompilerParams(collective_id=1, has_side_effects=True),
        name="gather_weights",
    )(order, x, w)


def reduce_kernel(order_ref, x_ref, sums_0, sums_1, left_0, left_1, right_0, right_1, out_ref, moved_ref, total_ref,
                  sums_ref, g_ref, a0, b0, l0, r0, q0, a1, b1, l1, r1, q1, a2, b2, l2, r2, beside, slots, send_sems, recv_sems, *move_refs):
    spot = Spot()
    copies = Copies(send_sems, recv_sems)
    move = Move(spot, order_ref, x_ref, moved_ref, *move_refs)
    greet(spot, move, True)
    move.begin()
    sums_ref[0:12] = sums_0[...]
    sums_ref[12:24] = sums_1[...]
    vector_copies = [copies.start(sums_ref, beside, spot.sibling())]

    def spread(axis, n):
        me = spot.at(axis)
        return [copies.start(slots.at[n, me], slots.at[n, me], spot.device(axis, by)) for by in (1, -1, 2)]

    def gathered_sum(n):
        for copy in vector_copies.pop():
            copy.wait_recv()
        return (slots[n, 0] + slots[n, 1]) + (slots[n, 2] + slots[n, 3])

    def make_part(k):
        for layer, (left_ref, right_ref) in enumerate(((left_0, right_0), (left_1, right_1))):
            @pl.loop(0, 2)
            def _(half):
                def product(which, columns):
                    return lax.dot_general(
                        left_ref[which], right_ref[k, half, :, columns], (((0,), (0,)), ((), ())),
                        preferred_element_type=jnp.float32).astype(jnp.bfloat16).reshape(4, 4, 48, -1)
                x = half * 2 + layer
                if k == 1:
                    g_ref[k, x, :, :, :, EARLY] = product(1, EARLY)
                    g_ref[k, x, :, :, :, LATE] = product(2, LATE)
                else:
                    g_ref[k, x] = product(3 if k == 2 else 0, slice(0, 768))
    first_in, second_in = [(a0, b0), (a1, b1), (a2, b2)], [(l0, r0), (l1, r1), (l2, r2)]
    quarters = [q0, q1]

    def source(k, phase, order, position, piece=None):
        axis = order[phase]
        rest = order[phase + 1:]
        if phase == 0:
            index = {axis: position}
            for n, name in enumerate(rest):
                index[name] = slice(None)
            if piece is not None:
                index[max(rest)] = pl.ds(2 * piece, 2)
            return g_ref.at[k, index["x"], index["y"], index["z"]]
        held = quarters[phase - 1].at[k]
        names = [n for n in "xyz" if n in order[phase:]]
        index = []
        for name in names:
            if name == axis:
                index.append(position)
            elif piece is not None and name == rest[0]:
                index.append(pl.ds(2 * piece, 2))
            else:
                index.append(slice(None))
        rows = slice(None)
        if phase == 2 and piece is not None:
            rows = pl.ds(0, 32) if piece == 0 else pl.ds(32, 16)
        return held.at[tuple(index) + (rows,)]

    def slot(buffer, k, phase, order, piece):
        held = buffer.at[k]
        if piece is None:
            return held
        if phase == 2:
            return held.at[pl.ds(0, 32) if piece == 0 else pl.ds(32, 16)]
        rest = order[phase + 1:]
        names = [n for n in "xyz" if n in rest]
        return held.at[tuple(pl.ds(2 * piece, 2) if n == max(rest) else slice(None) for n in names)]

    def each(shape, body):
        lead = shape[:-2]
        if not lead:
            body(())
        elif len(lead) == 1:
            @pl.loop(0, lead[0])
            def _(i):
                body((i,))
        else:
            @pl.loop(0, lead[0])
            def _(i):
                @pl.loop(0, lead[1])
                def _(j):
                    body((i, j))

    for phase in range(3):
        started = []
        for k, gathered in enumerate(ORDERS):
            if phase == 0:
                make_part(k)
            order = gathered[::-1]
            axis = order[phase]
            right, left = spot.device(axis, 1), spot.device(axis, -1)
            a, b = first_in[phase]
            l, r = second_in[phase]
            far = spot.shifted(axis, 2)
            ca = copies.start(source(k, phase, order, far, 0), a.at[k], right)
            cb = copies.start(source(k, phase, order, far, 1), b.at[k], left)
            started.append([ca, cb])
        for k, gathered in enumerate(ORDERS):
            order = gathered[::-1]
            axis = order[phase]
            right, left = spot.device(axis, 1), spot.device(axis, -1)
            l, r = second_in[phase]
            after, before = spot.shifted(axis, 1), spot.shifted(axis, -1)
            started[k].append(copies.start(source(k, phase, order, after, 1), slot(l, k, phase, order, 1), right))
            started[k].append(copies.start(source(k, phase, order, before, 0), slot(r, k, phase, order, 0), left))
        for k, gathered in enumerate(ORDERS):
            order = gathered[::-1]
            axis = order[phase]
            right, left = spot.device(axis, 1), spot.device(axis, -1)
            a, b = first_in[phase]
            l, r = second_in[phase]
            after, before = spot.shifted(axis, 1), spot.shifted(axis, -1)

            def join(buffer, own):
                def body(i):
                    buffer[i] = (buffer[i].astype(jnp.float32) + own[i].astype(jnp.float32)).astype(jnp.bfloat16)
                each(buffer.shape, body)

            started[k][0].wait_recv()
            join(a.at[k], source(k, phase, order, after, 0))
            started[k].append(copies.start(a.at[k], slot(l, k, phase, order, 0), right))
            started[k][1].wait_recv()
            join(b.at[k], source(k, phase, order, before, 1))
            started[k].append(copies.start(b.at[k], slot(r, k, phase, order, 1), left))
        if phase == 0:
            vector_copies.pop().wait_recv()
            slots[0, spot.x] = sums_ref[...] + beside[...]
            vector_copies.append(spread("x", 0))
            move.turn()
        else:
            slots[phase, spot.at("xyz"[phase])] = gathered_sum(phase - 1)
            vector_copies.append(spread("xyz"[phase], phase))
        for k, gathered in enumerate(ORDERS):
            order = gathered[::-1]
            axis = order[phase]
            l, r = second_in[phase]
            for copy in started[k][2:]:
                copy.wait_recv()
            own = source(k, phase, order, spot.at(axis))
            left_in, right_in = l.at[k], r.at[k]
            target = out_ref.at[k] if phase == 2 else quarters[phase].at[k]

            def body(i):
                target[i] = (own[i].astype(jnp.float32) + left_in[i].astype(jnp.float32)
                             + right_in[i].astype(jnp.float32)).astype(target.dtype)
            each(target.shape, body)
    total_ref[...] = gathered_sum(2)
    copies.finish()
    move.end()


def reduce_grads(order, x, sums, lefts, rights):
    vmem = pl.BlockSpec(memory_space=pltpu.VMEM)
    return pl.pallas_call(
        reduce_kernel,
        out_shape=(jax.ShapeDtypeStruct((3, 48, 768), jnp.float32), jax.ShapeDtypeStruct(x.shape, x.dtype),
                   jax.ShapeDtypeStruct((24, 768), jnp.float32)),
        in_specs=[pl.BlockSpec(memory_space=pltpu.SMEM)] + [vmem] * 7,
        out_specs=(vmem,) * 3,
        scratch_shapes=[
            pltpu.VMEM((24, 768), jnp.float32), tiles(3, 4, 4, 4, 48, 768),
            tiles(3, 4, 2, 48, 768), tiles(3, 4, 2, 48, 768), tiles(3, 4, 4, 48, 768), tiles(3, 4, 4, 48, 768), tiles(3, 4, 4, 48, 768),
            tiles(3, 2, 48, 768), tiles(3, 2, 48, 768), tiles(3, 4, 48, 768), tiles(3, 4, 48, 768), tiles(3, 4, 48, 768),
            tiles(3, 32, 768), tiles(3, 16, 768), tiles(3, 48, 768), tiles(3, 48, 768),
            pltpu.VMEM((24, 768), jnp.float32), pltpu.VMEM((3, 4, 24, 768), jnp.float32),
            pltpu.SemaphoreType.DMA((80,)), pltpu.SemaphoreType.DMA((80,)),
        ] + move_scratch(x.shape),
        compiler_params=pltpu.CompilerParams(collective_id=2, has_side_effects=True, vmem_limit_bytes=56 * 2**20),
        name="reduce_grads",
    )(order, x, *sums, *lefts, *rights)


def lanes_swapped(tile):
    return pltpu.roll(tile, 64, 1)


def split_pair(tile):
    tile = tile.astype(jnp.float32)
    top, low = tile[0:64], tile[64:128]
    left = lax.broadcasted_iota(jnp.int32, (64, 128), 1) < 64
    first = jnp.where(left, top, lanes_swapped(low))
    second = jnp.where(left, lanes_swapped(top), low)
    return first.astype(jnp.bfloat16), second.astype(jnp.bfloat16)


def join_pair(first, second):
    first, second = first.astype(jnp.float32), second.astype(jnp.float32)
    left = lax.broadcasted_iota(jnp.int32, (64, 128), 1) < 64
    top = jnp.where(left, first, lanes_swapped(second))
    low = jnp.where(left, lanes_swapped(first), second)
    return top.astype(jnp.bfloat16), low.astype(jnp.bfloat16)


def pack_rows(block):
    return jnp.concatenate([block[0:64], block[64:128]], axis=1)


class Group:
    def __init__(self):
        self.s, self.y, self.z, self.c, self.t = (lax.axis_index(a) for a in "syzct")
        self.micro = lax.rem(self.s + self.t, 2)
        y, z = lax.rem(self.y, 2), lax.rem(self.z, 2)
        self.me = y * 8 + z * 4 + self.c * 2 + self.t
        self.active = jnp.logical_or(self.c == 0, lax.rem(y + z + self.t, 2) == 0)
        self.head = jnp.where(self.c == 0, y * 4 + z * 2 + self.t, 8 + y * 2 + z)

    def member(self, index):
        t = lax.rem(index, 2)
        y = lax.div(self.y, 2) * 2 + lax.div(index, 8)
        z = lax.div(self.z, 2) * 2 + lax.rem(lax.div(index, 4), 2)
        return (lax.rem(self.micro + t, 2), y, z, lax.rem(lax.div(index, 2), 2), t)

    def holder(self, head):
        late = head - 8
        y, z = lax.div(late, 2), lax.rem(late, 2)
        return jnp.where(
            head < 8, lax.div(head, 4) * 8 + lax.rem(lax.div(head, 2), 2) * 4 + lax.rem(head, 2),
            y * 8 + z * 4 + 2 + lax.rem(y + z, 2))

    def greet(self):
        barrier = pltpu.get_barrier_semaphore()

        @pl.loop(1, 16)
        def _(n):
            pl.semaphore_signal(barrier, inc=1, device_id=self.member(lax.rem(self.me + n, 16)), device_id_type=MESH)

    def met(self):
        pl.semaphore_wait(pltpu.get_barrier_semaphore(), 15)


def out_to_heads(group, packed, landed, send_sems, recv_sems):
    @pl.loop(0, 12)
    def _(n):
        head = lax.rem(group.me + n, 12)
        target = group.holder(head)

        @pl.when(target != group.me)
        def _():
            pltpu.make_async_remote_copy(
                src_ref=packed.at[head], dst_ref=landed.at[group.me], send_sem=send_sems.at[head],
                recv_sem=recv_sems.at[group.me], device_id=group.member(target), device_id_type=MESH).start()

    @pl.when(group.active)
    def _():
        landed[group.me] = packed[group.head]


def await_member(group, packed, landed, send_sems, recv_sems, index):
    @pl.when(group.me != index)
    def _():
        pltpu.make_async_remote_copy(
            src_ref=packed.at[0], dst_ref=landed.at[index], send_sem=send_sems.at[0],
            recv_sem=recv_sems.at[index], device_id=group.member(index), device_id_type=MESH).wait_recv()


def sent_to_heads(group, packed, landed, send_sems, recv_sems):
    @pl.loop(0, 12)
    def _(head):
        @pl.when(group.holder(head) != group.me)
        def _():
            pltpu.make_async_remote_copy(
                src_ref=packed.at[head], dst_ref=landed.at[group.me], send_sem=send_sems.at[head],
                recv_sem=recv_sems.at[group.me], device_id=group.member(group.holder(head)),
                device_id_type=MESH).wait_send()


def back_to_member(group, packed, landed, send_sems, recv_sems, index):
    @pl.when(group.me != index)
    def _():
        pltpu.make_async_remote_copy(
            src_ref=packed.at[index], dst_ref=landed.at[group.head], send_sem=send_sems.at[index],
            recv_sem=recv_sems.at[group.head], device_id=group.member(index), device_id_type=MESH).start()

    @pl.when(group.me == index)
    def _():
        landed[group.head] = packed[index]


def finish_back(group, packed, landed, send_sems, recv_sems):
    @pl.when(group.active)
    def _():
        @pl.loop(0, 16)
        def _(index):
            @pl.when(group.me != index)
            def _():
                pltpu.make_async_remote_copy(
                    src_ref=packed.at[index], dst_ref=landed.at[group.head], send_sem=send_sems.at[index],
                    recv_sem=recv_sems.at[group.head], device_id=group.member(index),
                    device_id_type=MESH).wait_send()

    @pl.loop(0, 12)
    def _(head):
        holder = group.holder(head)

        @pl.when(holder != group.me)
        def _():
            pltpu.make_async_remote_copy(
                src_ref=packed.at[0], dst_ref=landed.at[head], send_sem=send_sems.at[0],
                recv_sem=recv_sems.at[head], device_id=group.member(holder), device_id_type=MESH).wait_recv()


def dot_right(left, right):
    return lax.dot_general(left, right, (((1,), (1,)), ((), ())), preferred_element_type=jnp.float32)


def dot(left, right):
    return jnp.dot(left, right, preferred_element_type=jnp.float32)


def masked_scores(scores, block):
    key = lax.broadcasted_iota(jnp.int32, scores.shape, 0)
    query = lax.broadcasted_iota(jnp.int32, scores.shape, 1) + block * 256
    return jnp.where(key <= query, scores, -1e30)


epsilon = 1e-05


def low(value):
    return value.astype(jnp.bfloat16)


def standard(values):
    centred = values - jnp.mean(values, axis=-1, keepdims=True)
    factor = lax.rsqrt(jnp.mean(centred * centred, axis=-1, keepdims=True) + epsilon)
    return centred * factor, factor


def norm_back(values, gain, grad):
    unit, factor = standard(values)
    scaled = grad * gain
    through = factor * (scaled - jnp.mean(scaled, axis=-1, keepdims=True)
                        - unit * jnp.mean(scaled * unit, axis=-1, keepdims=True))
    return through, jnp.sum(grad * unit, axis=0, keepdims=True), jnp.sum(grad, axis=0, keepdims=True)


def normal_share(values):
    return 0.5 * (1.0 + lax.erf(values * 0.7071067811865476))


class Weights:
    def __init__(self, layer, source, held, sems, parts):
        self.held, self.copies = held, {}
        for part in parts:
            for half in range(2):
                copy = pltpu.make_async_copy(
                    source.at[part, half * 2 + layer], held.at[part, half], sems.at[part * 2 + half])
                copy.start()
                self.copies[part, half] = copy

    def ready(self, part, half):
        copy = self.copies.pop((part, half), None)
        if copy is not None:
            copy.wait()

    def __call__(self, part, half, columns=slice(0, 768)):
        self.ready(part, half)
        return self.held[part, half, :, columns]


def forward_kernel(layer, x_ref, rows_ref, w_ref,
                   out_ref, normed_ref, mixed_ref, heads_ref, total_ref, hidden_ref, normed_two_ref, pre_ref, active_ref,
                   held, w_sems, packed, landed, back, home, value_turned, send_a, recv_a, send_b, recv_b):
    group = Group()
    group.greet()
    weights = Weights(layer, w_ref, held, w_sems, range(6))
    entering = x_ref[...].astype(jnp.float32)
    rows = [rows_ref[n:n + 1, :] for n in range(12)]
    normed = low(standard(entering)[0] * rows[0] + rows[1])
    normed_ref[...] = normed

    def pack(kind, half, values):
        for pair in range(3):
            first, second = split_pair(low(values[:, pair * 128:pair * 128 + 128]))
            packed[half * 6 + 2 * pair, kind * 64:kind * 64 + 64] = first
            packed[half * 6 + 2 * pair + 1, kind * 64:kind * 64 + 64] = second
    for half in range(2):
        both = dot(normed, weights(0, half))
        cut = slice(half * 384, half * 384 + 384)
        pack(0, half, (both[:, EARLY] + rows[6][:, cut]) * 0.125)
        pack(1, half, both[:, LATE])
        pack(2, half, dot(normed, weights(1, half, EARLY)) + rows[7][:, cut])
    group.met()
    out_to_heads(group, packed, landed, send_a, recv_a)

    @pl.when(group.active)
    def _():
        for block in range(8):
            for index in (2 * block, 2 * block + 1):
                await_member(group, packed, landed, send_a, recv_a, index)
                for n in range(3):
                    tile = landed[index, n * 64:n * 64 + 64]
                    heads_ref[n, index * 128:index * 128 + 64] = tile[:, 0:64]
                    heads_ref[n, index * 128 + 64:index * 128 + 128] = tile[:, 64:128]
            own = slice(block * 256, block * 256 + 256)
            value_turned[:, own] = heads_ref[2, own].T
            count = block * 256 + 256
            scores = masked_scores(dot_right(heads_ref[1, 0:count], heads_ref[0, own]), block)
            largest = jnp.max(scores, axis=0, keepdims=True)
            shares = jnp.exp(scores - largest)
            total = jnp.sum(shares, axis=0, keepdims=True)
            total_ref[block:block + 1, :] = largest + jnp.log(total)
            mixed = dot(value_turned[:, 0:count], low(shares)) / total
            mixed = mixed.T
            for n, index in enumerate((2 * block, 2 * block + 1)):
                back[index] = low(pack_rows(mixed[n * 128:n * 128 + 128]))
                back_to_member(group, back, home, send_b, recv_b, index)

    sent_to_heads(group, packed, landed, send_a, recv_a)
    finish_back(group, back, home, send_b, recv_b)
    for pair in range(6):
        mixed_ref[0:64, pair * 128:pair * 128 + 128], mixed_ref[64:128, pair * 128:pair * 128 + 128] = join_pair(
            home[2 * pair], home[2 * pair + 1])
    hidden = entering + rows[2]
    for half in range(2):
        hidden += dot_right(mixed_ref[:, half * 384:half * 384 + 384], weights(1, half, LATE))
    hidden_ref[...] = hidden
    normed_two = low(standard(hidden)[0] * rows[3] + rows[4])
    normed_two_ref[...] = normed_two
    leaving = hidden + rows[5]
    for half in range(2):
        for n in range(2):
            cut = slice((half * 2 + n) * 768, (half * 2 + n) * 768 + 768)
            pre = dot(normed_two, weights(2 + n, half)) + rows[8 + half * 2 + n]
            pre_ref[:, cut] = pre
            active = low(pre * normal_share(pre))
            active_ref[:, cut] = active
            leaving += dot_right(active, weights(4 + n, half))
    out_ref[...] = low(leaving)


def tiles(*shape):
    return pltpu.VMEM(shape, jnp.bfloat16)


def shapes(kind, *all_shapes):
    return tuple(jax.ShapeDtypeStruct(shape, kind) for shape in all_shapes)


def layer_forward(entering, rows, gathered, layer):
    vmem = pl.BlockSpec(memory_space=pltpu.VMEM)
    block = (128, 768)
    return pl.pallas_call(
        functools.partial(forward_kernel, layer),
        out_shape=shapes(jnp.bfloat16, block, block, block, (3, 2048, 64)) + shapes(jnp.float32, (8, 256), block)
        + shapes(jnp.bfloat16, block) + shapes(jnp.float32, (128, 3072)) + shapes(jnp.bfloat16, (128, 3072)),
        in_specs=[vmem, vmem, pl.BlockSpec(memory_space=pl.ANY)],
        out_specs=(vmem,) * 9,
        scratch_shapes=[
            tiles(6, 2, 768, 768), pltpu.SemaphoreType.DMA((12,)),
            tiles(12, 192, 128), tiles(16, 192, 128), tiles(16, 64, 128), tiles(12, 64, 128), tiles(64, 2048),
            pltpu.SemaphoreType.DMA((12,)), pltpu.SemaphoreType.DMA((16,)),
            pltpu.SemaphoreType.DMA((16,)), pltpu.SemaphoreType.DMA((12,)),
        ],
        compiler_params=pltpu.CompilerParams(
            collective_id=3 + layer, has_side_effects=True, vmem_limit_bytes=56 * 2**20),
        name="layer_forward",
    )(entering, rows, gathered)


def backward_kernel(layer, arriving_ref, x_ref, rows_ref, normed_ref, mixed_ref, heads_ref, total_ref, hidden_ref,
                    normed_two_ref, pre_ref, active_ref, w_ref,
                    out_ref, sums_ref, left_ref, right_ref,
                    held, w_sems, packed, landed, back, home, grad_heads, key_turned, key_sum, value_sum,
                    grad_pre, left_out, right_out, send_a, recv_a, send_b, recv_b, pair_sems):
    group = Group()
    group.greet()
    weights = Weights(layer, w_ref, held, w_sems, (4, 5, 2, 3, 1, 0))
    rows = [rows_ref[n:n + 1, :] for n in range(12)]

    def role(core, own, other, value):
        @pl.when(group.c == core)
        def _():
            own[...] = value

        @pl.when(group.c != core)
        def _():
            other[...] = value

    def left_role(core, n, value):
        role(core, left_ref.at[n, 0:128], left_out.at[n], value)

    def right_role(core, n, half, value, columns=slice(0, 768)):
        role(core, right_ref.at[n, half, 0:128, columns], right_out.at[n, half, :, columns], value)

    def to_sibling(n, source, target):
        return pltpu.make_async_remote_copy(
            src_ref=source, dst_ref=target, send_sem=pair_sems.at[n], recv_sem=pair_sems.at[n + 2],
            device_id=(group.s, group.y, group.z, 1 - group.c, group.t), device_id_type=MESH)

    arriving = arriving_ref[...]
    carried = arriving.astype(jnp.float32)
    sums_ref[5:6, :] = jnp.sum(carried, axis=0, keepdims=True)
    grad_normed_two = jnp.zeros((128, 768), jnp.float32)
    for half in range(2):
        for n in range(2):
            place = half * 2 + n
            cut = slice(place * 768, place * 768 + 768)
            pre = pre_ref[:, cut]
            slope = normal_share(pre) + pre * (jnp.exp(pre * pre * -0.5) * 0.3989422804014327)
            grad = low(dot(arriving, weights(4 + n, half)) * slope)
            grad_pre[:, cut] = grad
            sums_ref[8 + place:9 + place, :] = jnp.sum(grad.astype(jnp.float32), axis=0, keepdims=True)
            grad_normed_two += dot_right(grad, weights(2 + n, half))
    hidden = hidden_ref[...]
    through, gain, shift = norm_back(hidden, rows[3], grad_normed_two)
    sums_ref[3:4, :], sums_ref[4:5, :] = gain, shift
    grad_hidden = carried + through
    hidden_low = low(grad_hidden)
    sums_ref[2:3, :] = jnp.sum(hidden_low.astype(jnp.float32), axis=0, keepdims=True)
    for half in range(2):
        grad_mixed = low(dot(hidden_low, weights(1, half, LATE)))
        for pair in range(3):
            packed[half * 6 + 2 * pair], packed[half * 6 + 2 * pair + 1] = split_pair(
                grad_mixed[:, pair * 128:pair * 128 + 128])
    group.met()
    out_to_heads(group, packed, landed, send_a, recv_a)

    normed, normed_two = normed_ref[...], normed_two_ref[...]
    for n, value in enumerate((normed, normed, hidden_low, normed_two)):
        left_role(0, n, value)
    for n, value in enumerate((normed_two, arriving, arriving, arriving)):
        left_role(1, n, value)
    left_copy = to_sibling(0, left_out, left_ref.at[:, 128:256])
    left_copy.start()
    for half in range(2):
        first, second = slice(half * 1536, half * 1536 + 768), slice(half * 1536 + 768, half * 1536 + 1536)
        right_role(0, 1, half, mixed_ref[:, half * 384:half * 384 + 384], LATE)
        right_role(0, 2, half, grad_pre[:, first])
        right_role(1, 0, half, grad_pre[:, second])
        right_role(1, 1, half, active_ref[:, first])
        right_role(1, 2, half, active_ref[:, second])

    @pl.when(group.active)
    def _():
        key_turned[...] = heads_ref[1].T
        for block in reversed(range(8)):
            for index in (2 * block, 2 * block + 1):
                await_member(group, packed, landed, send_a, recv_a, index)
                tile = landed[index]
                grad_heads[index * 128:index * 128 + 64] = tile[:, 0:64]
                grad_heads[index * 128 + 64:index * 128 + 128] = tile[:, 64:128]
            own = slice(block * 256, block * 256 + 256)
            count = block * 256 + 256
            query, grad = heads_ref[0, own], grad_heads[own]
            scores = masked_scores(dot_right(heads_ref[1, 0:count], query), block)
            shares = jnp.exp(scores - total_ref[block:block + 1, :])
            soft = dot_right(heads_ref[2, 0:count], grad)
            dots = jnp.sum(shares * soft, axis=0, keepdims=True)
            moved = low(shares * (soft - dots))
            for_key, for_value = dot(moved, query), dot(low(shares), grad)
            if block == 7:
                key_sum[...] = for_key
                value_sum[...] = for_value
            else:
                key_sum[0:count] = key_sum[0:count] + for_key
                value_sum[0:count] = value_sum[0:count] + for_value
            for_query = low(dot(key_turned[:, 0:count], moved).T).astype(jnp.float32) * 0.125
            for n, index in enumerate((2 * block, 2 * block + 1)):
                part = slice(index * 128, index * 128 + 128)
                back[index, 0:64] = low(pack_rows(for_query[n * 128:n * 128 + 128]))
                back[index, 64:128] = low(pack_rows(key_sum[part]))
                back[index, 128:192] = low(pack_rows(value_sum[part]))
                back_to_member(group, back, home, send_b, recv_b, index)

    sent_to_heads(group, packed, landed, send_a, recv_a)
    finish_back(group, back, home, send_b, recv_b)
    grad_normed = jnp.zeros((128, 768), jnp.float32)
    for half in range(2):
        def joined(kind):
            whole = []
            for pair in range(3):
                head = half * 6 + 2 * pair
                top, bottom = join_pair(home[head, kind * 64:kind * 64 + 64], home[head + 1, kind * 64:kind * 64 + 64])
                whole.append(jnp.concatenate([top, bottom], axis=0))
            return jnp.concatenate(whole, axis=1)
        grad_q, grad_k, grad_v = joined(0), joined(1), joined(2)
        cut = slice(half * 384, half * 384 + 384)
        sums_ref[6:7, cut] = jnp.sum(grad_q.astype(jnp.float32), axis=0, keepdims=True)
        sums_ref[7:8, cut] = jnp.sum(grad_v.astype(jnp.float32), axis=0, keepdims=True)
        right_role(0, 0, half, grad_q, EARLY)
        right_role(0, 0, half, grad_k, LATE)
        right_role(0, 1, half, grad_v, EARLY)
        grad_normed += dot_right(grad_q, weights(0, half, EARLY)) + dot_right(grad_k, weights(0, half, LATE))
        grad_normed += dot_right(grad_v, weights(1, half, EARLY))
    right_copy = to_sibling(1, right_out, right_ref.at[:, :, 128:256])
    right_copy.start()
    through, gain, shift = norm_back(x_ref[...].astype(jnp.float32), rows[0], grad_normed)
    sums_ref[0:1, :], sums_ref[1:2, :] = gain, shift
    out_ref[...] = low(grad_hidden + through)
    left_copy.wait()
    right_copy.wait()


def layer_backward(arriving, entering, rows, kept, gathered, layer):
    vmem = pl.BlockSpec(memory_space=pltpu.VMEM)
    block = (128, 768)
    return pl.pallas_call(
        functools.partial(backward_kernel, layer),
        out_shape=shapes(jnp.bfloat16, block) + shapes(jnp.float32, (12, 768))
        + shapes(jnp.bfloat16, (4, 256, 768), (3, 2, 256, 768)),
        in_specs=[vmem] * 11 + [pl.BlockSpec(memory_space=pl.ANY)],
        out_specs=(vmem,) * 4,
        scratch_shapes=[
            tiles(6, 2, 768, 768), pltpu.SemaphoreType.DMA((12,)),
            tiles(12, 64, 128), tiles(16, 64, 128), tiles(16, 192, 128), tiles(12, 192, 128), tiles(2048, 64), tiles(64, 2048),
            pltpu.VMEM((2048, 64), jnp.float32), pltpu.VMEM((2048, 64), jnp.float32),
            tiles(128, 3072), tiles(4, 128, 768), tiles(3, 2, 128, 768),
            pltpu.SemaphoreType.DMA((12,)), pltpu.SemaphoreType.DMA((16,)),
            pltpu.SemaphoreType.DMA((16,)), pltpu.SemaphoreType.DMA((12,)), pltpu.SemaphoreType.DMA((4,)),
        ],
        compiler_params=pltpu.CompilerParams(
            collective_id=5 + layer, has_side_effects=True, vmem_limit_bytes=56 * 2**20),
        name="layer_backward",
    )(arriving, entering, rows, *kept, gathered)


def swap(value, axis):
    return lax.ppermute(value, axis, [(0, 1), (1, 0)])


def look_up(table, index):
    found = index[:, None] == jnp.arange(table.shape[0], dtype=jnp.int32)[None, :]
    return jnp.sum(jnp.where(found, table[None, :], 0), axis=1)


def on_device(tokens_in, cotangent, place, w_qkv, w_out, w_up, w_down, qv_bias, up_bias, vectors):
    section = lax.axis_index("s")
    core = lax.axis_index("c")
    half = lax.axis_index("t")
    inverse = jnp.sum(
        jnp.where(place[None, :] == jnp.arange(32, dtype=jnp.int32)[:, None], jnp.arange(32, dtype=jnp.int32)[None, :], 0),
        axis=1)

    shard = jnp.stack([
        jnp.concatenate([w_qkv[0, 0], w_qkv[0, 1]], axis=1), jnp.concatenate([w_qkv[0, 2], w_out[0].T], axis=1),
        w_up[0, :, :768], w_up[0, :, 768:], w_down[0, :768].T, w_down[0, 768:].T])
    own = jnp.where(core == 0, shard[:3], shard[3:])
    got = swap(jnp.where(core == 0, shard[3:], shard[:3]), "c")
    both = jnp.where(core == 0, jnp.concatenate([own, got], axis=1), jnp.concatenate([got, own], axis=1))
    micro = lax.rem(section + half, 2)
    device = jnp.arange(32, dtype=jnp.int32)
    y, z = device // 8, device // 2 % 4
    seat = ((y // 2) * 2 + z // 2) * 8 + (y % 2) * 4 + (z % 2) * 2 + device % 2
    mine = jnp.stack([jnp.where(micro == 0, a[0], a[1]) for a in (tokens_in, cotangent)])
    mine = mine.reshape(2, 32, 4, 768).transpose(1, 0, 2, 3).reshape(32, 48, 128)
    gathered, mine = gather_weights(look_up(inverse, seat), mine, both)
    mine = mine.reshape(32, 2, 4, 768).transpose(1, 0, 2, 3).reshape(2, 128, 768)
    gathered = gathered.reshape(6, 4, 768, 768)

    small = jnp.concatenate([
        vectors[0].astype(jnp.float32).reshape(-1),
        jnp.zeros((2, 2, 384), jnp.float32).at[:, half].set(qv_bias[0].reshape(2, 384).astype(jnp.float32)).reshape(-1) * 1.0,
        jnp.zeros((2, 1536), jnp.float32).at[half].set(up_bias[0].astype(jnp.float32)).reshape(-1),
    ])
    split = jnp.arange(4608 + 1536 + 3072) >= 4608
    partner = swap(small, "t")
    small = jnp.where(split, small + partner, small)
    beside = swap(small, "s")
    small = jnp.where(section == 0, jnp.stack([small, beside]), jnp.stack([beside, small]))
    rows = small.reshape(2, 12, 768)

    acts, kept, entering = [], [], [mine[0]]
    for layer in range(2):
        leaving, *state = layer_forward(entering[layer], rows[layer], gathered, layer)
        entering.append(leaving)
        acts.append(leaving)
        kept.append(state)
    acts_kept = jnp.where(section == 0, acts[0], acts[1])
    acts_came = swap(jnp.where(section == 0, acts[1], acts[0]), "s")
    arriving = mine[1]
    input_grads, sums, lefts, rights = [None] * 2, [None] * 2, [None] * 2, [None] * 2
    for layer in (1, 0):
        arriving, sums[layer], lefts[layer], rights[layer] = layer_backward(
            arriving, entering[layer], rows[layer], kept[layer], gathered, layer)
        input_grads[layer] = arriving
    grads_kept = jnp.where(section == 0, input_grads[0], input_grads[1])
    grads_came = swap(jnp.where(section == 0, input_grads[1], input_grads[0]), "s")
    kept_rows, came_rows = jnp.stack([acts_kept, grads_kept]), jnp.stack([acts_came, grads_came])
    rows_out = jnp.where(micro == 0, jnp.stack([kept_rows, came_rows]), jnp.stack([came_rows, kept_rows]))
    rows_out = rows_out.reshape(4, 32, 4, 768).transpose(1, 0, 2, 3).reshape(32, 96, 128)
    seq, part = place // 8, place % 8
    holder = (seq // 2 * 2 + part // 4) * 8 + (seq % 2 * 2 + part // 2 % 2) * 2 + part % 2
    summed, rows_out, total = reduce_grads(holder, rows_out, sums, lefts, rights)
    rows_out = rows_out.reshape(32, 4, 4, 768).transpose(1, 0, 2, 3).reshape(2, 2, 128, 768)
    acts_out = rows_out[:, 0][None]
    grads_out = rows_out[:, 1].astype(jnp.float32)[None]
    own_rows = lax.dynamic_slice_in_dim(summed, core * 24, 24, 1)
    got = swap(lax.dynamic_slice_in_dim(summed, (1 - core) * 24, 24, 1), "c")
    full = jnp.where(core == 0, jnp.concatenate([own_rows, got]), jnp.concatenate([got, own_rows]))
    grad_qkv = jnp.stack([full[0, :, :384], full[0, :, 384:], full[1, :, :384]])[None]
    grad_out = full[1, :, 384:].T[None]
    grad_up = jnp.concatenate([full[2], full[3]], axis=1)[None]
    grad_down = jnp.concatenate([full[4].T, full[5].T], axis=0)[None]

    total = total.reshape(2, 9216)
    total = jnp.where(section == 0, total[0], total[1])
    grad_vectors = total[:4608].reshape(1, 6, 768)
    grad_qv = lax.dynamic_slice_in_dim(total[4608:6144].reshape(2, 768), half * 384, 384, 1)[None]
    grad_up_bias = lax.dynamic_slice_in_dim(total[6144:], half * 1536, 1536)[None]

    return acts_out, grads_out, grad_qkv, grad_out, grad_up, grad_down, grad_qv, grad_up_bias, grad_vectors


def solution(mesh):
    fine = Mesh(mesh.devices.reshape(2, 4, 4, 2, 2), ("s", "y", "z", "c", "t"))
    dp = ("y", "z", "c")
    blocks = P(None, dp + ("t",), None)
    weights = (P("s", None, dp, "t"), P("s", "t", dp), P("s", dp, "t"), P("s", "t", dp))
    small = (P("s", None, "t"), P("s", "t"), P("s", None, None))
    rows = P("s", None, dp + ("t",), None)
    return jax.shard_map(
        on_device, mesh=fine,
        in_specs=(blocks, blocks, P()) + weights + small,
        out_specs=(rows, rows) + weights + small,
        check_vma=False)
```

```python
import functools

import jax
import jax.numpy as jnp
from jax import lax
from jax.experimental import pallas as pl
from jax.experimental.pallas import tpu as pltpu
from jax.sharding import Mesh, PartitionSpec as P
MESH = pl.DeviceIdType.MESH
ORDERS = ("xyz", "yzx", "zxy")
EARLY, LATE = slice(0, 384), slice(384, 768)


class Spot:
    def __init__(self):
        self.s, self.y, self.z, self.c, self.t = (lax.axis_index(a) for a in "syzct")
        self.x = self.t * 2 + self.s

    def at(self, axis):
        return {"x": self.x, "y": self.y, "z": self.z}[axis]

    def shifted(self, axis, by):
        return lax.rem(self.at(axis) + (by + 4), 4)

    def device(self, axis, by):
        x, y, z = self.x, self.y, self.z
        moved = self.shifted(axis, by)
        if axis == "x":
            x = moved
        elif axis == "y":
            y = moved
        else:
            z = moved
        return (lax.rem(x, 2), y, z, self.c, lax.div(x, 2))

    def fourth(self, section_by, core_by):
        return (lax.rem(self.s + section_by, 2), self.y, self.z, lax.rem(self.c + core_by, 2), self.t)

    def sibling(self):
        return (self.s, self.y, self.z, 1 - self.c, self.t)


class Copies:
    def __init__(self, send_sems, recv_sems):
        self.send_sems, self.recv_sems, self.count = send_sems, recv_sems, 0
        self.sent = []

    def make(self, src, dst, device):
        n = self.count
        self.count += 1
        copy = pltpu.make_async_remote_copy(
            src_ref=src, dst_ref=dst, send_sem=self.send_sems.at[n], recv_sem=self.recv_sems.at[n],
            device_id=device, device_id_type=MESH)
        self.sent.append(copy)
        return copy

    def start(self, src, dst, device):
        copy = self.make(src, dst, device)
        copy.start()
        return copy

    def finish(self):
        for copy in self.sent:
            copy.wait_send()


class Move:
    def __init__(self, spot, order_ref, x_ref, out_ref, middle, turned, send_a, recv_a, send_b, recv_b):
        self.spot, self.order, self.turned, self.middle = spot, order_ref, turned, middle
        self.me = spot.y * 8 + spot.z * 2 + spot.c
        self.first = (x_ref, middle, send_a, recv_a)
        self.second = (turned, out_ref, send_b, recv_b)
        self.leads = range(x_ref.shape[0]) if len(x_ref.shape) == 4 else None

    def member(self, index):
        return (self.spot.s, lax.div(index, 8), lax.rem(lax.div(index, 2), 4), lax.rem(index, 2), self.spot.t)

    def piece(self, ref, index):
        return ref.at[index] if self.leads is None else ref.at[:, index]

    def local(self, target, to, source, index):
        if self.leads is None:
            target[to] = source[index]
        else:
            for lead in self.leads:
                target[lead, to] = source[lead, index]

    def copy(self, which, n):
        source, target, send_sems, recv_sems = which
        to = lax.rem(self.me + n, 32)
        return pltpu.make_async_remote_copy(
            src_ref=self.piece(source, to), dst_ref=self.piece(target, self.me), send_sem=send_sems.at[n],
            recv_sem=recv_sems.at[n], device_id=self.member(to), device_id_type=MESH)

    def start(self, which):
        @pl.loop(1, 32)
        def _(n):
            self.copy(which, n).start()
        source, target = which[:2]
        self.local(target, self.me, source, self.me)

    def arrive(self, which):
        source, target, send_sems, recv_sems = which

        @pl.loop(1, 32)
        def _(n):
            came = lax.rem(self.me + 32 - n, 32)
            pltpu.make_async_remote_copy(
                src_ref=self.piece(source, came), dst_ref=self.piece(target, came), send_sem=send_sems.at[n],
                recv_sem=recv_sems.at[n], device_id=self.member(came), device_id_type=MESH).wait_recv()

    def begin(self):
        self.start(self.first)

    def turn(self):
        self.arrive(self.first)

        @pl.loop(0, 32)
        def _(n):
            self.local(self.turned, n, self.middle, self.order[n])
        self.start(self.second)

    def end(self):
        self.arrive(self.second)

        @pl.loop(1, 32)
        def _(n):
            self.copy(self.first, n).wait_send()
            self.copy(self.second, n).wait_send()


def greet(spot, move):
    barrier = pltpu.get_barrier_semaphore()
    for peer in [spot.device("x", by) for by in (1, -1, 2)] + [spot.fourth(1, 1)]:
        pl.semaphore_signal(barrier, inc=1, device_id=peer, device_id_type=MESH)

    @pl.loop(1, 32)
    def _(n):
        pl.semaphore_signal(barrier, inc=1, device_id=move.member(lax.rem(move.me + n, 32)), device_id_type=MESH)
    pl.semaphore_wait(barrier, 35)


def move_scratch(shape):
    return [pltpu.VMEM(shape, jnp.bfloat16)] * 2 + [pltpu.SemaphoreType.DMA((32,))] * 4


FOURTHS = ((0, 1), (1, 0), (1, 1))


def gather_steps(spot, copies, out_ref):
    half = out_ref.at[spot.c]

    def part(k, order, phase, position, piece=None):
        axis = order[phase]
        index = {}
        for n, name in enumerate(order):
            index[name] = slice(None) if n < phase else spot.at(name)
        index[axis] = position
        rows = slice(None)
        if piece is not None:
            start, size = piece
            if phase == 0:
                rows = pl.ds(start, size)
            else:
                index[order[0]] = pl.ds(start, size)
        return half.at[k, index["x"], index["y"], index["z"], rows]

    def ring(k, order, phase, position, piece, by):
        ref = part(k, order, phase, position, piece)
        return copies.start(ref, ref, spot.device(order[phase], by))

    def push(k, order, phase, position, piece):
        ref = part(k, order, phase, position, piece)
        return copies.start(ref, ref, spot.sibling())

    pushes = []
    for phase in range(3):
        if phase == 0:
            to_right, to_left = [(0, 32), (32, 16)], [(32, 16), (0, 32)]
            pass_right, pass_left = [(0, 32)], [(32, 16)]
        elif phase == 1:
            to_right, to_left = [(0, 2), (2, 2)], [(2, 2), (0, 2)]
            pass_right, pass_left = [(0, 2)], [(2, 2)]
        else:
            to_right, to_left = [(0, 1), (1, 1), (2, 1), (3, 1)], [(2, 1), (3, 1), (0, 1), (1, 1)]
            pass_right, pass_left = [(0, 1), (1, 1)], [(2, 1), (3, 1)]
        first = {}
        for n in range(len(to_right)):
            for k, order in enumerate(ORDERS):
                me = spot.at(order[phase])
                first[k, "r", to_right[n]] = ring(k, order, phase, me, to_right[n], 1)
                first[k, "l", to_left[n]] = ring(k, order, phase, me, to_left[n], -1)
        if phase == 2:
            for k, order in enumerate(ORDERS):
                pushes.append(push(k, order, phase, spot.at(order[phase]), None))
        yield
        second = []
        for n in range(len(to_right)):
            for k, order in enumerate(ORDERS):
                axis = order[phase]
                before, after = spot.shifted(axis, -1), spot.shifted(axis, 1)
                first[k, "r", to_right[n]].wait_recv()
                if to_right[n] in pass_right:
                    second.append((k, to_right[n], ring(k, order, phase, before, to_right[n], 1)))
                first[k, "l", to_left[n]].wait_recv()
                if to_left[n] in pass_left:
                    second.append((k, to_left[n], ring(k, order, phase, after, to_left[n], -1)))
                if phase == 2:
                    pushes.append(push(k, order, phase, before, to_right[n]))
                    pushes.append(push(k, order, phase, after, to_left[n]))
            yield
        for k, piece, copy in second:
            copy.wait_recv()
            if phase == 2:
                order = ORDERS[k]
                pushes.append(push(k, order, phase, spot.shifted(order[phase], 2), piece))
    for copy in pushes:
        copy.wait_recv()
    copies.finish()


def place_own(spot, block_ref, out_ref, sems):
    return [pltpu.make_async_copy(block_ref.at[k], out_ref.at[spot.c, k, spot.x, spot.y, spot.z], sems.at[k]) for k in range(3)]


GATHERED = (2, 3, 4, 4, 4, 48, 384)


def gather_scratch():
    return [pltpu.SemaphoreType.DMA((112,)), pltpu.SemaphoreType.DMA((112,)), pltpu.SemaphoreType.DMA((3,))]


def start_kernel(order_ref, x_ref, small_ref, shard_ref, w_ref, block_ref, moved_ref, rows_ref,
                 fourths, own, smalls, pair_sems, send_sems, recv_sems, own_sems, *move_refs):
    spot = Spot()
    move = Move(spot, order_ref, x_ref, moved_ref, *move_refs)
    copies = Copies(send_sems, recv_sems)
    greet(spot, move)
    near = []
    for n, (section_by, core_by) in enumerate(FOURTHS):
        section, core = lax.rem(spot.s + section_by, 2), lax.rem(spot.c + core_by, 2)
        near.append(pltpu.make_async_remote_copy(
            src_ref=shard_ref.at[pl.ds((core * 2 + section) * 3, 3)], dst_ref=fourths.at[spot.s * 2 + spot.c],
            send_sem=pair_sems.at[n], recv_sem=pair_sems.at[n + 6],
            device_id=spot.fourth(section_by, core_by), device_id_type=MESH))
    for n, by in enumerate((1, -1, 2)):
        near.append(pltpu.make_async_remote_copy(
            src_ref=small_ref, dst_ref=smalls.at[spot.x], send_sem=pair_sems.at[n + 3], recv_sem=pair_sems.at[n + 9],
            device_id=spot.device("x", by), device_id_type=MESH))
    for copy in near:
        copy.start()
    move.begin()
    fourths[spot.s * 2 + spot.c] = shard_ref[pl.ds((spot.c * 2 + spot.s) * 3, 3)]
    smalls[spot.x] = small_ref[...]
    for copy in near[:3]:
        copy.wait_recv()

    def both_cores(layer, k):
        return jnp.concatenate([fourths[layer * 2, k], fourths[layer * 2 + 1, k]], axis=0).astype(jnp.bfloat16)
    for k in range(3):
        own[k] = both_cores(0, k)
    placed = place_own(spot, own, w_ref, own_sems)
    for copy in placed:
        copy.start()
    for copy in placed:
        copy.wait()
    steps = gather_steps(spot, copies, w_ref)
    next(steps)
    for k in range(3):
        block_ref[k] = both_cores(1, k)
    for copy in near[3:]:
        copy.wait_recv()
    for layer in range(2):
        first, second = smalls[layer].astype(jnp.float32), smalls[layer + 2].astype(jnp.float32)
        rows_ref[layer, 0:6] = first[0:6]
        rows_ref[layer, 6:7] = jnp.concatenate([first[6:7, EARLY], second[6:7, EARLY]], axis=1)
        rows_ref[layer, 7:8] = jnp.concatenate([first[6:7, LATE], second[6:7, LATE]], axis=1)
        rows_ref[layer, 8:10] = first[7:9]
        rows_ref[layer, 10:12] = second[7:9]
    for _ in range(3):
        next(steps)
    move.turn()
    for _ in steps:
        pass
    move.end()
    for copy in near:
        copy.wait_send()


def start(order, x, small, shard):
    vmem, any_place = pl.BlockSpec(memory_space=pltpu.VMEM), pl.BlockSpec(memory_space=pl.ANY)
    return pl.pallas_call(
        start_kernel,
        out_shape=shapes(jnp.bfloat16, GATHERED, (3, 48, 384), x.shape) + shapes(jnp.float32, (2, 12, 768)),
        in_specs=[pl.BlockSpec(memory_space=pltpu.SMEM), vmem, vmem, vmem],
        out_specs=(any_place, vmem, vmem, vmem),
        scratch_shapes=[
            pltpu.VMEM((4, 3, 24, 384), jnp.float32), tiles(3, 48, 384), tiles(4, 16, 768), pltpu.SemaphoreType.DMA((12,)),
        ] + gather_scratch() + move_scratch(x.shape),
        compiler_params=pltpu.CompilerParams(collective_id=1, has_side_effects=True),
        name="start",
    )(order, x, small, shard)


SLOTS = (0, 0, 1, 2, 3, 3)


def reduce_steps(spot, copies, left_ref, right_ref, out_ref, beside_steps,
                 g_ref, a0, b0, l0, r0, q0, a1, b1, l1, r1, q1, a2, b2, l2, r2):
    def make_part(k):
        for section in range(2):
            @pl.loop(0, 2)
            def _(half):
                unit = section * 3 + k
                product = lax.dot_general(
                    left_ref[SLOTS[unit]], right_ref[unit, half], (((0,), (0,)), ((), ())),
                    preferred_element_type=jnp.float32)
                g_ref[k, half * 2 + section] = low(product).reshape(4, 4, 48, 384)
    first_in, second_in = [(a0, b0), (a1, b1), (a2, b2)], [(l0, r0), (l1, r1), (l2, r2)]
    quarters = [q0, q1]

    def source(k, phase, order, position, piece=None):
        axis = order[phase]
        rest = order[phase + 1:]
        if phase == 0:
            index = {axis: position}
            for n, name in enumerate(rest):
                index[name] = slice(None)
            if piece is not None:
                index[max(rest)] = pl.ds(2 * piece, 2)
            return g_ref.at[k, index["x"], index["y"], index["z"]]
        held = quarters[phase - 1].at[k]
        names = [n for n in "xyz" if n in order[phase:]]
        index = []
        for name in names:
            if name == axis:
                index.append(position)
            elif piece is not None and name == rest[0]:
                index.append(pl.ds(2 * piece, 2))
            else:
                index.append(slice(None))
        rows = slice(None)
        if phase == 2 and piece is not None:
            rows = pl.ds(0, 32) if piece == 0 else pl.ds(32, 16)
        return held.at[tuple(index) + (rows,)]

    def slot(buffer, k, phase, order, piece):
        held = buffer.at[k]
        if piece is None:
            return held
        if phase == 2:
            return held.at[pl.ds(0, 32) if piece == 0 else pl.ds(32, 16)]
        rest = order[phase + 1:]
        names = [n for n in "xyz" if n in rest]
        return held.at[tuple(pl.ds(2 * piece, 2) if n == max(rest) else slice(None) for n in names)]

    def each(shape, body):
        lead = shape[:-2]
        if not lead:
            body(())
        elif len(lead) == 1:
            @pl.loop(0, lead[0])
            def _(i):
                body((i,))
        else:
            @pl.loop(0, lead[0])
            def _(i):
                @pl.loop(0, lead[1])
                def _(j):
                    body((i, j))

    for phase in range(3):
        started = []
        for k, gathered in enumerate(ORDERS):
            if phase == 0:
                make_part(k)
            order = gathered[::-1]
            axis = order[phase]
            right, left = spot.device(axis, 1), spot.device(axis, -1)
            a, b = first_in[phase]
            l, r = second_in[phase]
            far = spot.shifted(axis, 2)
            ca = copies.start(source(k, phase, order, far, 0), a.at[k], right)
            cb = copies.start(source(k, phase, order, far, 1), b.at[k], left)
            started.append([ca, cb])
            if phase == 0:
                yield
        for k, gathered in enumerate(ORDERS):
            order = gathered[::-1]
            axis = order[phase]
            right, left = spot.device(axis, 1), spot.device(axis, -1)
            l, r = second_in[phase]
            after, before = spot.shifted(axis, 1), spot.shifted(axis, -1)
            started[k].append(copies.start(source(k, phase, order, after, 1), slot(l, k, phase, order, 1), right))
            started[k].append(copies.start(source(k, phase, order, before, 0), slot(r, k, phase, order, 0), left))
        yield
        for k, gathered in enumerate(ORDERS):
            order = gathered[::-1]
            axis = order[phase]
            right, left = spot.device(axis, 1), spot.device(axis, -1)
            a, b = first_in[phase]
            l, r = second_in[phase]
            after, before = spot.shifted(axis, 1), spot.shifted(axis, -1)

            def join(buffer, own):
                def body(i):
                    buffer[i] = (buffer[i].astype(jnp.float32) + own[i].astype(jnp.float32)).astype(jnp.bfloat16)
                each(buffer.shape, body)

            started[k][0].wait_recv()
            join(a.at[k], source(k, phase, order, after, 0))
            started[k].append(copies.start(a.at[k], slot(l, k, phase, order, 0), right))
            started[k][1].wait_recv()
            join(b.at[k], source(k, phase, order, before, 1))
            started[k].append(copies.start(b.at[k], slot(r, k, phase, order, 1), left))
            yield
        beside_steps(phase)
        for k, gathered in enumerate(ORDERS):
            order = gathered[::-1]
            axis = order[phase]
            l, r = second_in[phase]
            for copy in started[k][2:]:
                copy.wait_recv()
            own = source(k, phase, order, spot.at(axis))
            left_in, right_in = l.at[k], r.at[k]
            target = out_ref.at[k] if phase == 2 else quarters[phase].at[k]

            def body(i):
                target[i] = (own[i].astype(jnp.float32) + left_in[i].astype(jnp.float32)
                             + right_in[i].astype(jnp.float32)).astype(target.dtype)
            each(target.shape, body)
            yield
    copies.finish()


def reduce_scratch():
    return [
        tiles(3, 4, 4, 4, 48, 384),
        tiles(3, 4, 2, 48, 384), tiles(3, 4, 2, 48, 384), tiles(3, 4, 4, 48, 384), tiles(3, 4, 4, 48, 384), tiles(3, 4, 4, 48, 384),
        tiles(3, 2, 48, 384), tiles(3, 2, 48, 384), tiles(3, 4, 48, 384), tiles(3, 4, 48, 384), tiles(3, 4, 48, 384),
        tiles(3, 32, 384), tiles(3, 16, 384), tiles(3, 48, 384), tiles(3, 48, 384),
    ]


REDUCED = 15


def end_kernel(order_ref, x_ref, sums_0, sums_1, left_ref, right_ref, partial_ref, out_ref, moved_ref, total_ref,
               sums_ref, beside, slots, both, mine, pair_sems, send_sems, recv_sems, *refs):
    spot = Spot()
    copies = Copies(send_sems, recv_sems)
    move = Move(spot, order_ref, mine, moved_ref, *refs[REDUCED:])
    greet(spot, move)
    micro = lax.rem(spot.s + spot.t, 2)
    exchange = pltpu.make_async_remote_copy(
        src_ref=x_ref.at[1 - spot.s], dst_ref=mine.at[micro], send_sem=pair_sems.at[0], recv_sem=pair_sems.at[1],
        device_id=spot.fourth(1, 0), device_id_type=MESH)
    exchange.start()
    sums_ref[0:12] = sums_0[...]
    sums_ref[12:24] = sums_1[...]
    vector_copies = [copies.start(sums_ref, beside, spot.sibling())]
    mine[micro] = x_ref[spot.s]

    def spread(axis, n):
        me = spot.at(axis)
        return [copies.start(slots.at[n, me], slots.at[n, me], spot.device(axis, by)) for by in (1, -1, 2)]

    def gathered_sum(n):
        for copy in vector_copies.pop():
            copy.wait_recv()
        return (slots[n, 0] + slots[n, 1]) + (slots[n, 2] + slots[n, 3])

    def beside_steps(phase):
        if phase == 0:
            vector_copies.pop().wait_recv()
            slots[0, spot.x] = sums_ref[...] + beside[...]
            vector_copies.append(spread("x", 0))
            move.turn()
        else:
            slots[phase, spot.at("xyz"[phase])] = gathered_sum(phase - 1)
            vector_copies.append(spread("xyz"[phase], phase))

    steps = reduce_steps(spot, copies, left_ref, right_ref, both.at[0], beside_steps, *refs[:REDUCED])
    for _ in range(4):
        next(steps)
    exchange.wait_recv()
    move.begin()
    for _ in steps:
        pass
    total_ref[...] = gathered_sum(2)
    both[1] = partial_ref[...]
    near = []
    for n, (section_by, core_by) in enumerate(FOURTHS):
        section, core = lax.rem(spot.s + section_by, 2), lax.rem(spot.c + core_by, 2)
        near.append(pltpu.make_async_remote_copy(
            src_ref=both.at[section, :, pl.ds(pl.multiple_of(core * 24, 8), 24)],
            dst_ref=out_ref.at[pl.ds((spot.c * 2 + spot.s) * 3, 3)],
            send_sem=pair_sems.at[n + 2], recv_sem=pair_sems.at[n + 5],
            device_id=spot.fourth(section_by, core_by), device_id_type=MESH))
    for copy in near:
        copy.start()
    for core in range(2):
        @pl.when(spot.c == core)
        def _():
            out_ref[pl.ds((spot.c * 2 + spot.s) * 3, 3)] = both[spot.s, :, core * 24:core * 24 + 24]
    move.end()
    exchange.wait_send()
    for copy in near:
        copy.wait()


def end(order, x, sums, left, right, partial):
    vmem = pl.BlockSpec(memory_space=pltpu.VMEM)
    return pl.pallas_call(
        end_kernel,
        out_shape=shapes(jnp.float32, (12, 24, 384)) + shapes(jnp.bfloat16, x.shape) + shapes(jnp.float32, (24, 768)),
        in_specs=[pl.BlockSpec(memory_space=pltpu.SMEM)] + [vmem] * 6,
        out_specs=(vmem,) * 3,
        scratch_shapes=[
            pltpu.VMEM((24, 768), jnp.float32), pltpu.VMEM((24, 768), jnp.float32), pltpu.VMEM((3, 4, 24, 768), jnp.float32),
            pltpu.VMEM((2, 3, 48, 384), jnp.float32), pltpu.VMEM(x.shape, x.dtype), pltpu.SemaphoreType.DMA((8,)),
            pltpu.SemaphoreType.DMA((80,)), pltpu.SemaphoreType.DMA((80,)),
        ] + reduce_scratch() + move_scratch(x.shape),
        compiler_params=pltpu.CompilerParams(collective_id=2, has_side_effects=True, vmem_limit_bytes=56 * 2**20),
        name="end",
    )(order, x, *sums, left, right, partial)


def lanes_swapped(tile):
    return pltpu.roll(tile, 64, 1)


def split_pair(tile):
    tile = tile.astype(jnp.float32)
    top, low = tile[0:64], tile[64:128]
    left = lax.broadcasted_iota(jnp.int32, (64, 128), 1) < 64
    first = jnp.where(left, top, lanes_swapped(low))
    second = jnp.where(left, lanes_swapped(top), low)
    return first.astype(jnp.bfloat16), second.astype(jnp.bfloat16)


def join_pair(first, second):
    first, second = first.astype(jnp.float32), second.astype(jnp.float32)
    left = lax.broadcasted_iota(jnp.int32, (64, 128), 1) < 64
    top = jnp.where(left, first, lanes_swapped(second))
    low = jnp.where(left, lanes_swapped(first), second)
    return top.astype(jnp.bfloat16), low.astype(jnp.bfloat16)


def pack_rows(block):
    return jnp.concatenate([block[0:64], block[64:128]], axis=1)


class Group:
    def __init__(self):
        self.s, self.y, self.z, self.c, self.t = (lax.axis_index(a) for a in "syzct")
        self.micro = lax.rem(self.s + self.t, 2)
        y, z = lax.rem(self.y, 2), lax.rem(self.z, 2)
        self.me = y * 8 + z * 4 + self.c * 2 + self.t
        self.active = jnp.logical_or(self.c == 0, lax.rem(y + z + self.t, 2) == 0)
        self.head = jnp.where(self.c == 0, y * 4 + z * 2 + self.t, 8 + y * 2 + z)

    def member(self, index):
        t = lax.rem(index, 2)
        y = lax.div(self.y, 2) * 2 + lax.div(index, 8)
        z = lax.div(self.z, 2) * 2 + lax.rem(lax.div(index, 4), 2)
        return (lax.rem(self.micro + t, 2), y, z, lax.rem(lax.div(index, 2), 2), t)

    def holder(self, head):
        late = head - 8
        y, z = lax.div(late, 2), lax.rem(late, 2)
        return jnp.where(
            head < 8, lax.div(head, 4) * 8 + lax.rem(lax.div(head, 2), 2) * 4 + lax.rem(head, 2),
            y * 8 + z * 4 + 2 + lax.rem(y + z, 2))

    def greet(self, ring):
        barrier = pltpu.get_barrier_semaphore()
        self.signals = 15
        if ring:
            spot = Spot()
            for axis in "xyz":
                for by in (1, -1):
                    self.signals += 1
                    pl.semaphore_signal(barrier, inc=1, device_id=spot.device(axis, by), device_id_type=MESH)

        @pl.loop(1, 16)
        def _(n):
            pl.semaphore_signal(barrier, inc=1, device_id=self.member(lax.rem(self.me + n, 16)), device_id_type=MESH)

    def met(self):
        pl.semaphore_wait(pltpu.get_barrier_semaphore(), self.signals)


def idle():
    while True:
        yield


def out_to_heads(group, packed, landed, send_sems, recv_sems):
    @pl.loop(0, 12)
    def _(n):
        head = lax.rem(group.me + n, 12)
        target = group.holder(head)

        @pl.when(target != group.me)
        def _():
            pltpu.make_async_remote_copy(
                src_ref=packed.at[head], dst_ref=landed.at[group.me], send_sem=send_sems.at[head],
                recv_sem=recv_sems.at[group.me], device_id=group.member(target), device_id_type=MESH).start()

    @pl.when(group.active)
    def _():
        landed[group.me] = packed[group.head]


def await_member(group, packed, landed, send_sems, recv_sems, index):
    @pl.when(group.me != index)
    def _():
        pltpu.make_async_remote_copy(
            src_ref=packed.at[0], dst_ref=landed.at[index], send_sem=send_sems.at[0],
            recv_sem=recv_sems.at[index], device_id=group.member(index), device_id_type=MESH).wait_recv()


def sent_to_heads(group, packed, landed, send_sems, recv_sems):
    @pl.loop(0, 12)
    def _(head):
        @pl.when(group.holder(head) != group.me)
        def _():
            pltpu.make_async_remote_copy(
                src_ref=packed.at[head], dst_ref=landed.at[group.me], send_sem=send_sems.at[head],
                recv_sem=recv_sems.at[group.me], device_id=group.member(group.holder(head)),
                device_id_type=MESH).wait_send()


def back_to_member(group, packed, landed, send_sems, recv_sems, index):
    @pl.when(group.me != index)
    def _():
        pltpu.make_async_remote_copy(
            src_ref=packed.at[index], dst_ref=landed.at[group.head], send_sem=send_sems.at[index],
            recv_sem=recv_sems.at[group.head], device_id=group.member(index), device_id_type=MESH).start()

    @pl.when(group.me == index)
    def _():
        landed[group.head] = packed[index]


def finish_back(group, packed, landed, send_sems, recv_sems):
    @pl.when(group.active)
    def _():
        @pl.loop(0, 16)
        def _(index):
            @pl.when(group.me != index)
            def _():
                pltpu.make_async_remote_copy(
                    src_ref=packed.at[index], dst_ref=landed.at[group.head], send_sem=send_sems.at[index],
                    recv_sem=recv_sems.at[group.head], device_id=group.member(index),
                    device_id_type=MESH).wait_send()

    @pl.loop(0, 12)
    def _(head):
        holder = group.holder(head)

        @pl.when(holder != group.me)
        def _():
            pltpu.make_async_remote_copy(
                src_ref=packed.at[0], dst_ref=landed.at[head], send_sem=send_sems.at[0],
                recv_sem=recv_sems.at[head], device_id=group.member(holder), device_id_type=MESH).wait_recv()


def dot_right(left, right):
    return lax.dot_general(left, right, (((1,), (1,)), ((), ())), preferred_element_type=jnp.float32)


def dot(left, right):
    return jnp.dot(left, right, preferred_element_type=jnp.float32)


def masked_scores(scores, block):
    key = lax.broadcasted_iota(jnp.int32, scores.shape, 0)
    query = lax.broadcasted_iota(jnp.int32, scores.shape, 1) + block * 256
    return jnp.where(key <= query, scores, -1e30)


epsilon = 1e-05


def low(value):
    return value.astype(jnp.bfloat16)


def standard(values):
    centred = values - jnp.mean(values, axis=-1, keepdims=True)
    factor = lax.rsqrt(jnp.mean(centred * centred, axis=-1, keepdims=True) + epsilon)
    return centred * factor, factor


def norm_back(values, gain, grad):
    unit, factor = standard(values)
    scaled = grad * gain
    through = factor * (scaled - jnp.mean(scaled, axis=-1, keepdims=True)
                        - unit * jnp.mean(scaled * unit, axis=-1, keepdims=True))
    return through, jnp.sum(grad * unit, axis=0, keepdims=True), jnp.sum(grad, axis=0, keepdims=True)


def normal_share(values):
    return 0.5 * (1.0 + lax.erf(values * 0.7071067811865476))


class Weights:
    def __init__(self, source, held, sems, parts):
        self.held, self.copies = held, {}
        for part in parts:
            for half in range(2):
                for unit in (2 * part, 2 * part + 1):
                    columns = pl.ds(unit % 2 * 384, 384)
                    copy = pltpu.make_async_copy(
                        source.at[unit // 6, unit % 3, half * 2 + unit // 3 % 2], held.at[part, half, :, columns],
                        sems.at[unit * 2 + half])
                    copy.start()
                    self.copies[unit, half] = copy

    def ready(self, part, half):
        for unit in (2 * part, 2 * part + 1):
            copy = self.copies.pop((unit, half), None)
            if copy is not None:
                copy.wait()

    def __call__(self, part, half, columns=slice(0, 768)):
        self.ready(part, half)
        return self.held[part, half, :, columns]


def forward_kernel(layer, x_ref, rows_ref, w_ref, *refs):
    if layer == 0:
        block_ref, *refs = refs
        next_ref = refs.pop(9)
        refs, (ring_send, ring_recv, own_sems) = refs[:-3], refs[-3:]
    (out_ref, normed_ref, mixed_ref, heads_ref, total_ref, hidden_ref, normed_two_ref, pre_ref, active_ref,
     held, w_sems, packed, landed, back, home, value_turned, send_a, recv_a, send_b, recv_b) = refs
    group = Group()
    group.greet(layer == 0)
    weights = Weights(w_ref, held, w_sems, range(6))
    steps = idle()
    if layer == 0:
        spot = Spot()
        placed = place_own(spot, block_ref, next_ref, own_sems)
        for copy in placed:
            copy.start()
        steps = gather_steps(spot, Copies(ring_send, ring_recv), next_ref)
    entering = x_ref[...].astype(jnp.float32)
    rows = [rows_ref[n:n + 1, :] for n in range(12)]
    normed = low(standard(entering)[0] * rows[0] + rows[1])
    normed_ref[...] = normed

    def pack(kind, half, values):
        for pair in range(3):
            first, second = split_pair(low(values[:, pair * 128:pair * 128 + 128]))
            packed[half * 6 + 2 * pair, kind * 64:kind * 64 + 64] = first
            packed[half * 6 + 2 * pair + 1, kind * 64:kind * 64 + 64] = second
    if layer == 0:
        for copy in placed:
            copy.wait()
        group.met()
        next(steps)
    for half in range(2):
        both = dot(normed, weights(0, half))
        cut = slice(half * 384, half * 384 + 384)
        pack(0, half, (both[:, EARLY] + rows[6][:, cut]) * 0.125)
        pack(1, half, both[:, LATE])
        pack(2, half, dot(normed, weights(1, half, EARLY)) + rows[7][:, cut])
        next(steps)
    if layer != 0:
        group.met()
    out_to_heads(group, packed, landed, send_a, recv_a)

    for block in range(8):
        if block < 4:
            next(steps)

        @pl.when(group.active)
        def _():
            for index in (2 * block, 2 * block + 1):
                await_member(group, packed, landed, send_a, recv_a, index)
                for n in range(3):
                    tile = landed[index, n * 64:n * 64 + 64]
                    heads_ref[n, index * 128:index * 128 + 64] = tile[:, 0:64]
                    heads_ref[n, index * 128 + 64:index * 128 + 128] = tile[:, 64:128]
            own = slice(block * 256, block * 256 + 256)
            value_turned[:, own] = heads_ref[2, own].T
            count = block * 256 + 256
            scores = masked_scores(dot_right(heads_ref[1, 0:count], heads_ref[0, own]), block)
            largest = jnp.max(scores, axis=0, keepdims=True)
            shares = jnp.exp(scores - largest)
            total = jnp.sum(shares, axis=0, keepdims=True)
            total_ref[block:block + 1, :] = largest + jnp.log(total)
            mixed = dot(value_turned[:, 0:count], low(shares)) / total
            mixed = mixed.T
            for n, index in enumerate((2 * block, 2 * block + 1)):
                back[index] = low(pack_rows(mixed[n * 128:n * 128 + 128]))
                back_to_member(group, back, home, send_b, recv_b, index)

    sent_to_heads(group, packed, landed, send_a, recv_a)
    finish_back(group, back, home, send_b, recv_b)
    for pair in range(6):
        mixed_ref[0:64, pair * 128:pair * 128 + 128], mixed_ref[64:128, pair * 128:pair * 128 + 128] = join_pair(
            home[2 * pair], home[2 * pair + 1])
    hidden = entering + rows[2]
    for half in range(2):
        hidden += dot_right(mixed_ref[:, half * 384:half * 384 + 384], weights(1, half, LATE))
    hidden_ref[...] = hidden
    normed_two = low(standard(hidden)[0] * rows[3] + rows[4])
    normed_two_ref[...] = normed_two
    leaving = hidden + rows[5]
    for half in range(2):
        for n in range(2):
            cut = slice((half * 2 + n) * 768, (half * 2 + n) * 768 + 768)
            pre = dot(normed_two, weights(2 + n, half)) + rows[8 + half * 2 + n]
            pre_ref[:, cut] = pre
            active = low(pre * normal_share(pre))
            active_ref[:, cut] = active
            leaving += dot_right(active, weights(4 + n, half))
            next(steps)
    out_ref[...] = low(leaving)
    if layer == 0:
        for _ in steps:
            pass


def tiles(*shape):
    return pltpu.VMEM(shape, jnp.bfloat16)


def shapes(kind, *all_shapes):
    return tuple(jax.ShapeDtypeStruct(shape, kind) for shape in all_shapes)


def layer_forward(entering, rows, gathered, layer, block_own=None):
    vmem, any_place = pl.BlockSpec(memory_space=pltpu.VMEM), pl.BlockSpec(memory_space=pl.ANY)
    more = layer == 0
    block = (128, 768)
    return pl.pallas_call(
        functools.partial(forward_kernel, layer),
        out_shape=shapes(jnp.bfloat16, block, block, block, (3, 2048, 64)) + shapes(jnp.float32, (8, 256), block)
        + shapes(jnp.bfloat16, block) + shapes(jnp.float32, (128, 3072)) + shapes(jnp.bfloat16, (128, 3072))
        + shapes(jnp.bfloat16, GATHERED) * more,
        in_specs=[vmem, vmem, any_place] + [vmem] * more,
        out_specs=(vmem,) * 9 + (any_place,) * more,
        scratch_shapes=[
            tiles(6, 2, 768, 768), pltpu.SemaphoreType.DMA((24,)),
            tiles(12, 192, 128), tiles(16, 192, 128), tiles(16, 64, 128), tiles(12, 64, 128), tiles(64, 2048),
            pltpu.SemaphoreType.DMA((12,)), pltpu.SemaphoreType.DMA((16,)),
            pltpu.SemaphoreType.DMA((16,)), pltpu.SemaphoreType.DMA((12,)),
        ] + gather_scratch() * more,
        compiler_params=pltpu.CompilerParams(
            collective_id=3 + layer, has_side_effects=True, vmem_limit_bytes=56 * 2**20),
        name="layer_forward",
    )(entering, rows, gathered, *([block_own] * more))


def backward_kernel(layer, arriving_ref, x_ref, rows_ref, normed_ref, mixed_ref, heads_ref, total_ref, hidden_ref,
                    normed_two_ref, pre_ref, active_ref, w_ref, *refs):
    if layer == 0:
        later_left, later_right, *refs = refs
        partial_ref = refs.pop(4)
        refs, (ring_send, ring_recv, *reduce_refs) = refs[:-REDUCED - 2], refs[-REDUCED - 2:]
    (out_ref, sums_ref, left_ref, right_ref,
     held, w_sems, packed, landed, back, home, grad_heads, key_turned, key_sum, value_sum,
     grad_pre, left_out, right_out, send_a, recv_a, send_b, recv_b, pair_sems) = refs
    group = Group()
    group.greet(layer == 0)
    weights = Weights(w_ref, held, w_sems, (4, 5, 2, 3, 1, 0))
    steps = idle()
    if layer == 0:
        steps = reduce_steps(Spot(), Copies(ring_send, ring_recv), later_left, later_right, partial_ref, lambda phase: None,
                             *reduce_refs)
    rows = [rows_ref[n:n + 1, :] for n in range(12)]

    def role(core, own, other, value):
        @pl.when(group.c == core)
        def _():
            own[...] = value

        @pl.when(group.c != core)
        def _():
            other[...] = value

    def left_role(core, n, value):
        role(core, left_ref.at[n, 0:128], left_out.at[n], value)

    def right_role(core, n, half, value):
        role(core, right_ref.at[n, half, 0:128], right_out.at[n, half], value)

    def to_sibling(n, source, target):
        return pltpu.make_async_remote_copy(
            src_ref=source, dst_ref=target, send_sem=pair_sems.at[n], recv_sem=pair_sems.at[n + 2],
            device_id=(group.s, group.y, group.z, 1 - group.c, group.t), device_id_type=MESH)

    arriving = arriving_ref[...]
    carried = arriving.astype(jnp.float32)
    sums_ref[5:6, :] = jnp.sum(carried, axis=0, keepdims=True)
    if layer == 0:
        group.met()
    for _ in range(4):
        next(steps)
    grad_normed_two = jnp.zeros((128, 768), jnp.float32)
    for half in range(2):
        for n in range(2):
            place = half * 2 + n
            cut = slice(place * 768, place * 768 + 768)
            pre = pre_ref[:, cut]
            slope = normal_share(pre) + pre * (jnp.exp(pre * pre * -0.5) * 0.3989422804014327)
            grad = low(dot(arriving, weights(4 + n, half)) * slope)
            grad_pre[:, cut] = grad
            sums_ref[8 + place:9 + place, :] = jnp.sum(grad.astype(jnp.float32), axis=0, keepdims=True)
            grad_normed_two += dot_right(grad, weights(2 + n, half))
            if place > 0:
                next(steps)
    hidden = hidden_ref[...]
    through, gain, shift = norm_back(hidden, rows[3], grad_normed_two)
    sums_ref[3:4, :], sums_ref[4:5, :] = gain, shift
    grad_hidden = carried + through
    hidden_low = low(grad_hidden)
    sums_ref[2:3, :] = jnp.sum(hidden_low.astype(jnp.float32), axis=0, keepdims=True)
    for half in range(2):
        grad_mixed = low(dot(hidden_low, weights(1, half, LATE)))
        for pair in range(3):
            packed[half * 6 + 2 * pair], packed[half * 6 + 2 * pair + 1] = split_pair(
                grad_mixed[:, pair * 128:pair * 128 + 128])
    if layer != 0:
        group.met()
    out_to_heads(group, packed, landed, send_a, recv_a)

    normed, normed_two = normed_ref[...], normed_two_ref[...]
    for n, value in enumerate((normed, normed, hidden_low, normed_two)):
        left_role(0, n, value)
    for n, value in enumerate((normed_two, arriving, arriving, arriving)):
        left_role(1, n, value)
    left_copy = to_sibling(0, left_out, left_ref.at[:, 128:256])
    left_copy.start()
    for half in range(2):
        def columns(n):
            return slice(half * 1536 + n * 384, half * 1536 + n * 384 + 384)
        right_role(0, 3, half, mixed_ref[:, half * 384:half * 384 + 384])
        for n in range(2):
            right_role(0, 4 + n, half, grad_pre[:, columns(n)])
            right_role(1, n, half, grad_pre[:, columns(2 + n)])
        for n in range(4):
            right_role(1, 2 + n, half, active_ref[:, columns(n)])
    for _ in range(4):
        next(steps)

    @pl.when(group.active)
    def _():
        key_turned[...] = heads_ref[1].T

    for block in reversed(range(8)):
        if block < 7:
            next(steps)

        @pl.when(group.active)
        def _():
            for index in (2 * block, 2 * block + 1):
                await_member(group, packed, landed, send_a, recv_a, index)
                tile = landed[index]
                grad_heads[index * 128:index * 128 + 64] = tile[:, 0:64]
                grad_heads[index * 128 + 64:index * 128 + 128] = tile[:, 64:128]
            own = slice(block * 256, block * 256 + 256)
            count = block * 256 + 256
            query, grad = heads_ref[0, own], grad_heads[own]
            scores = masked_scores(dot_right(heads_ref[1, 0:count], query), block)
            shares = jnp.exp(scores - total_ref[block:block + 1, :])
            soft = dot_right(heads_ref[2, 0:count], grad)
            dots = jnp.sum(shares * soft, axis=0, keepdims=True)
            moved = low(shares * (soft - dots))
            for_key, for_value = dot(moved, query), dot(low(shares), grad)
            if block == 7:
                key_sum[...] = for_key
                value_sum[...] = for_value
            else:
                key_sum[0:count] = key_sum[0:count] + for_key
                value_sum[0:count] = value_sum[0:count] + for_value
            for_query = low(dot(key_turned[:, 0:count], moved).T).astype(jnp.float32) * 0.125
            for n, index in enumerate((2 * block, 2 * block + 1)):
                part = slice(index * 128, index * 128 + 128)
                back[index, 0:64] = low(pack_rows(for_query[n * 128:n * 128 + 128]))
                back[index, 64:128] = low(pack_rows(key_sum[part]))
                back[index, 128:192] = low(pack_rows(value_sum[part]))
                back_to_member(group, back, home, send_b, recv_b, index)

    sent_to_heads(group, packed, landed, send_a, recv_a)
    finish_back(group, back, home, send_b, recv_b)
    grad_normed = jnp.zeros((128, 768), jnp.float32)
    for half in range(2):
        def joined(kind):
            whole = []
            for pair in range(3):
                head = half * 6 + 2 * pair
                top, bottom = join_pair(home[head, kind * 64:kind * 64 + 64], home[head + 1, kind * 64:kind * 64 + 64])
                whole.append(jnp.concatenate([top, bottom], axis=0))
            return jnp.concatenate(whole, axis=1)
        grad_q, grad_k, grad_v = joined(0), joined(1), joined(2)
        cut = slice(half * 384, half * 384 + 384)
        sums_ref[6:7, cut] = jnp.sum(grad_q.astype(jnp.float32), axis=0, keepdims=True)
        sums_ref[7:8, cut] = jnp.sum(grad_v.astype(jnp.float32), axis=0, keepdims=True)
        for n, value in enumerate((grad_q, grad_k, grad_v)):
            right_role(0, n, half, value)
        grad_normed += dot_right(grad_q, weights(0, half, EARLY)) + dot_right(grad_k, weights(0, half, LATE))
        grad_normed += dot_right(grad_v, weights(1, half, EARLY))
    right_copy = to_sibling(1, right_out, right_ref.at[:, :, 128:256])
    right_copy.start()
    through, gain, shift = norm_back(x_ref[...].astype(jnp.float32), rows[0], grad_normed)
    sums_ref[0:1, :], sums_ref[1:2, :] = gain, shift
    out_ref[...] = low(grad_hidden + through)
    if layer == 0:
        for _ in steps:
            pass
    left_copy.wait()
    right_copy.wait()


def layer_backward(arriving, entering, rows, kept, gathered, layer, later=()):
    vmem = pl.BlockSpec(memory_space=pltpu.VMEM)
    more = layer == 0
    block = (128, 768)
    return pl.pallas_call(
        functools.partial(backward_kernel, layer),
        out_shape=shapes(jnp.bfloat16, block) + shapes(jnp.float32, (12, 768))
        + shapes(jnp.bfloat16, (4, 256, 768), (6, 2, 256, 384)) + shapes(jnp.float32, (3, 48, 384)) * more,
        in_specs=[vmem] * 11 + [pl.BlockSpec(memory_space=pl.ANY)] + [vmem] * 2 * more,
        out_specs=(vmem,) * (4 + more),
        scratch_shapes=[
            tiles(6, 2, 768, 768), pltpu.SemaphoreType.DMA((24,)),
            tiles(12, 64, 128), tiles(16, 64, 128), tiles(16, 192, 128), tiles(12, 192, 128), tiles(2048, 64), tiles(64, 2048),
            pltpu.VMEM((2048, 64), jnp.float32), pltpu.VMEM((2048, 64), jnp.float32),
            tiles(128, 3072), tiles(4, 128, 768), tiles(6, 2, 128, 384),
            pltpu.SemaphoreType.DMA((12,)), pltpu.SemaphoreType.DMA((16,)),
            pltpu.SemaphoreType.DMA((16,)), pltpu.SemaphoreType.DMA((12,)), pltpu.SemaphoreType.DMA((4,)),
        ] + ([pltpu.SemaphoreType.DMA((60,)), pltpu.SemaphoreType.DMA((60,))] + reduce_scratch()) * more,
        compiler_params=pltpu.CompilerParams(
            collective_id=5 + layer, has_side_effects=True, vmem_limit_bytes=60 * 2**20),
        name="layer_backward",
    )(arriving, entering, rows, *kept, gathered, *later)


def on_device(tokens_in, cotangent, place, w_qkv, w_out, w_up, w_down, qv_bias, up_bias, vectors):
    section = lax.axis_index("s")
    half = lax.axis_index("t")
    shard = jnp.concatenate([
        w_qkv[0], w_out[0].T[None], w_up[0].reshape(24, 4, 384).transpose(1, 0, 2),
        w_down[0].reshape(4, 384, 24).transpose(0, 2, 1)]).astype(jnp.float32)
    small = jnp.concatenate([vectors[0], qv_bias.reshape(1, 768), up_bias.reshape(2, 768), jnp.zeros((7, 768), jnp.bfloat16)])
    micro = lax.rem(section + half, 2)
    device = jnp.arange(32, dtype=jnp.int32)
    y, z = device // 8, device // 2 % 4
    seat = ((y // 2) * 2 + z // 2) * 8 + (y % 2) * 4 + (z % 2) * 2 + device % 2
    order = jnp.sum(jnp.where(place[None, :] == seat[:, None], device[None, :], 0), axis=1)
    mine = jnp.stack([jnp.where(micro == 0, a[0], a[1]) for a in (tokens_in, cotangent)])
    mine = mine.reshape(2, 32, 4, 768).transpose(1, 0, 2, 3).reshape(32, 48, 128)
    gathered, block_own, mine, rows = start(order, mine, small, shard)
    mine = mine.reshape(32, 2, 4, 768).transpose(1, 0, 2, 3).reshape(2, 128, 768)
    gathered = [gathered.reshape(2, 3, 4, 768, 384)]

    acts, kept, entering = [], [], [mine[0]]
    for layer in range(2):
        leaving, *state = layer_forward(entering[layer], rows[layer], gathered[layer], layer, block_own)
        if layer == 0:
            gathered.append(state.pop().reshape(2, 3, 4, 768, 384))
        entering.append(leaving)
        acts.append(leaving)
        kept.append(state)
    arriving = mine[1]
    grads_one, sums_one, *operands = layer_backward(arriving, entering[1], rows[1], kept[1], gathered[1], 1)
    grads_zero, sums_zero, left, right, partial = layer_backward(
        grads_one, entering[0], rows[0], kept[0], gathered[0], 0, operands)
    rows_out = jnp.stack([acts[0], grads_zero, acts[1], grads_one]).reshape(2, 2, 32, 4, 768)
    rows_out = rows_out.transpose(0, 2, 1, 3, 4).reshape(2, 32, 48, 128)
    seq, part = place // 8, place % 8
    holder = (seq // 2 * 2 + part // 4) * 8 + (seq % 2 * 2 + part // 2 % 2) * 2 + part % 2
    full, rows_out, total = end(holder, rows_out, (sums_zero, sums_one), left, right, partial)
    rows_out = rows_out.reshape(2, 32, 2, 4, 768)
    acts_out = rows_out[:, :, 0].reshape(1, 2, 128, 768)
    grads_out = rows_out[:, :, 1].reshape(1, 2, 128, 768).astype(jnp.float32)
    grad_qkv = full[None, 0:3]
    grad_out = full[3].T[None]
    grad_up = full[4:8].transpose(1, 0, 2).reshape(1, 24, 1536)
    grad_down = full[8:12].transpose(0, 2, 1).reshape(1, 1536, 24)

    total = total.reshape(2, 9216)
    total = jnp.where(section == 0, total[0], total[1])
    grad_vectors = total[:4608].reshape(1, 6, 768)
    grad_qv = lax.dynamic_slice_in_dim(total[4608:6144].reshape(2, 768), half * 384, 384, 1)[None]
    grad_up_bias = lax.dynamic_slice_in_dim(total[6144:], half * 1536, 1536)[None]
    return acts_out, grads_out, grad_qkv, grad_out, grad_up, grad_down, grad_qv, grad_up_bias, grad_vectors


def solution(mesh):
    fine = Mesh(mesh.devices.reshape(2, 4, 4, 2, 2), ("s", "y", "z", "c", "t"))
    dp = ("y", "z", "c")
    blocks = P(None, dp + ("t",), None)
    weights = (P("s", None, dp, "t"), P("s", "t", dp), P("s", dp, "t"), P("s", "t", dp))
    small = (P("s", None, "t"), P("s", "t"), P("s", None, None))
    rows = P("s", None, dp + ("t",), None)
    return jax.shard_map(
        on_device, mesh=fine,
        in_specs=(blocks, blocks, P()) + weights + small,
        out_specs=(rows, rows) + weights + small,
        check_vma=False)
```

```python
import functools

import jax
import jax.numpy as jnp
from jax import lax
from jax.experimental import pallas as pl
from jax.experimental.pallas import tpu as pltpu
from jax.sharding import Mesh, PartitionSpec as P
MESH = pl.DeviceIdType.MESH
ORDERS = ("xyz", "yzx", "zxy")
EARLY, LATE = slice(0, 384), slice(384, 768)


class Spot:
    def __init__(self):
        self.s, self.y, self.z, self.c, self.t = (lax.axis_index(a) for a in "syzct")
        self.x = self.t * 2 + self.s

    def at(self, axis):
        return {"x": self.x, "y": self.y, "z": self.z}[axis]

    def shifted(self, axis, by):
        return lax.rem(self.at(axis) + (by + 4), 4)

    def device(self, axis, by):
        x, y, z = self.x, self.y, self.z
        moved = self.shifted(axis, by)
        if axis == "x":
            x = moved
        elif axis == "y":
            y = moved
        else:
            z = moved
        return (lax.rem(x, 2), y, z, self.c, lax.div(x, 2))

    def fourth(self, section_by, core_by):
        return (lax.rem(self.s + section_by, 2), self.y, self.z, lax.rem(self.c + core_by, 2), self.t)

    def sibling(self):
        return (self.s, self.y, self.z, 1 - self.c, self.t)


class Copies:
    def __init__(self, send_sems, recv_sems):
        self.send_sems, self.recv_sems, self.count = send_sems, recv_sems, 0
        self.sent = []

    def make(self, src, dst, device):
        n = self.count
        self.count += 1
        copy = pltpu.make_async_remote_copy(
            src_ref=src, dst_ref=dst, send_sem=self.send_sems.at[n], recv_sem=self.recv_sems.at[n],
            device_id=device, device_id_type=MESH)
        self.sent.append(copy)
        return copy

    def start(self, src, dst, device):
        copy = self.make(src, dst, device)
        copy.start()
        return copy

    def finish(self):
        for copy in self.sent:
            copy.wait_send()


class Move:
    def __init__(self, spot, order_ref, x_ref, out_ref, middle, turned, send_a, recv_a, send_b, recv_b):
        self.spot, self.order, self.turned, self.middle = spot, order_ref, turned, middle
        self.me = spot.y * 8 + spot.z * 2 + spot.c
        self.first = (x_ref, middle, send_a, recv_a)
        self.second = (turned, out_ref, send_b, recv_b)
        self.leads = range(x_ref.shape[0]) if len(x_ref.shape) == 4 else None

    def member(self, index):
        return (self.spot.s, lax.div(index, 8), lax.rem(lax.div(index, 2), 4), lax.rem(index, 2), self.spot.t)

    def piece(self, ref, index):
        return ref.at[index] if self.leads is None else ref.at[:, index]

    def local(self, target, to, source, index):
        if self.leads is None:
            target[to] = source[index]
        else:
            for lead in self.leads:
                target[lead, to] = source[lead, index]

    def copy(self, which, n):
        source, target, send_sems, recv_sems = which
        to = lax.rem(self.me + n, 32)
        return pltpu.make_async_remote_copy(
            src_ref=self.piece(source, to), dst_ref=self.piece(target, self.me), send_sem=send_sems.at[n],
            recv_sem=recv_sems.at[n], device_id=self.member(to), device_id_type=MESH)

    def start(self, which):
        @pl.loop(1, 32)
        def _(n):
            self.copy(which, n).start()
        source, target = which[:2]
        self.local(target, self.me, source, self.me)

    def arrive(self, which):
        source, target, send_sems, recv_sems = which

        @pl.loop(1, 32)
        def _(n):
            came = lax.rem(self.me + 32 - n, 32)
            pltpu.make_async_remote_copy(
                src_ref=self.piece(source, came), dst_ref=self.piece(target, came), send_sem=send_sems.at[n],
                recv_sem=recv_sems.at[n], device_id=self.member(came), device_id_type=MESH).wait_recv()

    def begin(self):
        self.start(self.first)

    def turn(self):
        self.arrive(self.first)

        @pl.loop(0, 32)
        def _(n):
            self.local(self.turned, n, self.middle, self.order[n])
        self.start(self.second)

    def end(self):
        self.arrive(self.second)

        @pl.loop(1, 32)
        def _(n):
            self.copy(self.first, n).wait_send()
            self.copy(self.second, n).wait_send()


def greet(spot, move):
    barrier = pltpu.get_barrier_semaphore()
    for peer in [spot.device("x", by) for by in (1, -1, 2)] + [spot.fourth(1, 1)]:
        pl.semaphore_signal(barrier, inc=1, device_id=peer, device_id_type=MESH)

    @pl.loop(1, 32)
    def _(n):
        pl.semaphore_signal(barrier, inc=1, device_id=move.member(lax.rem(move.me + n, 32)), device_id_type=MESH)


def met():
    pl.semaphore_wait(pltpu.get_barrier_semaphore(), 35)


def tile_places():
    for which in range(2):
        for row in range(8):
            for column in range(6):
                tile = which * 48 + row * 6 + column
                rows, columns = slice(row * 16, row * 16 + 16), slice(column * 128, column * 128 + 128)
                yield which, rows, columns, tile // 3, slice(tile % 3 * 16, tile % 3 * 16 + 16)


def pack_tiles(first, second, target):
    for which, rows, columns, piece, part in tile_places():
        target[piece, part] = (first, second)[which][rows, columns]


def unpack_tiles(source, first, second):
    for which, rows, columns, piece, part in tile_places():
        target = (first, second)[which]
        target[rows, columns] = source[piece, part].astype(target.dtype)


def move_scratch(shape):
    return [pltpu.VMEM(shape, jnp.bfloat16)] * 2 + [pltpu.SemaphoreType.DMA((32,))] * 4


FOURTHS = ((0, 1), (1, 0), (1, 1))


def gather_steps(spot, copies, out_ref):
    half = out_ref.at[spot.c]

    def part(k, order, phase, position, piece=None):
        axis = order[phase]
        index = {}
        for n, name in enumerate(order):
            index[name] = slice(None) if n < phase else spot.at(name)
        index[axis] = position
        if piece is not None:
            index[order[0]] = pl.ds(*piece)
        return half.at[k, index["x"], index["y"], index["z"]]

    def ring(k, order, phase, position, piece, by):
        ref = part(k, order, phase, position, piece)
        return copies.start(ref, ref, spot.device(order[phase], by))

    def push(k, order, phase, position, piece):
        ref = part(k, order, phase, position, piece)
        return copies.start(ref, ref, spot.sibling())

    pushes = []
    for phase in range(3):
        if phase == 1:
            to_right, to_left = [(0, 2), (2, 2)], [(2, 2), (0, 2)]
            pass_right, pass_left = [(0, 2)], [(2, 2)]
        elif phase == 2:
            to_right, to_left = [(0, 1), (1, 1), (2, 1), (3, 1)], [(2, 1), (3, 1), (0, 1), (1, 1)]
            pass_right, pass_left = [(0, 1), (1, 1)], [(2, 1), (3, 1)]
        if phase == 0:
            straight = []
            for k, order in enumerate(ORDERS):
                for by in (2, 1, -1):
                    straight.append(ring(k, order, 0, spot.at(order[0]), None, by))
            yield
            for copy in straight:
                copy.wait_recv()
            continue
        first = {}
        for n in range(len(to_right)):
            for k, order in enumerate(ORDERS):
                me = spot.at(order[phase])
                first[k, "r", to_right[n]] = ring(k, order, phase, me, to_right[n], 1)
                first[k, "l", to_left[n]] = ring(k, order, phase, me, to_left[n], -1)
        if phase == 2:
            for k, order in enumerate(ORDERS):
                pushes.append(push(k, order, phase, spot.at(order[phase]), None))
        yield
        second = []
        for n in range(len(to_right)):
            for k, order in enumerate(ORDERS):
                axis = order[phase]
                before, after = spot.shifted(axis, -1), spot.shifted(axis, 1)
                first[k, "r", to_right[n]].wait_recv()
                if to_right[n] in pass_right:
                    second.append((k, to_right[n], ring(k, order, phase, before, to_right[n], 1)))
                first[k, "l", to_left[n]].wait_recv()
                if to_left[n] in pass_left:
                    second.append((k, to_left[n], ring(k, order, phase, after, to_left[n], -1)))
                if phase == 2:
                    pushes.append(push(k, order, phase, before, to_right[n]))
                    pushes.append(push(k, order, phase, after, to_left[n]))
            yield
        for k, piece, copy in second:
            copy.wait_recv()
            if phase == 2:
                order = ORDERS[k]
                pushes.append(push(k, order, phase, spot.shifted(order[phase], 2), piece))
    for copy in pushes:
        copy.wait_recv()
    copies.finish()


def place_own(spot, block_ref, out_ref, sems):
    return [pltpu.make_async_copy(block_ref.at[k], out_ref.at[spot.c, k, spot.x, spot.y, spot.z], sems.at[k]) for k in range(3)]


GATHERED = (2, 3, 4, 4, 4, 48, 768)


def gather_scratch():
    return [pltpu.SemaphoreType.DMA((112,)), pltpu.SemaphoreType.DMA((112,)), pltpu.SemaphoreType.DMA((3,))]


def start_kernel(order_ref, tokens_ref, cotangent_ref, small_ref, shard_ref, w_ref, rows_ref, tokens_out, cotangent_out,
                 x_ref, moved_ref, fourths, own, smalls, pair_sems, send_sems, recv_sems, own_sems, *move_refs):
    spot = Spot()
    move = Move(spot, order_ref, x_ref, moved_ref, *move_refs)
    copies = Copies(send_sems, recv_sems)
    greet(spot, move)
    micro = lax.rem(spot.s + spot.t, 2)
    pack_tiles(tokens_ref.at[micro], cotangent_ref.at[micro], x_ref)
    met()
    near = []
    for n, (section_by, core_by) in enumerate(FOURTHS):
        section, core = lax.rem(spot.s + section_by, 2), lax.rem(spot.c + core_by, 2)
        near.append(pltpu.make_async_remote_copy(
            src_ref=shard_ref.at[pl.ds((core * 2 + section) * 3, 3)], dst_ref=fourths.at[spot.s * 2 + spot.c],
            send_sem=pair_sems.at[n], recv_sem=pair_sems.at[n + 6],
            device_id=spot.fourth(section_by, core_by), device_id_type=MESH))
    for n, by in enumerate((1, -1, 2)):
        near.append(pltpu.make_async_remote_copy(
            src_ref=small_ref, dst_ref=smalls.at[spot.x], send_sem=pair_sems.at[n + 3], recv_sem=pair_sems.at[n + 9],
            device_id=spot.device("x", by), device_id_type=MESH))
    for copy in near:
        copy.start()
    move.begin()
    fourths[spot.s * 2 + spot.c] = shard_ref[pl.ds((spot.c * 2 + spot.s) * 3, 3)]
    smalls[spot.x] = small_ref[...]
    for copy in near[:3]:
        copy.wait_recv()

    def both_cores(layer, k):
        return jnp.concatenate([fourths[layer * 2, k], fourths[layer * 2 + 1, k]], axis=0).astype(jnp.bfloat16)
    for k in range(3):
        own[k, :, EARLY] = both_cores(0, k)
        own[k, :, LATE] = both_cores(1, k)
    placed = place_own(spot, own, w_ref, own_sems)
    for copy in placed:
        copy.start()
    for copy in placed:
        copy.wait()
    steps = gather_steps(spot, copies, w_ref)
    next(steps)
    for copy in near[3:]:
        copy.wait_recv()
    for layer in range(2):
        first, second = smalls[layer].astype(jnp.float32), smalls[layer + 2].astype(jnp.float32)
        rows_ref[layer, 0:6] = first[0:6]
        rows_ref[layer, 6:7] = jnp.concatenate([first[6:7, EARLY], second[6:7, EARLY]], axis=1)
        rows_ref[layer, 7:8] = jnp.concatenate([first[6:7, LATE], second[6:7, LATE]], axis=1)
        rows_ref[layer, 8:10] = first[7:9]
        rows_ref[layer, 10:12] = second[7:9]
    for _ in range(2):
        next(steps)
    move.turn()
    for _ in steps:
        pass
    move.end()
    unpack_tiles(moved_ref, tokens_out, cotangent_out)
    for copy in near:
        copy.wait_send()


def start(order, tokens, cotangent, small, shard):
    vmem, any_place = pl.BlockSpec(memory_space=pltpu.VMEM), pl.BlockSpec(memory_space=pl.ANY)
    return pl.pallas_call(
        start_kernel,
        out_shape=shapes(jnp.bfloat16, GATHERED) + shapes(jnp.float32, (2, 12, 768)) + shapes(jnp.bfloat16, (128, 768), (128, 768)),
        in_specs=[pl.BlockSpec(memory_space=pltpu.SMEM)] + [vmem] * 4,
        out_specs=(any_place, vmem, vmem, vmem),
        scratch_shapes=[
            tiles(32, 48, 128), tiles(32, 48, 128),
            pltpu.VMEM((4, 3, 24, 384), jnp.float32), tiles(3, 48, 768), tiles(4, 16, 768), pltpu.SemaphoreType.DMA((12,)),
        ] + gather_scratch() + move_scratch((32, 48, 128)),
        compiler_params=pltpu.CompilerParams(collective_id=1, has_side_effects=True, vmem_limit_bytes=32 * 2**20),
        name="start",
    )(order, tokens, cotangent, small, shard)


SLOTS = (0, 0, 1, 2, 3, 3)


def reduce_steps(spot, copies, operands, out_ref, beside_steps,
                 g_ref, a0, b0, l0, r0, q0, a1, b1, l1, r1, q1, a2, b2, l2, r2):
    def make_part(k):
        for columns, (left_ref, right_ref) in zip((EARLY, LATE), operands):
            for section in range(2):
                @pl.loop(0, 2)
                def _(half):
                    unit = section * 3 + k
                    product = dot(left_ref[SLOTS[unit]], right_ref[unit, half])
                    g_ref[k, half * 2 + section, :, :, :, columns] = low(product).reshape(4, 4, 48, 384)
    first_in, second_in = [(a0, b0), (a1, b1), (a2, b2)], [(l0, r0), (l1, r1), (l2, r2)]
    quarters = [q0, q1]

    def source(k, phase, order, position, piece=None):
        axis = order[phase]
        rest = order[phase + 1:]
        if phase == 0:
            index = {axis: position}
            for n, name in enumerate(rest):
                index[name] = slice(None)
            if piece is not None:
                index[max(rest)] = pl.ds(2 * piece, 2)
            return g_ref.at[k, index["x"], index["y"], index["z"]]
        held = quarters[phase - 1].at[k]
        names = [n for n in "xyz" if n in order[phase:]]
        index = []
        for name in names:
            if name == axis:
                index.append(position)
            elif piece is not None and name == rest[0]:
                index.append(pl.ds(2 * piece, 2))
            else:
                index.append(slice(None))
        rows = slice(None)
        if phase == 2 and piece is not None:
            rows = pl.ds(0, 32) if piece == 0 else pl.ds(32, 16)
        return held.at[tuple(index) + (rows,)]

    def slot(buffer, k, phase, order, piece):
        held = buffer.at[k]
        if piece is None:
            return held
        if phase == 2:
            return held.at[pl.ds(0, 32) if piece == 0 else pl.ds(32, 16)]
        rest = order[phase + 1:]
        names = [n for n in "xyz" if n in rest]
        return held.at[tuple(pl.ds(2 * piece, 2) if n == max(rest) else slice(None) for n in names)]

    def each(shape, body):
        lead = shape[:-2]
        if not lead:
            body(())
        elif len(lead) == 1:
            @pl.loop(0, lead[0])
            def _(i):
                body((i,))
        else:
            @pl.loop(0, lead[0])
            def _(i):
                @pl.loop(0, lead[1])
                def _(j):
                    body((i, j))

    for phase in range(3):
        started = []
        for k, gathered in enumerate(ORDERS):
            if phase == 0:
                make_part(k)
            order = gathered[::-1]
            axis = order[phase]
            right, left = spot.device(axis, 1), spot.device(axis, -1)
            a, b = first_in[phase]
            l, r = second_in[phase]
            far = spot.shifted(axis, 2)
            ca = copies.start(source(k, phase, order, far, 0), a.at[k], right)
            cb = copies.start(source(k, phase, order, far, 1), b.at[k], left)
            started.append([ca, cb])
            if phase == 0:
                yield
        for k, gathered in enumerate(ORDERS):
            order = gathered[::-1]
            axis = order[phase]
            right, left = spot.device(axis, 1), spot.device(axis, -1)
            l, r = second_in[phase]
            after, before = spot.shifted(axis, 1), spot.shifted(axis, -1)
            started[k].append(copies.start(source(k, phase, order, after, 1), slot(l, k, phase, order, 1), right))
            started[k].append(copies.start(source(k, phase, order, before, 0), slot(r, k, phase, order, 0), left))
        yield
        for k, gathered in enumerate(ORDERS):
            order = gathered[::-1]
            axis = order[phase]
            right, left = spot.device(axis, 1), spot.device(axis, -1)
            a, b = first_in[phase]
            l, r = second_in[phase]
            after, before = spot.shifted(axis, 1), spot.shifted(axis, -1)

            def join(buffer, own):
                def body(i):
                    buffer[i] = (buffer[i].astype(jnp.float32) + own[i].astype(jnp.float32)).astype(jnp.bfloat16)
                each(buffer.shape, body)

            started[k][0].wait_recv()
            join(a.at[k], source(k, phase, order, after, 0))
            started[k].append(copies.start(a.at[k], slot(l, k, phase, order, 0), right))
            started[k][1].wait_recv()
            join(b.at[k], source(k, phase, order, before, 1))
            started[k].append(copies.start(b.at[k], slot(r, k, phase, order, 1), left))
            yield
        beside_steps(phase)
        for k, gathered in enumerate(ORDERS):
            order = gathered[::-1]
            axis = order[phase]
            l, r = second_in[phase]
            for copy in started[k][2:]:
                copy.wait_recv()
            own = source(k, phase, order, spot.at(axis))
            left_in, right_in = l.at[k], r.at[k]
            target = out_ref.at[k] if phase == 2 else quarters[phase].at[k]

            def body(i):
                target[i] = (own[i].astype(jnp.float32) + left_in[i].astype(jnp.float32)
                             + right_in[i].astype(jnp.float32)).astype(target.dtype)
            each(target.shape, body)
            yield
    copies.finish()


def reduce_scratch():
    return [
        tiles(3, 4, 4, 4, 48, 768),
        tiles(3, 4, 2, 48, 768), tiles(3, 4, 2, 48, 768), tiles(3, 4, 4, 48, 768), tiles(3, 4, 4, 48, 768), tiles(3, 4, 4, 48, 768),
        tiles(3, 2, 48, 768), tiles(3, 2, 48, 768), tiles(3, 4, 48, 768), tiles(3, 4, 48, 768), tiles(3, 4, 48, 768),
        tiles(3, 32, 768), tiles(3, 16, 768), tiles(3, 48, 768), tiles(3, 48, 768),
    ]


REDUCED = 15


def end_kernel(order_ref, acts_0, acts_1, grads_0, grads_1, sums_0, sums_1, left_0, left_1, right_0, right_1,
               out_ref, acts_out, grads_out, total_ref, leaving, moved_ref, turned_left, sums_ref, beside, slots, summed, both, mine, pair_sems, send_sems, recv_sems, *refs):
    spot = Spot()
    copies = Copies(send_sems, recv_sems)
    move = Move(spot, order_ref, mine, moved_ref, *refs[REDUCED:])
    greet(spot, move)
    micro = lax.rem(spot.s + spot.t, 2)
    layers = ((acts_0, grads_0), (acts_1, grads_1))
    for section in range(2):
        @pl.when(spot.s == section)
        def _():
            pack_tiles(*layers[section], mine.at[micro])
            pack_tiles(*layers[1 - section], leaving)
    for layer, ref in enumerate((left_0, left_1)):
        for n in range(4):
            turned_left[layer, n] = ref[n].T
    met()
    exchange = pltpu.make_async_remote_copy(
        src_ref=leaving, dst_ref=mine.at[micro], send_sem=pair_sems.at[0], recv_sem=pair_sems.at[1],
        device_id=spot.fourth(1, 0), device_id_type=MESH)
    exchange.start()
    sums_ref[0:12] = sums_0[...]
    sums_ref[12:24] = sums_1[...]
    vector_copies = [copies.start(sums_ref, beside, spot.sibling())]

    def spread(axis, n):
        me = spot.at(axis)
        return [copies.start(slots.at[n, me], slots.at[n, me], spot.device(axis, by)) for by in (1, -1, 2)]

    def gathered_sum(n):
        for copy in vector_copies.pop():
            copy.wait_recv()
        return (slots[n, 0] + slots[n, 1]) + (slots[n, 2] + slots[n, 3])

    def beside_steps(phase):
        if phase == 0:
            vector_copies.pop().wait_recv()
            slots[0, spot.x] = sums_ref[...] + beside[...]
            vector_copies.append(spread("x", 0))
            move.turn()
        else:
            slots[phase, spot.at("xyz"[phase])] = gathered_sum(phase - 1)
            vector_copies.append(spread("xyz"[phase], phase))

    steps = reduce_steps(
        spot, copies, ((turned_left.at[0], right_0), (turned_left.at[1], right_1)), summed, beside_steps, *refs[:REDUCED])
    for _ in range(4):
        next(steps)
    exchange.wait_recv()
    move.begin()
    for _ in steps:
        pass
    total_ref[...] = gathered_sum(2)
    both[0] = summed[:, :, EARLY]
    both[1] = summed[:, :, LATE]
    near = []
    for n, (section_by, core_by) in enumerate(FOURTHS):
        section, core = lax.rem(spot.s + section_by, 2), lax.rem(spot.c + core_by, 2)
        near.append(pltpu.make_async_remote_copy(
            src_ref=both.at[section, :, pl.ds(pl.multiple_of(core * 24, 8), 24)],
            dst_ref=out_ref.at[pl.ds((spot.c * 2 + spot.s) * 3, 3)],
            send_sem=pair_sems.at[n + 2], recv_sem=pair_sems.at[n + 5],
            device_id=spot.fourth(section_by, core_by), device_id_type=MESH))
    for copy in near:
        copy.start()
    for core in range(2):
        @pl.when(spot.c == core)
        def _():
            out_ref[pl.ds((spot.c * 2 + spot.s) * 3, 3)] = both[spot.s, :, core * 24:core * 24 + 24]
    move.end()
    for n in range(2):
        unpack_tiles(moved_ref.at[n], acts_out.at[n], grads_out.at[n])
    exchange.wait_send()
    for copy in near:
        copy.wait()


def end(order, acts, grads, sums, lefts, rights):
    vmem = pl.BlockSpec(memory_space=pltpu.VMEM)
    return pl.pallas_call(
        end_kernel,
        out_shape=shapes(jnp.float32, (12, 24, 384)) + shapes(jnp.bfloat16, (2, 128, 768))
        + shapes(jnp.float32, (2, 128, 768), (24, 768)),
        in_specs=[pl.BlockSpec(memory_space=pltpu.SMEM)] + [vmem] * 10,
        out_specs=(vmem,) * 4,
        scratch_shapes=[
            tiles(32, 48, 128), tiles(2, 32, 48, 128), tiles(2, 4, 768, 256),
            pltpu.VMEM((24, 768), jnp.float32), pltpu.VMEM((24, 768), jnp.float32), pltpu.VMEM((3, 4, 24, 768), jnp.float32),
            pltpu.VMEM((3, 48, 768), jnp.float32), pltpu.VMEM((2, 3, 48, 384), jnp.float32), tiles(2, 32, 48, 128), pltpu.SemaphoreType.DMA((8,)),
            pltpu.SemaphoreType.DMA((80,)), pltpu.SemaphoreType.DMA((80,)),
        ] + reduce_scratch() + move_scratch((2, 32, 48, 128)),
        compiler_params=pltpu.CompilerParams(collective_id=2, has_side_effects=True, vmem_limit_bytes=60 * 2**20),
        name="end",
    )(order, *acts, *grads, *sums, *lefts, *rights)


def lanes_swapped(tile):
    return pltpu.roll(tile, 64, 1)


def split_pair(tile):
    tile = tile.astype(jnp.float32)
    top, low = tile[0:64], tile[64:128]
    left = lax.broadcasted_iota(jnp.int32, (64, 128), 1) < 64
    first = jnp.where(left, top, lanes_swapped(low))
    second = jnp.where(left, lanes_swapped(top), low)
    return first.astype(jnp.bfloat16), second.astype(jnp.bfloat16)


def join_pair(first, second):
    first, second = first.astype(jnp.float32), second.astype(jnp.float32)
    left = lax.broadcasted_iota(jnp.int32, (64, 128), 1) < 64
    top = jnp.where(left, first, lanes_swapped(second))
    low = jnp.where(left, lanes_swapped(first), second)
    return top.astype(jnp.bfloat16), low.astype(jnp.bfloat16)


def pack_rows(block):
    return jnp.concatenate([block[0:64], block[64:128]], axis=1)


class Group:
    def __init__(self):
        self.s, self.y, self.z, self.c, self.t = (lax.axis_index(a) for a in "syzct")
        self.micro = lax.rem(self.s + self.t, 2)
        y, z = lax.rem(self.y, 2), lax.rem(self.z, 2)
        self.me = y * 8 + z * 4 + self.c * 2 + self.t
        self.active = jnp.logical_or(self.c == 0, lax.rem(y + z + self.t, 2) == 0)
        self.head = jnp.where(self.c == 0, y * 4 + z * 2 + self.t, 8 + y * 2 + z)

    def member(self, index):
        t = lax.rem(index, 2)
        y = lax.div(self.y, 2) * 2 + lax.div(index, 8)
        z = lax.div(self.z, 2) * 2 + lax.rem(lax.div(index, 4), 2)
        return (lax.rem(self.micro + t, 2), y, z, lax.rem(lax.div(index, 2), 2), t)

    def holder(self, head):
        late = head - 8
        y, z = lax.div(late, 2), lax.rem(late, 2)
        return jnp.where(
            head < 8, lax.div(head, 4) * 8 + lax.rem(lax.div(head, 2), 2) * 4 + lax.rem(head, 2),
            y * 8 + z * 4 + 2 + lax.rem(y + z, 2))

    def greet(self):
        barrier = pltpu.get_barrier_semaphore()

        @pl.loop(1, 16)
        def _(n):
            pl.semaphore_signal(barrier, inc=1, device_id=self.member(lax.rem(self.me + n, 16)), device_id_type=MESH)

    def met(self):
        pl.semaphore_wait(pltpu.get_barrier_semaphore(), 15)


def out_to_heads(group, packed, landed, send_sems, recv_sems):
    @pl.loop(0, 12)
    def _(n):
        head = lax.rem(group.me + n, 12)
        target = group.holder(head)

        @pl.when(target != group.me)
        def _():
            pltpu.make_async_remote_copy(
                src_ref=packed.at[head], dst_ref=landed.at[group.me], send_sem=send_sems.at[head],
                recv_sem=recv_sems.at[group.me], device_id=group.member(target), device_id_type=MESH).start()

    @pl.when(group.active)
    def _():
        landed[group.me] = packed[group.head]


def await_member(group, packed, landed, send_sems, recv_sems, index):
    @pl.when(group.me != index)
    def _():
        pltpu.make_async_remote_copy(
            src_ref=packed.at[0], dst_ref=landed.at[index], send_sem=send_sems.at[0],
            recv_sem=recv_sems.at[index], device_id=group.member(index), device_id_type=MESH).wait_recv()


def sent_to_heads(group, packed, landed, send_sems, recv_sems):
    @pl.loop(0, 12)
    def _(head):
        @pl.when(group.holder(head) != group.me)
        def _():
            pltpu.make_async_remote_copy(
                src_ref=packed.at[head], dst_ref=landed.at[group.me], send_sem=send_sems.at[head],
                recv_sem=recv_sems.at[group.me], device_id=group.member(group.holder(head)),
                device_id_type=MESH).wait_send()


def back_to_member(group, packed, landed, send_sems, recv_sems, index):
    @pl.when(group.me != index)
    def _():
        pltpu.make_async_remote_copy(
            src_ref=packed.at[index], dst_ref=landed.at[group.head], send_sem=send_sems.at[index],
            recv_sem=recv_sems.at[group.head], device_id=group.member(index), device_id_type=MESH).start()

    @pl.when(group.me == index)
    def _():
        landed[group.head] = packed[index]


def finish_back(group, packed, landed, send_sems, recv_sems):
    @pl.when(group.active)
    def _():
        @pl.loop(0, 16)
        def _(index):
            @pl.when(group.me != index)
            def _():
                pltpu.make_async_remote_copy(
                    src_ref=packed.at[index], dst_ref=landed.at[group.head], send_sem=send_sems.at[index],
                    recv_sem=recv_sems.at[group.head], device_id=group.member(index),
                    device_id_type=MESH).wait_send()

    @pl.loop(0, 12)
    def _(head):
        holder = group.holder(head)

        @pl.when(holder != group.me)
        def _():
            pltpu.make_async_remote_copy(
                src_ref=packed.at[0], dst_ref=landed.at[head], send_sem=send_sems.at[0],
                recv_sem=recv_sems.at[head], device_id=group.member(holder), device_id_type=MESH).wait_recv()


def dot_right(left, right):
    return lax.dot_general(left, right, (((1,), (1,)), ((), ())), preferred_element_type=jnp.float32)


def dot(left, right):
    return jnp.dot(left, right, preferred_element_type=jnp.float32)


def key_spans(block):
    own = slice(block * 256, block * 256 + 256)
    return ([(slice(0, block * 256), False)] if block else []) + [(own, True)]


def masked_scores(keys, query, masked):
    scores = dot_right(keys, query)
    if not masked:
        return scores
    key = lax.broadcasted_iota(jnp.int32, scores.shape, 0)
    return jnp.where(key <= lax.broadcasted_iota(jnp.int32, scores.shape, 1), scores, -1e30)


epsilon = 1e-05


def low(value):
    return value.astype(jnp.bfloat16)


def standard(values):
    centred = values - jnp.mean(values, axis=-1, keepdims=True)
    factor = lax.rsqrt(jnp.mean(centred * centred, axis=-1, keepdims=True) + epsilon)
    return centred * factor, factor


def norm_back(values, gain, grad):
    unit, factor = standard(values)
    scaled = grad * gain
    through = factor * (scaled - jnp.mean(scaled, axis=-1, keepdims=True)
                        - unit * jnp.mean(scaled * unit, axis=-1, keepdims=True))
    return through, jnp.sum(grad * unit, axis=0, keepdims=True), jnp.sum(grad, axis=0, keepdims=True)


def normal_share(values):
    return 0.5 * (1.0 + lax.erf(values * 0.7071067811865476))


class Weights:
    def __init__(self, layer, source, held, sems, parts):
        self.held, self.copies = held, {}
        for part in parts:
            for half in range(2):
                for unit in (2 * part, 2 * part + 1):
                    columns = pl.ds(unit % 2 * 384, 384)
                    copy = pltpu.make_async_copy(
                        source.at[unit // 6, unit % 3, half * 2 + unit // 3 % 2, :, pl.ds(layer * 384, 384)], held.at[part, half, :, columns],
                        sems.at[unit * 2 + half])
                    copy.start()
                    self.copies[unit, half] = copy

    def ready(self, part, half):
        for unit in (2 * part, 2 * part + 1):
            copy = self.copies.pop((unit, half), None)
            if copy is not None:
                copy.wait()

    def __call__(self, part, half, columns=slice(0, 768)):
        self.ready(part, half)
        return self.held[part, half, :, columns]


def forward_kernel(layer, x_ref, rows_ref, w_ref,
                   out_ref, normed_ref, mixed_ref, heads_ref, total_ref, hidden_ref, normed_two_ref, pre_ref, active_ref,
                   held, w_sems, packed, landed, back, home, value_turned, send_a, recv_a, send_b, recv_b):
    group = Group()
    group.greet()
    weights = Weights(layer, w_ref, held, w_sems, range(6))
    entering = x_ref[...].astype(jnp.float32)
    rows = [rows_ref[n:n + 1, :] for n in range(12)]
    normed = low(standard(entering)[0] * rows[0] + rows[1])
    normed_ref[...] = normed

    def pack(kind, half, values):
        for pair in range(3):
            first, second = split_pair(low(values[:, pair * 128:pair * 128 + 128]))
            packed[half * 6 + 2 * pair, kind * 64:kind * 64 + 64] = first
            packed[half * 6 + 2 * pair + 1, kind * 64:kind * 64 + 64] = second
    for half in range(2):
        both = dot(normed, weights(0, half))
        cut = slice(half * 384, half * 384 + 384)
        pack(0, half, (both[:, EARLY] + rows[6][:, cut]) * 0.125)
        pack(1, half, both[:, LATE])
        pack(2, half, dot(normed, weights(1, half, EARLY)) + rows[7][:, cut])
    group.met()
    out_to_heads(group, packed, landed, send_a, recv_a)

    for block in range(8):
        @pl.when(group.active)
        def _():
            for index in (2 * block, 2 * block + 1):
                await_member(group, packed, landed, send_a, recv_a, index)
                for n in range(3):
                    tile = landed[index, n * 64:n * 64 + 64]
                    heads_ref[n, index * 128:index * 128 + 64] = tile[:, 0:64]
                    heads_ref[n, index * 128 + 64:index * 128 + 128] = tile[:, 64:128]
            own = slice(block * 256, block * 256 + 256)
            value_turned[:, own] = heads_ref[2, own].T
            spans = key_spans(block)
            scores = [masked_scores(heads_ref[1, keys], heads_ref[0, own], masked) for keys, masked in spans]
            largest = functools.reduce(jnp.maximum, [jnp.max(part, axis=0, keepdims=True) for part in scores])
            shares = [jnp.exp(part - largest) for part in scores]
            total = sum(jnp.sum(part, axis=0, keepdims=True) for part in shares)
            total_ref[block:block + 1, :] = largest + jnp.log(total)
            mixed = sum(dot(value_turned[:, keys], low(part)) for (keys, _), part in zip(spans, shares)) / total
            mixed = mixed.T
            for n, index in enumerate((2 * block, 2 * block + 1)):
                back[index] = low(pack_rows(mixed[n * 128:n * 128 + 128]))
                back_to_member(group, back, home, send_b, recv_b, index)

    sent_to_heads(group, packed, landed, send_a, recv_a)
    finish_back(group, back, home, send_b, recv_b)
    for pair in range(6):
        mixed_ref[0:64, pair * 128:pair * 128 + 128], mixed_ref[64:128, pair * 128:pair * 128 + 128] = join_pair(
            home[2 * pair], home[2 * pair + 1])
    hidden = entering + rows[2]
    for half in range(2):
        hidden += dot_right(mixed_ref[:, half * 384:half * 384 + 384], weights(1, half, LATE))
    hidden_ref[...] = hidden
    normed_two = low(standard(hidden)[0] * rows[3] + rows[4])
    normed_two_ref[...] = normed_two
    leaving = hidden + rows[5]
    for half in range(2):
        for n in range(2):
            cut = slice((half * 2 + n) * 768, (half * 2 + n) * 768 + 768)
            pre = dot(normed_two, weights(2 + n, half)) + rows[8 + half * 2 + n]
            pre_ref[:, cut] = pre
            active = low(pre * normal_share(pre))
            active_ref[:, cut] = active
            leaving += dot_right(active, weights(4 + n, half))
    out_ref[...] = low(leaving)


def tiles(*shape):
    return pltpu.VMEM(shape, jnp.bfloat16)


def shapes(kind, *all_shapes):
    return tuple(jax.ShapeDtypeStruct(shape, kind) for shape in all_shapes)


def layer_forward(entering, rows, gathered, layer):
    vmem = pl.BlockSpec(memory_space=pltpu.VMEM)
    block = (128, 768)
    return pl.pallas_call(
        functools.partial(forward_kernel, layer),
        out_shape=shapes(jnp.bfloat16, block, block, block, (3, 2048, 64)) + shapes(jnp.float32, (8, 256), block)
        + shapes(jnp.bfloat16, block) + shapes(jnp.float32, (128, 3072)) + shapes(jnp.bfloat16, (128, 3072)),
        in_specs=[vmem, vmem, pl.BlockSpec(memory_space=pl.ANY)],
        out_specs=(vmem,) * 9,
        scratch_shapes=[
            tiles(6, 2, 768, 768), pltpu.SemaphoreType.DMA((24,)),
            tiles(12, 192, 128), tiles(16, 192, 128), tiles(16, 64, 128), tiles(12, 64, 128), tiles(64, 2048),
            pltpu.SemaphoreType.DMA((12,)), pltpu.SemaphoreType.DMA((16,)),
            pltpu.SemaphoreType.DMA((16,)), pltpu.SemaphoreType.DMA((12,)),
        ],
        compiler_params=pltpu.CompilerParams(
            collective_id=3 + layer, has_side_effects=True, vmem_limit_bytes=56 * 2**20),
        name="layer_forward",
    )(entering, rows, gathered)


def backward_kernel(layer, arriving_ref, x_ref, rows_ref, normed_ref, mixed_ref, heads_ref, total_ref, hidden_ref,
                    normed_two_ref, pre_ref, active_ref, w_ref,
                    out_ref, sums_ref, left_ref, right_ref,
                    held, w_sems, packed, landed, back, home, grad_heads, key_turned, key_sum, value_sum,
                    grad_pre, left_out, right_out, send_a, recv_a, send_b, recv_b, pair_sems):
    group = Group()
    group.greet()
    weights = Weights(layer, w_ref, held, w_sems, (4, 5, 2, 3, 1, 0))
    rows = [rows_ref[n:n + 1, :] for n in range(12)]

    def role(core, own, other, value):
        @pl.when(group.c == core)
        def _():
            own[...] = value

        @pl.when(group.c != core)
        def _():
            other[...] = value

    def left_role(core, n, value):
        role(core, left_ref.at[n, 0:128], left_out.at[n], value)

    def right_role(core, n, half, value):
        role(core, right_ref.at[n, half, 0:128], right_out.at[n, half], value)

    def to_sibling(n, source, target):
        return pltpu.make_async_remote_copy(
            src_ref=source, dst_ref=target, send_sem=pair_sems.at[n], recv_sem=pair_sems.at[n + 3],
            device_id=(group.s, group.y, group.z, 1 - group.c, group.t), device_id_type=MESH)

    arriving = arriving_ref[...]
    carried = arriving.astype(jnp.float32)
    sums_ref[5:6, :] = jnp.sum(carried, axis=0, keepdims=True)
    grad_normed_two = jnp.zeros((128, 768), jnp.float32)
    for half in range(2):
        for n in range(2):
            place = half * 2 + n
            cut = slice(place * 768, place * 768 + 768)
            pre = pre_ref[:, cut]
            slope = normal_share(pre) + pre * (jnp.exp(pre * pre * -0.5) * 0.3989422804014327)
            grad = low(dot(arriving, weights(4 + n, half)) * slope)
            grad_pre[:, cut] = grad
            sums_ref[8 + place:9 + place, :] = jnp.sum(grad.astype(jnp.float32), axis=0, keepdims=True)
            grad_normed_two += dot_right(grad, weights(2 + n, half))
    hidden = hidden_ref[...]
    through, gain, shift = norm_back(hidden, rows[3], grad_normed_two)
    sums_ref[3:4, :], sums_ref[4:5, :] = gain, shift
    grad_hidden = carried + through
    hidden_low = low(grad_hidden)
    sums_ref[2:3, :] = jnp.sum(hidden_low.astype(jnp.float32), axis=0, keepdims=True)
    for half in range(2):
        grad_mixed = low(dot(hidden_low, weights(1, half, LATE)))
        for pair in range(3):
            packed[half * 6 + 2 * pair], packed[half * 6 + 2 * pair + 1] = split_pair(
                grad_mixed[:, pair * 128:pair * 128 + 128])
    group.met()
    out_to_heads(group, packed, landed, send_a, recv_a)

    normed, normed_two = normed_ref[...], normed_two_ref[...]
    for n, value in enumerate((normed, normed, hidden_low, normed_two)):
        left_role(0, n, value)
    for n, value in enumerate((normed_two, arriving, arriving, arriving)):
        left_role(1, n, value)
    left_copy = to_sibling(0, left_out, left_ref.at[:, 128:256])
    left_copy.start()
    for half in range(2):
        def columns(n):
            return slice(half * 1536 + n * 384, half * 1536 + n * 384 + 384)
        right_role(0, 3, half, mixed_ref[:, half * 384:half * 384 + 384])
        for n in range(2):
            right_role(0, 4 + n, half, grad_pre[:, columns(n)])
            right_role(1, n, half, grad_pre[:, columns(2 + n)])
        for n in range(4):
            right_role(1, 2 + n, half, active_ref[:, columns(n)])

    early_copy = to_sibling(2, right_out.at[3:6], right_ref.at[3:6, :, 128:256])
    early_copy.start()

    @pl.when(group.active)
    def _():
        key_turned[...] = heads_ref[1].T

    for block in reversed(range(8)):
        @pl.when(group.active)
        def _():
            for index in (2 * block, 2 * block + 1):
                await_member(group, packed, landed, send_a, recv_a, index)
                tile = landed[index]
                grad_heads[index * 128:index * 128 + 64] = tile[:, 0:64]
                grad_heads[index * 128 + 64:index * 128 + 128] = tile[:, 64:128]
            own = slice(block * 256, block * 256 + 256)
            query, grad = heads_ref[0, own], grad_heads[own]
            spans, shares, softs = key_spans(block), [], []
            for keys, masked in spans:
                shares.append(jnp.exp(masked_scores(heads_ref[1, keys], query, masked) - total_ref[block:block + 1, :]))
                softs.append(dot_right(heads_ref[2, keys], grad))
            dots = sum(jnp.sum(share * soft, axis=0, keepdims=True) for share, soft in zip(shares, softs))
            for_query = 0.0
            for (keys, _), share, soft in zip(spans, shares, softs):
                moved = low(share * (soft - dots))
                for_key, for_value = dot(moved, query), dot(low(share), grad)
                if block == 7:
                    key_sum[keys] = for_key
                    value_sum[keys] = for_value
                else:
                    key_sum[keys] = key_sum[keys] + for_key
                    value_sum[keys] = value_sum[keys] + for_value
                for_query += dot(key_turned[:, keys], moved)
            for_query = low(for_query.T).astype(jnp.float32) * 0.125
            for n, index in enumerate((2 * block, 2 * block + 1)):
                part = slice(index * 128, index * 128 + 128)
                back[index, 0:64] = low(pack_rows(for_query[n * 128:n * 128 + 128]))
                back[index, 64:128] = low(pack_rows(key_sum[part]))
                back[index, 128:192] = low(pack_rows(value_sum[part]))
                back_to_member(group, back, home, send_b, recv_b, index)

    sent_to_heads(group, packed, landed, send_a, recv_a)
    finish_back(group, back, home, send_b, recv_b)
    grad_normed = jnp.zeros((128, 768), jnp.float32)
    for half in range(2):
        def joined(kind):
            whole = []
            for pair in range(3):
                head = half * 6 + 2 * pair
                top, bottom = join_pair(home[head, kind * 64:kind * 64 + 64], home[head + 1, kind * 64:kind * 64 + 64])
                whole.append(jnp.concatenate([top, bottom], axis=0))
            return jnp.concatenate(whole, axis=1)
        grad_q, grad_k, grad_v = joined(0), joined(1), joined(2)
        cut = slice(half * 384, half * 384 + 384)
        sums_ref[6:7, cut] = jnp.sum(grad_q.astype(jnp.float32), axis=0, keepdims=True)
        sums_ref[7:8, cut] = jnp.sum(grad_v.astype(jnp.float32), axis=0, keepdims=True)
        for n, value in enumerate((grad_q, grad_k, grad_v)):
            right_role(0, n, half, value)
        grad_normed += dot_right(grad_q, weights(0, half, EARLY)) + dot_right(grad_k, weights(0, half, LATE))
        grad_normed += dot_right(grad_v, weights(1, half, EARLY))
    right_copy = to_sibling(1, right_out.at[0:3], right_ref.at[0:3, :, 128:256])
    right_copy.start()
    through, gain, shift = norm_back(x_ref[...].astype(jnp.float32), rows[0], grad_normed)
    sums_ref[0:1, :], sums_ref[1:2, :] = gain, shift
    out_ref[...] = low(grad_hidden + through)
    left_copy.wait()
    early_copy.wait()
    right_copy.wait()


def layer_backward(arriving, entering, rows, kept, gathered, layer):
    vmem = pl.BlockSpec(memory_space=pltpu.VMEM)
    block = (128, 768)
    return pl.pallas_call(
        functools.partial(backward_kernel, layer),
        out_shape=shapes(jnp.bfloat16, block) + shapes(jnp.float32, (12, 768))
        + shapes(jnp.bfloat16, (4, 256, 768), (6, 2, 256, 384)),
        in_specs=[vmem] * 11 + [pl.BlockSpec(memory_space=pl.ANY)],
        out_specs=(vmem,) * 4,
        scratch_shapes=[
            tiles(6, 2, 768, 768), pltpu.SemaphoreType.DMA((24,)),
            tiles(12, 64, 128), tiles(16, 64, 128), tiles(16, 192, 128), tiles(12, 192, 128), tiles(2048, 64), tiles(64, 2048),
            pltpu.VMEM((2048, 64), jnp.float32), pltpu.VMEM((2048, 64), jnp.float32),
            tiles(128, 3072), tiles(4, 128, 768), tiles(6, 2, 128, 384),
            pltpu.SemaphoreType.DMA((12,)), pltpu.SemaphoreType.DMA((16,)),
            pltpu.SemaphoreType.DMA((16,)), pltpu.SemaphoreType.DMA((12,)), pltpu.SemaphoreType.DMA((6,)),
        ],
        compiler_params=pltpu.CompilerParams(
            collective_id=5 + layer, has_side_effects=True, vmem_limit_bytes=60 * 2**20),
        name="layer_backward",
    )(arriving, entering, rows, *kept, gathered)


def on_device(tokens_in, cotangent, place, w_qkv, w_out, w_up, w_down, qv_bias, up_bias, vectors):
    section = lax.axis_index("s")
    half = lax.axis_index("t")
    shard = jnp.concatenate([
        w_qkv[0], w_out[0].T[None], w_up[0].reshape(24, 4, 384).transpose(1, 0, 2),
        w_down[0].reshape(4, 384, 24).transpose(0, 2, 1)]).astype(jnp.float32)
    small = jnp.concatenate([vectors[0], qv_bias.reshape(1, 768), up_bias.reshape(2, 768), jnp.zeros((7, 768), jnp.bfloat16)])
    device = jnp.arange(32, dtype=jnp.int32)
    y, z = device // 8, device // 2 % 4
    seat = ((y // 2) * 2 + z // 2) * 8 + (y % 2) * 4 + (z % 2) * 2 + device % 2
    order = jnp.sum(jnp.where(place[None, :] == seat[:, None], device[None, :], 0), axis=1)
    gathered, rows, tokens, arriving = start(order, tokens_in, cotangent, small, shard)
    gathered = gathered.reshape(2, 3, 4, 768, 768)

    acts, kept, entering = [], [], [tokens]
    for layer in range(2):
        leaving, *state = layer_forward(entering[layer], rows[layer], gathered, layer)
        entering.append(leaving)
        acts.append(leaving)
        kept.append(state)
    grads_one, sums_one, left_one, right_one = layer_backward(arriving, entering[1], rows[1], kept[1], gathered, 1)
    grads_zero, sums_zero, left_zero, right_zero = layer_backward(grads_one, entering[0], rows[0], kept[0], gathered, 0)
    seq, part = place // 8, place % 8
    holder = (seq // 2 * 2 + part // 4) * 8 + (seq % 2 * 2 + part // 2 % 2) * 2 + part % 2
    full, acts_out, grads_out, total = end(
        holder, acts, (grads_zero, grads_one), (sums_zero, sums_one), (left_zero, left_one), (right_zero, right_one))
    acts_out, grads_out = acts_out[None], grads_out[None]
    grad_qkv = full[None, 0:3]
    grad_out = full[3].T[None]
    grad_up = full[4:8].transpose(1, 0, 2).reshape(1, 24, 1536)
    grad_down = full[8:12].transpose(0, 2, 1).reshape(1, 1536, 24)

    total = total.reshape(2, 9216)
    total = jnp.where(section == 0, total[0], total[1])
    grad_vectors = total[:4608].reshape(1, 6, 768)
    grad_qv = lax.dynamic_slice_in_dim(total[4608:6144].reshape(2, 768), half * 384, 384, 1)[None]
    grad_up_bias = lax.dynamic_slice_in_dim(total[6144:], half * 1536, 1536)[None]
    return acts_out, grads_out, grad_qkv, grad_out, grad_up, grad_down, grad_qv, grad_up_bias, grad_vectors


def solution(mesh):
    fine = Mesh(mesh.devices.reshape(2, 4, 4, 2, 2), ("s", "y", "z", "c", "t"))
    dp = ("y", "z", "c")
    blocks = P(None, dp + ("t",), None)
    weights = (P("s", None, dp, "t"), P("s", "t", dp), P("s", dp, "t"), P("s", "t", dp))
    small = (P("s", None, "t"), P("s", "t"), P("s", None, None))
    rows = P("s", None, dp + ("t",), None)
    return jax.shard_map(
        on_device, mesh=fine,
        in_specs=(blocks, blocks, P()) + weights + small,
        out_specs=(rows, rows) + weights + small,
        check_vma=False)
```

```python
import functools

import jax
import jax.numpy as jnp
from jax import lax
from jax.experimental import pallas as pl
from jax.experimental.pallas import tpu as pltpu
from jax.sharding import Mesh, PartitionSpec as P
MESH = pl.DeviceIdType.MESH
ORDERS = ("xyz", "yzx", "zxy")
EARLY, LATE = slice(0, 384), slice(384, 768)


class Spot:
    def __init__(self):
        self.s, self.y, self.z, self.c, self.t = (lax.axis_index(a) for a in "syzct")
        self.x = self.t * 2 + self.s

    def at(self, axis):
        return {"x": self.x, "y": self.y, "z": self.z}[axis]

    def shifted(self, axis, by):
        return lax.rem(self.at(axis) + (by + 4), 4)

    def device(self, axis, by):
        x, y, z = self.x, self.y, self.z
        moved = self.shifted(axis, by)
        if axis == "x":
            x = moved
        elif axis == "y":
            y = moved
        else:
            z = moved
        return (lax.rem(x, 2), y, z, self.c, lax.div(x, 2))

    def fourth(self, section_by, core_by):
        return (lax.rem(self.s + section_by, 2), self.y, self.z, lax.rem(self.c + core_by, 2), self.t)

    def sibling(self):
        return (self.s, self.y, self.z, 1 - self.c, self.t)


class Copies:
    def __init__(self, send_sems, recv_sems):
        self.send_sems, self.recv_sems, self.count = send_sems, recv_sems, 0
        self.sent = []

    def make(self, src, dst, device):
        n = self.count
        self.count += 1
        copy = pltpu.make_async_remote_copy(
            src_ref=src, dst_ref=dst, send_sem=self.send_sems.at[n], recv_sem=self.recv_sems.at[n],
            device_id=device, device_id_type=MESH)
        self.sent.append(copy)
        return copy

    def start(self, src, dst, device):
        copy = self.make(src, dst, device)
        copy.start()
        return copy

    def finish(self):
        for copy in self.sent:
            copy.wait_send()


class Move:
    def __init__(self, spot, order_ref, x_ref, out_ref, middle, turned, send_a, recv_a, send_b, recv_b):
        self.spot, self.order, self.turned, self.middle = spot, order_ref, turned, middle
        self.me = spot.y * 8 + spot.z * 2 + spot.c
        self.first = (x_ref, middle, send_a, recv_a)
        self.second = (turned, out_ref, send_b, recv_b)
        self.leads = range(x_ref.shape[0]) if len(x_ref.shape) == 4 else None

    def member(self, index):
        return (self.spot.s, lax.div(index, 8), lax.rem(lax.div(index, 2), 4), lax.rem(index, 2), self.spot.t)

    def piece(self, ref, index):
        return ref.at[index] if self.leads is None else ref.at[:, index]

    def local(self, target, to, source, index):
        if self.leads is None:
            target[to] = source[index]
        else:
            for lead in self.leads:
                target[lead, to] = source[lead, index]

    def copy(self, which, n):
        source, target, send_sems, recv_sems = which
        to = lax.rem(self.me + n, 32)
        return pltpu.make_async_remote_copy(
            src_ref=self.piece(source, to), dst_ref=self.piece(target, self.me), send_sem=send_sems.at[n],
            recv_sem=recv_sems.at[n], device_id=self.member(to), device_id_type=MESH)

    def start(self, which):
        @pl.loop(1, 32)
        def _(n):
            self.copy(which, n).start()
        source, target = which[:2]
        self.local(target, self.me, source, self.me)

    def arrive(self, which):
        source, target, send_sems, recv_sems = which

        @pl.loop(1, 32)
        def _(n):
            came = lax.rem(self.me + 32 - n, 32)
            pltpu.make_async_remote_copy(
                src_ref=self.piece(source, came), dst_ref=self.piece(target, came), send_sem=send_sems.at[n],
                recv_sem=recv_sems.at[n], device_id=self.member(came), device_id_type=MESH).wait_recv()

    def begin(self):
        self.start(self.first)

    def turn(self):
        self.arrive(self.first)

        @pl.loop(0, 32)
        def _(n):
            self.local(self.turned, n, self.middle, self.order[n])
        self.start(self.second)

    def end(self):
        self.arrive(self.second)

        @pl.loop(1, 32)
        def _(n):
            self.copy(self.first, n).wait_send()
            self.copy(self.second, n).wait_send()


def greet(spot, move):
    barrier = pltpu.get_barrier_semaphore()
    for peer in [spot.device("x", by) for by in (1, -1, 2)] + [spot.fourth(1, 1)]:
        pl.semaphore_signal(barrier, inc=1, device_id=peer, device_id_type=MESH)

    @pl.loop(1, 32)
    def _(n):
        pl.semaphore_signal(barrier, inc=1, device_id=move.member(lax.rem(move.me + n, 32)), device_id_type=MESH)


def met():
    pl.semaphore_wait(pltpu.get_barrier_semaphore(), 35)


def tile_places():
    for which in range(2):
        for row in range(8):
            for column in range(6):
                tile = which * 48 + row * 6 + column
                rows, columns = slice(row * 16, row * 16 + 16), slice(column * 128, column * 128 + 128)
                yield which, rows, columns, tile // 3, slice(tile % 3 * 16, tile % 3 * 16 + 16)


def pack_tiles(first, second, target):
    for which, rows, columns, piece, part in tile_places():
        target[piece, part] = (first, second)[which][rows, columns]


def unpack_tiles(source, first, second):
    for which, rows, columns, piece, part in tile_places():
        target = (first, second)[which]
        target[rows, columns] = source[piece, part].astype(target.dtype)


def move_scratch(shape):
    return [pltpu.VMEM(shape, jnp.bfloat16)] * 2 + [pltpu.SemaphoreType.DMA((32,))] * 4


FOURTHS = ((0, 1), (1, 0), (1, 1))


def gather_steps(spot, copies, own_ref, out_ref):
    half = out_ref.at[spot.c]

    def part(k, order, phase, position, piece=None):
        axis = order[phase]
        index = {}
        for n, name in enumerate(order):
            index[name] = slice(None) if n < phase else spot.at(name)
        index[axis] = position
        if piece is not None:
            index[order[0]] = pl.ds(*piece)
        return half.at[k, index["x"], index["y"], index["z"]]

    def ring(k, order, phase, position, piece, by):
        ref = part(k, order, phase, position, piece)
        return copies.start(ref, ref, spot.device(order[phase], by))

    def push(k, order, phase, position, piece):
        ref = part(k, order, phase, position, piece)
        return copies.start(ref, ref, spot.sibling())

    pushes = []
    for phase in range(3):
        if phase == 1:
            to_right, to_left = [(0, 2), (2, 2)], [(2, 2), (0, 2)]
            pass_right, pass_left = [(0, 2)], [(2, 2)]
        elif phase == 2:
            to_right, to_left = [(0, 1), (1, 1), (2, 1), (3, 1)], [(2, 1), (3, 1), (0, 1), (1, 1)]
            pass_right, pass_left = [(0, 1), (1, 1)], [(2, 1), (3, 1)]
        if phase == 0:
            straight = []
            for k, order in enumerate(ORDERS):
                for by in (2, 1, -1):
                    straight.append(copies.start(
                        own_ref.at[k], part(k, order, 0, spot.at(order[0])), spot.device(order[0], by)))
            yield
            for copy in straight:
                copy.wait_recv()
            continue
        first = {}
        for n in range(len(to_right)):
            for k, order in enumerate(ORDERS):
                me = spot.at(order[phase])
                first[k, "r", to_right[n]] = ring(k, order, phase, me, to_right[n], 1)
                first[k, "l", to_left[n]] = ring(k, order, phase, me, to_left[n], -1)
        if phase == 2:
            for k, order in enumerate(ORDERS):
                pushes.append(push(k, order, phase, spot.at(order[phase]), None))
        yield
        second = []
        for n in range(len(to_right)):
            for k, order in enumerate(ORDERS):
                axis = order[phase]
                before, after = spot.shifted(axis, -1), spot.shifted(axis, 1)
                first[k, "r", to_right[n]].wait_recv()
                if to_right[n] in pass_right:
                    second.append((k, to_right[n], ring(k, order, phase, before, to_right[n], 1)))
                first[k, "l", to_left[n]].wait_recv()
                if to_left[n] in pass_left:
                    second.append((k, to_left[n], ring(k, order, phase, after, to_left[n], -1)))
                if phase == 2:
                    pushes.append(push(k, order, phase, before, to_right[n]))
                    pushes.append(push(k, order, phase, after, to_left[n]))
            yield
        for k, piece, copy in second:
            copy.wait_recv()
            if phase == 2:
                order = ORDERS[k]
                pushes.append(push(k, order, phase, spot.shifted(order[phase], 2), piece))
    for copy in pushes:
        copy.wait_recv()
    copies.finish()


def place_own(spot, block_ref, out_ref, sems):
    return [pltpu.make_async_copy(block_ref.at[k], out_ref.at[spot.c, k, spot.x, spot.y, spot.z], sems.at[k]) for k in range(3)]


GATHERED = (2, 3, 4, 4, 4, 48, 768)


def gather_scratch():
    return [pltpu.SemaphoreType.DMA((112,)), pltpu.SemaphoreType.DMA((112,)), pltpu.SemaphoreType.DMA((3,))]


def start_kernel(order_ref, tokens_ref, cotangent_ref, small_ref, shard_ref, w_ref, rows_ref, tokens_out, cotangent_out,
                 x_ref, moved_ref, fourths, own, smalls, pair_sems, send_sems, recv_sems, own_sems, *move_refs):
    spot = Spot()
    move = Move(spot, order_ref, x_ref, moved_ref, *move_refs)
    copies = Copies(send_sems, recv_sems)
    greet(spot, move)
    micro = lax.rem(spot.s + spot.t, 2)
    pack_tiles(tokens_ref.at[micro], cotangent_ref.at[micro], x_ref)
    met()
    near = []
    for n, (section_by, core_by) in enumerate(FOURTHS):
        section, core = lax.rem(spot.s + section_by, 2), lax.rem(spot.c + core_by, 2)
        near.append(pltpu.make_async_remote_copy(
            src_ref=shard_ref.at[pl.ds((core * 2 + section) * 3, 3)], dst_ref=fourths.at[spot.s * 2 + spot.c],
            send_sem=pair_sems.at[n], recv_sem=pair_sems.at[n + 6],
            device_id=spot.fourth(section_by, core_by), device_id_type=MESH))
    for n, by in enumerate((1, -1, 2)):
        near.append(pltpu.make_async_remote_copy(
            src_ref=small_ref, dst_ref=smalls.at[spot.x], send_sem=pair_sems.at[n + 3], recv_sem=pair_sems.at[n + 9],
            device_id=spot.device("x", by), device_id_type=MESH))
    for copy in near:
        copy.start()
    fourths[spot.s * 2 + spot.c] = shard_ref[pl.ds((spot.c * 2 + spot.s) * 3, 3)]
    smalls[spot.x] = small_ref[...]
    for copy in near[:3]:
        copy.wait_recv()

    def both_cores(layer, k):
        return jnp.concatenate([fourths[layer * 2, k], fourths[layer * 2 + 1, k]], axis=0).astype(jnp.bfloat16)
    for k in range(3):
        own[k, :, EARLY] = both_cores(0, k)
        own[k, :, LATE] = both_cores(1, k)
    placed = place_own(spot, own, w_ref, own_sems)
    steps = gather_steps(spot, copies, own, w_ref)
    next(steps)
    for copy in placed:
        copy.start()
    move.begin()
    for copy in placed:
        copy.wait()
    for copy in near[3:]:
        copy.wait_recv()
    for layer in range(2):
        first, second = smalls[layer].astype(jnp.float32), smalls[layer + 2].astype(jnp.float32)
        rows_ref[layer, 0:6] = first[0:6]
        rows_ref[layer, 6:7] = jnp.concatenate([first[6:7, EARLY], second[6:7, EARLY]], axis=1)
        rows_ref[layer, 7:8] = jnp.concatenate([first[6:7, LATE], second[6:7, LATE]], axis=1)
        rows_ref[layer, 8:10] = first[7:9]
        rows_ref[layer, 10:12] = second[7:9]
    for _ in range(2):
        next(steps)
    move.turn()
    for _ in steps:
        pass
    move.end()
    unpack_tiles(moved_ref, tokens_out, cotangent_out)
    for copy in near:
        copy.wait_send()


def start(order, tokens, cotangent, small, shard):
    vmem, any_place = pl.BlockSpec(memory_space=pltpu.VMEM), pl.BlockSpec(memory_space=pl.ANY)
    return pl.pallas_call(
        start_kernel,
        out_shape=shapes(jnp.bfloat16, GATHERED) + shapes(jnp.float32, (2, 12, 768)) + shapes(jnp.bfloat16, (128, 768), (128, 768)),
        in_specs=[pl.BlockSpec(memory_space=pltpu.SMEM)] + [vmem] * 4,
        out_specs=(any_place, vmem, vmem, vmem),
        scratch_shapes=[
            tiles(32, 48, 128), tiles(32, 48, 128),
            pltpu.VMEM((4, 3, 24, 384), jnp.float32), tiles(3, 48, 768), tiles(4, 16, 768), pltpu.SemaphoreType.DMA((12,)),
        ] + gather_scratch() + move_scratch((32, 48, 128)),
        compiler_params=pltpu.CompilerParams(collective_id=1, has_side_effects=True, vmem_limit_bytes=32 * 2**20),
        name="start",
    )(order, tokens, cotangent, small, shard)


SLOTS = (0, 0, 1, 2, 3, 3)


def reduce_steps(spot, copies, operands, out_ref, beside_steps,
                 g_ref, a0, b0, l0, r0, q0, a1, b1, l1, r1, q1, a2, b2, l2, r2):
    def make_part(k):
        for columns, (left_ref, right_ref) in zip((EARLY, LATE), operands):
            for section in range(2):
                @pl.loop(0, 2)
                def _(half):
                    unit = section * 3 + k
                    product = dot(left_ref[SLOTS[unit]], right_ref[unit, half])
                    g_ref[k, half * 2 + section, :, :, :, columns] = low(product).reshape(4, 4, 48, 384)
    first_in, second_in = [(a0, b0), (a1, b1), (a2, b2)], [(l0, r0), (l1, r1), (l2, r2)]
    quarters = [q0, q1]

    def source(k, phase, order, position, piece=None):
        axis = order[phase]
        rest = order[phase + 1:]
        if phase == 0:
            index = {axis: position}
            for n, name in enumerate(rest):
                index[name] = slice(None)
            if piece is not None:
                index[max(rest)] = pl.ds(2 * piece, 2)
            return g_ref.at[k, index["x"], index["y"], index["z"]]
        held = quarters[phase - 1].at[k]
        names = [n for n in "xyz" if n in order[phase:]]
        index = []
        for name in names:
            if name == axis:
                index.append(position)
            elif piece is not None and name == rest[0]:
                index.append(pl.ds(2 * piece, 2))
            else:
                index.append(slice(None))
        rows = slice(None)
        if phase == 2 and piece is not None:
            rows = pl.ds(0, 32) if piece == 0 else pl.ds(32, 16)
        return held.at[tuple(index) + (rows,)]

    def slot(buffer, k, phase, order, piece):
        held = buffer.at[k]
        if piece is None:
            return held
        if phase == 2:
            return held.at[pl.ds(0, 32) if piece == 0 else pl.ds(32, 16)]
        rest = order[phase + 1:]
        names = [n for n in "xyz" if n in rest]
        return held.at[tuple(pl.ds(2 * piece, 2) if n == max(rest) else slice(None) for n in names)]

    def each(shape, body):
        lead = shape[:-2]
        if not lead:
            body(())
        elif len(lead) == 1:
            @pl.loop(0, lead[0])
            def _(i):
                body((i,))
        else:
            @pl.loop(0, lead[0])
            def _(i):
                @pl.loop(0, lead[1])
                def _(j):
                    body((i, j))

    for phase in range(3):
        started = []
        if phase == 0:
            make_part(0)
            yield
        for k, gathered in enumerate(ORDERS):
            if phase == 0 and k > 0:
                make_part(k)
            order = gathered[::-1]
            axis = order[phase]
            right, left = spot.device(axis, 1), spot.device(axis, -1)
            a, b = first_in[phase]
            l, r = second_in[phase]
            far = spot.shifted(axis, 2)
            ca = copies.start(source(k, phase, order, far, 0), a.at[k], right)
            cb = copies.start(source(k, phase, order, far, 1), b.at[k], left)
            started.append([ca, cb])
            if phase == 0:
                yield
        for k, gathered in enumerate(ORDERS):
            order = gathered[::-1]
            axis = order[phase]
            right, left = spot.device(axis, 1), spot.device(axis, -1)
            l, r = second_in[phase]
            after, before = spot.shifted(axis, 1), spot.shifted(axis, -1)
            started[k].append(copies.start(source(k, phase, order, after, 1), slot(l, k, phase, order, 1), right))
            started[k].append(copies.start(source(k, phase, order, before, 0), slot(r, k, phase, order, 0), left))
        yield
        for k, gathered in enumerate(ORDERS):
            order = gathered[::-1]
            axis = order[phase]
            right, left = spot.device(axis, 1), spot.device(axis, -1)
            a, b = first_in[phase]
            l, r = second_in[phase]
            after, before = spot.shifted(axis, 1), spot.shifted(axis, -1)

            def join(buffer, own):
                def body(i):
                    buffer[i] = (buffer[i].astype(jnp.float32) + own[i].astype(jnp.float32)).astype(jnp.bfloat16)
                each(buffer.shape, body)

            started[k][0].wait_recv()
            join(a.at[k], source(k, phase, order, after, 0))
            started[k].append(copies.start(a.at[k], slot(l, k, phase, order, 0), right))
            started[k][1].wait_recv()
            join(b.at[k], source(k, phase, order, before, 1))
            started[k].append(copies.start(b.at[k], slot(r, k, phase, order, 1), left))
            yield
        beside_steps(phase)
        for k, gathered in enumerate(ORDERS):
            order = gathered[::-1]
            axis = order[phase]
            l, r = second_in[phase]
            for copy in started[k][2:]:
                copy.wait_recv()
            own = source(k, phase, order, spot.at(axis))
            left_in, right_in = l.at[k], r.at[k]
            target = out_ref.at[k] if phase == 2 else quarters[phase].at[k]

            def body(i):
                target[i] = (own[i].astype(jnp.float32) + left_in[i].astype(jnp.float32)
                             + right_in[i].astype(jnp.float32)).astype(target.dtype)
            each(target.shape, body)
            yield
    copies.finish()


def reduce_scratch():
    return [
        tiles(3, 4, 4, 4, 48, 768),
        tiles(3, 4, 2, 48, 768), tiles(3, 4, 2, 48, 768), tiles(3, 4, 4, 48, 768), tiles(3, 4, 4, 48, 768), tiles(3, 4, 4, 48, 768),
        tiles(3, 2, 48, 768), tiles(3, 2, 48, 768), tiles(3, 4, 48, 768), tiles(3, 4, 48, 768), tiles(3, 4, 48, 768),
        tiles(3, 32, 768), tiles(3, 16, 768), tiles(3, 48, 768), tiles(3, 48, 768),
    ]


REDUCED = 15


def end_kernel(order_ref, acts_0, acts_1, grads_0, grads_1, sums_0, sums_1, left_0, left_1, right_0, right_1,
               out_ref, acts_out, grads_out, total_ref, leaving, moved_ref, turned_left, sums_ref, beside, slots, summed, both, mine, pair_sems, send_sems, recv_sems, *refs):
    spot = Spot()
    copies = Copies(send_sems, recv_sems)
    move = Move(spot, order_ref, mine, moved_ref, *refs[REDUCED:])
    greet(spot, move)
    micro = lax.rem(spot.s + spot.t, 2)
    for layer, ref in enumerate((left_0, left_1)):
        for n in range(4):
            turned_left[layer, n] = ref[n].T
    def spread(axis, n):
        me = spot.at(axis)
        return [copies.start(slots.at[n, me], slots.at[n, me], spot.device(axis, by)) for by in (1, -1, 2)]

    def gathered_sum(n):
        for copy in vector_copies.pop():
            copy.wait_recv()
        return (slots[n, 0] + slots[n, 1]) + (slots[n, 2] + slots[n, 3])

    def beside_steps(phase):
        if phase == 0:
            vector_copies.pop().wait_recv()
            slots[0, spot.x] = sums_ref[...] + beside[...]
            vector_copies.append(spread("x", 0))
            move.turn()
        else:
            slots[phase, spot.at("xyz"[phase])] = gathered_sum(phase - 1)
            vector_copies.append(spread("xyz"[phase], phase))

    steps = reduce_steps(
        spot, copies, ((turned_left.at[0], right_0), (turned_left.at[1], right_1)), summed, beside_steps, *refs[:REDUCED])
    next(steps)
    met()
    next(steps)
    layers = ((acts_0, grads_0), (acts_1, grads_1))
    for section in range(2):
        @pl.when(spot.s == section)
        def _():
            pack_tiles(*layers[section], mine.at[micro])
            pack_tiles(*layers[1 - section], leaving)
    exchange = pltpu.make_async_remote_copy(
        src_ref=leaving, dst_ref=mine.at[micro], send_sem=pair_sems.at[0], recv_sem=pair_sems.at[1],
        device_id=spot.fourth(1, 0), device_id_type=MESH)
    exchange.start()
    sums_ref[0:12] = sums_0[...]
    sums_ref[12:24] = sums_1[...]
    vector_copies = [copies.start(sums_ref, beside, spot.sibling())]

    for _ in range(3):
        next(steps)
    exchange.wait_recv()
    move.begin()
    for _ in steps:
        pass
    total_ref[...] = gathered_sum(2)
    both[0] = summed[:, :, EARLY]
    both[1] = summed[:, :, LATE]
    near = []
    for n, (section_by, core_by) in enumerate(FOURTHS):
        section, core = lax.rem(spot.s + section_by, 2), lax.rem(spot.c + core_by, 2)
        near.append(pltpu.make_async_remote_copy(
            src_ref=both.at[section, :, pl.ds(pl.multiple_of(core * 24, 8), 24)],
            dst_ref=out_ref.at[pl.ds((spot.c * 2 + spot.s) * 3, 3)],
            send_sem=pair_sems.at[n + 2], recv_sem=pair_sems.at[n + 5],
            device_id=spot.fourth(section_by, core_by), device_id_type=MESH))
    for copy in near:
        copy.start()
    for core in range(2):
        @pl.when(spot.c == core)
        def _():
            out_ref[pl.ds((spot.c * 2 + spot.s) * 3, 3)] = both[spot.s, :, core * 24:core * 24 + 24]
    move.end()
    for n in range(2):
        unpack_tiles(moved_ref.at[n], acts_out.at[n], grads_out.at[n])
    exchange.wait_send()
    for copy in near:
        copy.wait()


def end(order, acts, grads, sums, lefts, rights):
    vmem = pl.BlockSpec(memory_space=pltpu.VMEM)
    return pl.pallas_call(
        end_kernel,
        out_shape=shapes(jnp.float32, (12, 24, 384)) + shapes(jnp.bfloat16, (2, 128, 768))
        + shapes(jnp.float32, (2, 128, 768), (24, 768)),
        in_specs=[pl.BlockSpec(memory_space=pltpu.SMEM)] + [vmem] * 10,
        out_specs=(vmem,) * 4,
        scratch_shapes=[
            tiles(32, 48, 128), tiles(2, 32, 48, 128), tiles(2, 4, 768, 256),
            pltpu.VMEM((24, 768), jnp.float32), pltpu.VMEM((24, 768), jnp.float32), pltpu.VMEM((3, 4, 24, 768), jnp.float32),
            pltpu.VMEM((3, 48, 768), jnp.float32), pltpu.VMEM((2, 3, 48, 384), jnp.float32), tiles(2, 32, 48, 128), pltpu.SemaphoreType.DMA((8,)),
            pltpu.SemaphoreType.DMA((80,)), pltpu.SemaphoreType.DMA((80,)),
        ] + reduce_scratch() + move_scratch((2, 32, 48, 128)),
        compiler_params=pltpu.CompilerParams(collective_id=2, has_side_effects=True, vmem_limit_bytes=60 * 2**20),
        name="end",
    )(order, *acts, *grads, *sums, *lefts, *rights)


def lanes_swapped(tile):
    return pltpu.roll(tile, 64, 1)


def split_pair(tile):
    tile = tile.astype(jnp.float32)
    top, low = tile[0:64], tile[64:128]
    left = lax.broadcasted_iota(jnp.int32, (64, 128), 1) < 64
    first = jnp.where(left, top, lanes_swapped(low))
    second = jnp.where(left, lanes_swapped(top), low)
    return first.astype(jnp.bfloat16), second.astype(jnp.bfloat16)


def join_pair(first, second):
    first, second = first.astype(jnp.float32), second.astype(jnp.float32)
    left = lax.broadcasted_iota(jnp.int32, (64, 128), 1) < 64
    top = jnp.where(left, first, lanes_swapped(second))
    low = jnp.where(left, lanes_swapped(first), second)
    return top.astype(jnp.bfloat16), low.astype(jnp.bfloat16)


def pack_rows(block):
    return jnp.concatenate([block[0:64], block[64:128]], axis=1)


class Group:
    def __init__(self):
        self.known = False
        self.s, self.y, self.z, self.c, self.t = (lax.axis_index(a) for a in "syzct")
        self.micro = lax.rem(self.s + self.t, 2)
        y, z = lax.rem(self.y, 2), lax.rem(self.z, 2)
        self.me = y * 8 + z * 4 + self.c * 2 + self.t
        self.active = jnp.logical_or(self.c == 0, lax.rem(y + z + self.t, 2) == 0)
        self.head = jnp.where(self.c == 0, y * 4 + z * 2 + self.t, 8 + y * 2 + z)

    def member(self, index):
        t = lax.rem(index, 2)
        y = lax.div(self.y, 2) * 2 + lax.div(index, 8)
        z = lax.div(self.z, 2) * 2 + lax.rem(lax.div(index, 4), 2)
        return (lax.rem(self.micro + t, 2), y, z, lax.rem(lax.div(index, 2), 2), t)

    def holder(self, head):
        late = head - 8
        y, z = lax.div(late, 2), lax.rem(late, 2)
        return jnp.where(
            head < 8, lax.div(head, 4) * 8 + lax.rem(lax.div(head, 2), 2) * 4 + lax.rem(head, 2),
            y * 8 + z * 4 + 2 + lax.rem(y + z, 2))

    def greet(self):
        barrier = pltpu.get_barrier_semaphore()

        @pl.loop(1, 16)
        def _(n):
            pl.semaphore_signal(barrier, inc=1, device_id=self.member(lax.rem(self.me + n, 16)), device_id_type=MESH)

    def met(self):
        if self.known:
            return
        self.known = True
        pl.semaphore_wait(pltpu.get_barrier_semaphore(), 15)


def out_to_heads(group, packed, landed, send_sems, recv_sems):
    @pl.loop(0, 12)
    def _(n):
        head = lax.rem(group.me + n, 12)
        target = group.holder(head)

        @pl.when(target != group.me)
        def _():
            pltpu.make_async_remote_copy(
                src_ref=packed.at[head], dst_ref=landed.at[group.me], send_sem=send_sems.at[head],
                recv_sem=recv_sems.at[group.me], device_id=group.member(target), device_id_type=MESH).start()

    @pl.when(group.active)
    def _():
        landed[group.me] = packed[group.head]


def await_member(group, packed, landed, send_sems, recv_sems, index):
    @pl.when(group.me != index)
    def _():
        pltpu.make_async_remote_copy(
            src_ref=packed.at[0], dst_ref=landed.at[index], send_sem=send_sems.at[0],
            recv_sem=recv_sems.at[index], device_id=group.member(index), device_id_type=MESH).wait_recv()


def sent_to_heads(group, packed, landed, send_sems, recv_sems):
    @pl.loop(0, 12)
    def _(head):
        @pl.when(group.holder(head) != group.me)
        def _():
            pltpu.make_async_remote_copy(
                src_ref=packed.at[head], dst_ref=landed.at[group.me], send_sem=send_sems.at[head],
                recv_sem=recv_sems.at[group.me], device_id=group.member(group.holder(head)),
                device_id_type=MESH).wait_send()


def back_to_member(group, packed, landed, send_sems, recv_sems, index):
    @pl.when(group.me != index)
    def _():
        pltpu.make_async_remote_copy(
            src_ref=packed.at[index], dst_ref=landed.at[group.head], send_sem=send_sems.at[index],
            recv_sem=recv_sems.at[group.head], device_id=group.member(index), device_id_type=MESH).start()

    @pl.when(group.me == index)
    def _():
        landed[group.head] = packed[index]


def finish_back(group, packed, landed, send_sems, recv_sems):
    @pl.when(group.active)
    def _():
        @pl.loop(0, 16)
        def _(index):
            @pl.when(group.me != index)
            def _():
                pltpu.make_async_remote_copy(
                    src_ref=packed.at[index], dst_ref=landed.at[group.head], send_sem=send_sems.at[index],
                    recv_sem=recv_sems.at[group.head], device_id=group.member(index),
                    device_id_type=MESH).wait_send()

    @pl.loop(0, 12)
    def _(head):
        holder = group.holder(head)

        @pl.when(holder != group.me)
        def _():
            pltpu.make_async_remote_copy(
                src_ref=packed.at[0], dst_ref=landed.at[head], send_sem=send_sems.at[0],
                recv_sem=recv_sems.at[head], device_id=group.member(holder), device_id_type=MESH).wait_recv()


def dot_right(left, right):
    return lax.dot_general(left, right, (((1,), (1,)), ((), ())), preferred_element_type=jnp.float32)


def dot(left, right):
    return jnp.dot(left, right, preferred_element_type=jnp.float32)


def key_spans(block):
    own = slice(block * 256, block * 256 + 256)
    return ([(slice(0, block * 256), False)] if block else []) + [(own, True)]


def masked_scores(keys, query, masked):
    scores = dot_right(keys, query)
    if not masked:
        return scores
    key = lax.broadcasted_iota(jnp.int32, scores.shape, 0)
    return jnp.where(key <= lax.broadcasted_iota(jnp.int32, scores.shape, 1), scores, -1e30)


epsilon = 1e-05


def low(value):
    return value.astype(jnp.bfloat16)


def standard(values):
    centred = values - jnp.mean(values, axis=-1, keepdims=True)
    factor = lax.rsqrt(jnp.mean(centred * centred, axis=-1, keepdims=True) + epsilon)
    return centred * factor, factor


def norm_back(values, gain, grad):
    unit, factor = standard(values)
    scaled = grad * gain
    through = factor * (scaled - jnp.mean(scaled, axis=-1, keepdims=True)
                        - unit * jnp.mean(scaled * unit, axis=-1, keepdims=True))
    return through, jnp.sum(grad * unit, axis=0, keepdims=True), jnp.sum(grad, axis=0, keepdims=True)


def normal_share(values):
    return 0.5 * (1.0 + lax.erf(values * 0.7071067811865476))


class Weights:
    def __init__(self, source, held, sems):
        self.source, self.held, self.sems, self.copies = source, held, sems, {}

    def load(self, layer, part, half):
        if layer is None:
            return
        for unit in (2 * part, 2 * part + 1):
            copy = pltpu.make_async_copy(
                self.source.at[unit // 6, unit % 3, half * 2 + unit // 3 % 2, :, pl.ds(layer * 384, 384)],
                self.held.at[part, half, :, pl.ds(unit % 2 * 384, 384)], self.sems.at[unit * 2 + half])
            copy.start()
            self.copies[unit, half] = copy

    def ready(self, part, half):
        for unit in (2 * part, 2 * part + 1):
            copy = self.copies.pop((unit, half), None)
            if copy is not None:
                copy.wait()

    def __call__(self, part, half, columns=slice(0, 768)):
        self.ready(part, half)
        return self.held[part, half, :, columns]


def forward_layer(group, weights, following, x_ref, rows_ref, out_ref,
                  normed_ref, mixed_ref, heads_ref, total_ref, hidden_ref, normed_two_ref, pre_ref, active_ref,
                  packed, landed, back, home, value_turned, send_a, recv_a, send_b, recv_b):
    entering = x_ref[...].astype(jnp.float32)
    rows = [rows_ref[n:n + 1, :] for n in range(12)]
    normed = low(standard(entering)[0] * rows[0] + rows[1])
    normed_ref[...] = normed

    def pack(kind, half, values):
        for pair in range(3):
            first, second = split_pair(low(values[:, pair * 128:pair * 128 + 128]))
            packed[half * 6 + 2 * pair, kind * 64:kind * 64 + 64] = first
            packed[half * 6 + 2 * pair + 1, kind * 64:kind * 64 + 64] = second
    for half in range(2):
        both = dot(normed, weights(0, half))
        cut = slice(half * 384, half * 384 + 384)
        pack(0, half, (both[:, EARLY] + rows[6][:, cut]) * 0.125)
        pack(1, half, both[:, LATE])
        pack(2, half, dot(normed, weights(1, half, EARLY)) + rows[7][:, cut])
        weights.load(following, 0, half)
    group.met()
    out_to_heads(group, packed, landed, send_a, recv_a)

    for block in range(8):
        @pl.when(group.active)
        def _():
            for index in (2 * block, 2 * block + 1):
                await_member(group, packed, landed, send_a, recv_a, index)
                for n in range(3):
                    tile = landed[index, n * 64:n * 64 + 64]
                    heads_ref[n, index * 128:index * 128 + 64] = tile[:, 0:64]
                    heads_ref[n, index * 128 + 64:index * 128 + 128] = tile[:, 64:128]
            own = slice(block * 256, block * 256 + 256)
            value_turned[:, own] = heads_ref[2, own].T
            spans = key_spans(block)
            scores = [masked_scores(heads_ref[1, keys], heads_ref[0, own], masked) for keys, masked in spans]
            largest = functools.reduce(jnp.maximum, [jnp.max(part, axis=0, keepdims=True) for part in scores])
            shares = [jnp.exp(part - largest) for part in scores]
            total = sum(jnp.sum(part, axis=0, keepdims=True) for part in shares)
            total_ref[block:block + 1, :] = largest + jnp.log(total)
            mixed = sum(dot(value_turned[:, keys], low(part)) for (keys, _), part in zip(spans, shares)) / total
            mixed = mixed.T
            for n, index in enumerate((2 * block, 2 * block + 1)):
                back[index] = low(pack_rows(mixed[n * 128:n * 128 + 128]))
                back_to_member(group, back, home, send_b, recv_b, index)

    sent_to_heads(group, packed, landed, send_a, recv_a)
    finish_back(group, back, home, send_b, recv_b)
    for pair in range(6):
        mixed_ref[0:64, pair * 128:pair * 128 + 128], mixed_ref[64:128, pair * 128:pair * 128 + 128] = join_pair(
            home[2 * pair], home[2 * pair + 1])
    hidden = entering + rows[2]
    for half in range(2):
        hidden += dot_right(mixed_ref[:, half * 384:half * 384 + 384], weights(1, half, LATE))
        weights.load(following, 1, half)
    hidden_ref[...] = hidden
    normed_two = low(standard(hidden)[0] * rows[3] + rows[4])
    normed_two_ref[...] = normed_two
    leaving = hidden + rows[5]
    for half in range(2):
        for n in range(2):
            cut = slice((half * 2 + n) * 768, (half * 2 + n) * 768 + 768)
            pre = dot(normed_two, weights(2 + n, half)) + rows[8 + half * 2 + n]
            pre_ref[:, cut] = pre
            active = low(pre * normal_share(pre))
            active_ref[:, cut] = active
            leaving += dot_right(active, weights(4 + n, half))
            weights.load(following, 2 + n, half)
            weights.load(following, 4 + n, half)
    out_ref[...] = low(leaving)


def tiles(*shape):
    return pltpu.VMEM(shape, jnp.bfloat16)


def shapes(kind, *all_shapes):
    return tuple(jax.ShapeDtypeStruct(shape, kind) for shape in all_shapes)


def backward_layer(group, weights, following, arriving_ref, x_ref, rows_ref, out_ref, sums_ref, left_ref, right_ref,
                   normed_ref, mixed_ref, heads_ref, total_ref, hidden_ref, normed_two_ref, pre_ref, active_ref,
                   packed, landed, back, home, grad_heads, key_turned, key_sum, value_sum,
                   grad_pre, left_out, right_out, send_a, recv_a, send_b, recv_b, pair_sems):
    rows = [rows_ref[n:n + 1, :] for n in range(12)]

    def role(core, own, other, value):
        @pl.when(group.c == core)
        def _():
            own[...] = value

        @pl.when(group.c != core)
        def _():
            other[...] = value

    def left_role(core, n, value):
        role(core, left_ref.at[n, 0:128], left_out.at[n], value)

    def right_role(core, n, half, value):
        role(core, right_ref.at[n, half, 0:128], right_out.at[n, half], value)

    def to_sibling(n, source, target):
        return pltpu.make_async_remote_copy(
            src_ref=source, dst_ref=target, send_sem=pair_sems.at[n], recv_sem=pair_sems.at[n + 3],
            device_id=(group.s, group.y, group.z, 1 - group.c, group.t), device_id_type=MESH)

    arriving = arriving_ref[...]
    carried = arriving.astype(jnp.float32)
    sums_ref[5:6, :] = jnp.sum(carried, axis=0, keepdims=True)
    grad_normed_two = jnp.zeros((128, 768), jnp.float32)
    for half in range(2):
        for n in range(2):
            place = half * 2 + n
            cut = slice(place * 768, place * 768 + 768)
            pre = pre_ref[:, cut]
            slope = normal_share(pre) + pre * (jnp.exp(pre * pre * -0.5) * 0.3989422804014327)
            grad = low(dot(arriving, weights(4 + n, half)) * slope)
            grad_pre[:, cut] = grad
            sums_ref[8 + place:9 + place, :] = jnp.sum(grad.astype(jnp.float32), axis=0, keepdims=True)
            grad_normed_two += dot_right(grad, weights(2 + n, half))
            weights.load(following, 4 + n, half)
            weights.load(following, 2 + n, half)
    hidden = hidden_ref[...]
    through, gain, shift = norm_back(hidden, rows[3], grad_normed_two)
    sums_ref[3:4, :], sums_ref[4:5, :] = gain, shift
    grad_hidden = carried + through
    hidden_low = low(grad_hidden)
    sums_ref[2:3, :] = jnp.sum(hidden_low.astype(jnp.float32), axis=0, keepdims=True)
    for half in range(2):
        grad_mixed = low(dot(hidden_low, weights(1, half, LATE)))
        for pair in range(3):
            packed[half * 6 + 2 * pair], packed[half * 6 + 2 * pair + 1] = split_pair(
                grad_mixed[:, pair * 128:pair * 128 + 128])
    out_to_heads(group, packed, landed, send_a, recv_a)

    normed, normed_two = normed_ref[...], normed_two_ref[...]
    for n, value in enumerate((normed, normed, hidden_low, normed_two)):
        left_role(0, n, value)
    for n, value in enumerate((normed_two, arriving, arriving, arriving)):
        left_role(1, n, value)
    left_copy = to_sibling(0, left_out, left_ref.at[:, 128:256])
    left_copy.start()
    for half in range(2):
        def columns(n):
            return slice(half * 1536 + n * 384, half * 1536 + n * 384 + 384)
        right_role(0, 3, half, mixed_ref[:, half * 384:half * 384 + 384])
        for n in range(2):
            right_role(0, 4 + n, half, grad_pre[:, columns(n)])
            right_role(1, n, half, grad_pre[:, columns(2 + n)])
        for n in range(4):
            right_role(1, 2 + n, half, active_ref[:, columns(n)])

    early_copy = to_sibling(2, right_out.at[3:6], right_ref.at[3:6, :, 128:256])
    early_copy.start()

    @pl.when(group.active)
    def _():
        key_turned[...] = heads_ref[1].T

    for block in reversed(range(8)):
        @pl.when(group.active)
        def _():
            for index in (2 * block, 2 * block + 1):
                await_member(group, packed, landed, send_a, recv_a, index)
                tile = landed[index]
                grad_heads[index * 128:index * 128 + 64] = tile[:, 0:64]
                grad_heads[index * 128 + 64:index * 128 + 128] = tile[:, 64:128]
            own = slice(block * 256, block * 256 + 256)
            query, grad = heads_ref[0, own], grad_heads[own]
            spans, shares, softs = key_spans(block), [], []
            for keys, masked in spans:
                shares.append(jnp.exp(masked_scores(heads_ref[1, keys], query, masked) - total_ref[block:block + 1, :]))
                softs.append(dot_right(heads_ref[2, keys], grad))
            dots = sum(jnp.sum(share * soft, axis=0, keepdims=True) for share, soft in zip(shares, softs))
            for_query = 0.0
            for (keys, _), share, soft in zip(spans, shares, softs):
                moved = low(share * (soft - dots))
                for_key, for_value = dot(moved, query), dot(low(share), grad)
                if block == 7:
                    key_sum[keys] = for_key
                    value_sum[keys] = for_value
                else:
                    key_sum[keys] = key_sum[keys] + for_key
                    value_sum[keys] = value_sum[keys] + for_value
                for_query += dot(key_turned[:, keys], moved)
            for_query = low(for_query.T).astype(jnp.float32) * 0.125
            for n, index in enumerate((2 * block, 2 * block + 1)):
                part = slice(index * 128, index * 128 + 128)
                back[index, 0:64] = low(pack_rows(for_query[n * 128:n * 128 + 128]))
                back[index, 64:128] = low(pack_rows(key_sum[part]))
                back[index, 128:192] = low(pack_rows(value_sum[part]))
                back_to_member(group, back, home, send_b, recv_b, index)

    sent_to_heads(group, packed, landed, send_a, recv_a)
    finish_back(group, back, home, send_b, recv_b)
    grad_normed = jnp.zeros((128, 768), jnp.float32)
    for half in range(2):
        def joined(kind):
            whole = []
            for pair in range(3):
                head = half * 6 + 2 * pair
                top, bottom = join_pair(home[head, kind * 64:kind * 64 + 64], home[head + 1, kind * 64:kind * 64 + 64])
                whole.append(jnp.concatenate([top, bottom], axis=0))
            return jnp.concatenate(whole, axis=1)
        grad_q, grad_k, grad_v = joined(0), joined(1), joined(2)
        cut = slice(half * 384, half * 384 + 384)
        sums_ref[6:7, cut] = jnp.sum(grad_q.astype(jnp.float32), axis=0, keepdims=True)
        sums_ref[7:8, cut] = jnp.sum(grad_v.astype(jnp.float32), axis=0, keepdims=True)
        for n, value in enumerate((grad_q, grad_k, grad_v)):
            right_role(0, n, half, value)
        grad_normed += dot_right(grad_q, weights(0, half, EARLY)) + dot_right(grad_k, weights(0, half, LATE))
        grad_normed += dot_right(grad_v, weights(1, half, EARLY))
        weights.load(following, 1, half)
        weights.load(following, 0, half)
    right_copy = to_sibling(1, right_out.at[0:3], right_ref.at[0:3, :, 128:256])
    right_copy.start()
    through, gain, shift = norm_back(x_ref[...].astype(jnp.float32), rows[0], grad_normed)
    sums_ref[0:1, :], sums_ref[1:2, :] = gain, shift
    out_ref[...] = low(grad_hidden + through)
    left_copy.wait()
    early_copy.wait()
    right_copy.wait()


def layers_kernel(tokens_ref, cotangent_ref, rows_ref, w_ref,
                  acts_0, acts_1, grads_0, grads_1, sums_0, sums_1, left_0, left_1, right_0, right_1,
                  held, w_sems, *refs):
    group = Group()
    group.greet()
    weights = Weights(w_ref, held, w_sems)
    for part in range(6):
        for half in range(2):
            weights.load(0, part, half)
    states, forward, backward, pair_sems = (refs[0:8], refs[8:16]), refs[16:25], refs[25:-1], refs[-1]
    forward_layer(group, weights, 1, tokens_ref, rows_ref.at[0], acts_0, *states[0], *forward)
    forward_layer(group, weights, None, acts_0, rows_ref.at[1], acts_1, *states[1], *forward)
    backward_layer(group, weights, 0, cotangent_ref, acts_0, rows_ref.at[1], grads_1, sums_1, left_1, right_1,
                   *states[1], *backward, pair_sems.at[1])
    backward_layer(group, weights, None, grads_1, tokens_ref, rows_ref.at[0], grads_0, sums_0, left_0, right_0,
                   *states[0], *backward, pair_sems.at[0])


def layers(tokens, cotangent, rows, gathered):
    vmem = pl.BlockSpec(memory_space=pltpu.VMEM)
    block = (128, 768)
    wide = lambda *shape: pltpu.VMEM(shape, jnp.float32)
    state = [
        tiles(*block), tiles(*block), tiles(3, 2048, 64), wide(8, 256), wide(*block), tiles(*block), wide(128, 3072),
        tiles(128, 3072)]
    sems = [pltpu.SemaphoreType.DMA((count,)) for count in (12, 16, 16, 12)]
    return pl.pallas_call(
        layers_kernel,
        out_shape=shapes(jnp.bfloat16, block, block, block, block) + shapes(jnp.float32, (12, 768), (12, 768))
        + shapes(jnp.bfloat16, (4, 256, 768), (4, 256, 768), (6, 2, 256, 384), (6, 2, 256, 384)),
        in_specs=[vmem, vmem, vmem, pl.BlockSpec(memory_space=pl.ANY)],
        out_specs=(vmem,) * 10,
        scratch_shapes=[tiles(6, 2, 768, 768), pltpu.SemaphoreType.DMA((24,))] + state + state + [
            tiles(12, 192, 128), tiles(16, 192, 128), tiles(16, 64, 128), tiles(12, 64, 128), tiles(64, 2048),
        ] + sems + [
            tiles(12, 64, 128), tiles(16, 64, 128), tiles(16, 192, 128), tiles(12, 192, 128), tiles(2048, 64), tiles(64, 2048),
            wide(2048, 64), wide(2048, 64), tiles(128, 3072), tiles(4, 128, 768), tiles(6, 2, 128, 384),
        ] + sems + [pltpu.SemaphoreType.DMA((2, 6))],
        compiler_params=pltpu.CompilerParams(collective_id=3, has_side_effects=True, vmem_limit_bytes=62 * 2**20),
        name="layers",
    )(tokens, cotangent, rows, gathered)


def on_device(tokens_in, cotangent, place, w_qkv, w_out, w_up, w_down, qv_bias, up_bias, vectors):
    section = lax.axis_index("s")
    half = lax.axis_index("t")
    shard = jnp.concatenate([
        w_qkv[0], w_out[0].T[None], w_up[0].reshape(24, 4, 384).transpose(1, 0, 2),
        w_down[0].reshape(4, 384, 24).transpose(0, 2, 1)]).astype(jnp.float32)
    small = jnp.concatenate([vectors[0], qv_bias.reshape(1, 768), up_bias.reshape(2, 768), jnp.zeros((7, 768), jnp.bfloat16)])
    device = jnp.arange(32, dtype=jnp.int32)
    y, z = device // 8, device // 2 % 4
    seat = ((y // 2) * 2 + z // 2) * 8 + (y % 2) * 4 + (z % 2) * 2 + device % 2
    order = jnp.sum(jnp.where(place[None, :] == seat[:, None], device[None, :], 0), axis=1)
    gathered, rows, tokens, arriving = start(order, tokens_in, cotangent, small, shard)
    gathered = gathered.reshape(2, 3, 4, 768, 768)

    acts_zero, acts_one, grads_zero, grads_one, sums_zero, sums_one, *operands = layers(tokens, arriving, rows, gathered)
    left_zero, left_one, right_zero, right_one = operands
    seq, part = place // 8, place % 8
    holder = (seq // 2 * 2 + part // 4) * 8 + (seq % 2 * 2 + part // 2 % 2) * 2 + part % 2
    full, acts_out, grads_out, total = end(
        holder, (acts_zero, acts_one), (grads_zero, grads_one), (sums_zero, sums_one), (left_zero, left_one), (right_zero, right_one))
    acts_out, grads_out = acts_out[None], grads_out[None]
    grad_qkv = full[None, 0:3]
    grad_out = full[3].T[None]
    grad_up = full[4:8].transpose(1, 0, 2).reshape(1, 24, 1536)
    grad_down = full[8:12].transpose(0, 2, 1).reshape(1, 1536, 24)

    total = total.reshape(2, 9216)
    total = jnp.where(section == 0, total[0], total[1])
    grad_vectors = total[:4608].reshape(1, 6, 768)
    grad_qv = lax.dynamic_slice_in_dim(total[4608:6144].reshape(2, 768), half * 384, 384, 1)[None]
    grad_up_bias = lax.dynamic_slice_in_dim(total[6144:], half * 1536, 1536)[None]
    return acts_out, grads_out, grad_qkv, grad_out, grad_up, grad_down, grad_qv, grad_up_bias, grad_vectors


def solution(mesh):
    fine = Mesh(mesh.devices.reshape(2, 4, 4, 2, 2), ("s", "y", "z", "c", "t"))
    dp = ("y", "z", "c")
    blocks = P(None, dp + ("t",), None)
    weights = (P("s", None, dp, "t"), P("s", "t", dp), P("s", dp, "t"), P("s", "t", dp))
    small = (P("s", None, "t"), P("s", "t"), P("s", None, None))
    rows = P("s", None, dp + ("t",), None)
    return jax.shard_map(
        on_device, mesh=fine,
        in_specs=(blocks, blocks, P()) + weights + small,
        out_specs=(rows, rows) + weights + small,
        check_vma=False)
```

```python
import functools

import jax
import jax.numpy as jnp
from jax import lax
from jax.experimental import pallas as pl
from jax.experimental.pallas import tpu as pltpu
from jax.sharding import Mesh, PartitionSpec as P
MESH = pl.DeviceIdType.MESH
ORDERS = ("xyz", "yzx", "zxy")
EARLY, LATE = slice(0, 384), slice(384, 768)


class Spot:
    def __init__(self):
        self.s, self.y, self.z, self.c, self.t = (lax.axis_index(a) for a in "syzct")
        self.x = self.t * 2 + self.s

    def at(self, axis):
        return {"x": self.x, "y": self.y, "z": self.z}[axis]

    def shifted(self, axis, by):
        return lax.rem(self.at(axis) + (by + 4), 4)

    def device(self, axis, by):
        x, y, z = self.x, self.y, self.z
        moved = self.shifted(axis, by)
        if axis == "x":
            x = moved
        elif axis == "y":
            y = moved
        else:
            z = moved
        return (lax.rem(x, 2), y, z, self.c, lax.div(x, 2))

    def fourth(self, section_by, core_by):
        return (lax.rem(self.s + section_by, 2), self.y, self.z, lax.rem(self.c + core_by, 2), self.t)

    def sibling(self):
        return (self.s, self.y, self.z, 1 - self.c, self.t)


class Copies:
    def __init__(self, send_sems, recv_sems):
        self.send_sems, self.recv_sems, self.count = send_sems, recv_sems, 0
        self.sent = []

    def make(self, src, dst, device):
        n = self.count
        self.count += 1
        copy = pltpu.make_async_remote_copy(
            src_ref=src, dst_ref=dst, send_sem=self.send_sems.at[n], recv_sem=self.recv_sems.at[n],
            device_id=device, device_id_type=MESH)
        self.sent.append(copy)
        return copy

    def start(self, src, dst, device):
        copy = self.make(src, dst, device)
        copy.start()
        return copy

    def finish(self):
        for copy in self.sent:
            copy.wait_send()


class Move:
    def __init__(self, spot, order_ref, x_ref, out_ref, middle, turned, send_a, recv_a, send_b, recv_b):
        self.spot, self.order, self.turned, self.middle = spot, order_ref, turned, middle
        self.me = spot.y * 8 + spot.z * 2 + spot.c
        self.first = (x_ref, middle, send_a, recv_a)
        self.second = (turned, out_ref, send_b, recv_b)
        self.leads = range(x_ref.shape[0]) if len(x_ref.shape) == 4 else None

    def member(self, index):
        return (self.spot.s, lax.div(index, 8), lax.rem(lax.div(index, 2), 4), lax.rem(index, 2), self.spot.t)

    def piece(self, ref, index):
        return ref.at[index] if self.leads is None else ref.at[:, index]

    def local(self, target, to, source, index):
        if self.leads is None:
            target[to] = source[index]
        else:
            for lead in self.leads:
                target[lead, to] = source[lead, index]

    def copy(self, which, n):
        source, target, send_sems, recv_sems = which
        to = lax.rem(self.me + n, 32)
        return pltpu.make_async_remote_copy(
            src_ref=self.piece(source, to), dst_ref=self.piece(target, self.me), send_sem=send_sems.at[n],
            recv_sem=recv_sems.at[n], device_id=self.member(to), device_id_type=MESH)

    def start(self, which):
        @pl.loop(1, 32)
        def _(n):
            self.copy(which, n).start()
        source, target = which[:2]
        self.local(target, self.me, source, self.me)

    def arrive(self, which):
        source, target, send_sems, recv_sems = which

        @pl.loop(1, 32)
        def _(n):
            came = lax.rem(self.me + 32 - n, 32)
            pltpu.make_async_remote_copy(
                src_ref=self.piece(source, came), dst_ref=self.piece(target, came), send_sem=send_sems.at[n],
                recv_sem=recv_sems.at[n], device_id=self.member(came), device_id_type=MESH).wait_recv()

    def begin(self):
        self.start(self.first)

    def turn(self):
        self.arrive(self.first)

        @pl.loop(0, 32)
        def _(n):
            self.local(self.turned, n, self.middle, self.order[n])
        self.start(self.second)

    def end(self):
        self.arrive(self.second)

        @pl.loop(1, 32)
        def _(n):
            self.copy(self.first, n).wait_send()
            self.copy(self.second, n).wait_send()


def greet(spot, move):
    barrier = pltpu.get_barrier_semaphore()
    for peer in [spot.device("x", by) for by in (1, -1, 2)] + [spot.fourth(1, 1)]:
        pl.semaphore_signal(barrier, inc=1, device_id=peer, device_id_type=MESH)

    @pl.loop(1, 32)
    def _(n):
        pl.semaphore_signal(barrier, inc=1, device_id=move.member(lax.rem(move.me + n, 32)), device_id_type=MESH)


def met():
    pl.semaphore_wait(pltpu.get_barrier_semaphore(), 35)


def tile_places():
    for which in range(2):
        for row in range(8):
            for column in range(6):
                tile = which * 48 + row * 6 + column
                rows, columns = slice(row * 16, row * 16 + 16), slice(column * 128, column * 128 + 128)
                yield which, rows, columns, tile // 3, slice(tile % 3 * 16, tile % 3 * 16 + 16)


def pack_tiles(first, second, target):
    for which, rows, columns, piece, part in tile_places():
        target[piece, part] = (first, second)[which][rows, columns]


def unpack_tiles(source, first, second):
    for which, rows, columns, piece, part in tile_places():
        target = (first, second)[which]
        target[rows, columns] = source[piece, part].astype(target.dtype)


def move_scratch(shape):
    return [pltpu.VMEM(shape, jnp.bfloat16)] * 2 + [pltpu.SemaphoreType.DMA((32,))] * 4


FOURTHS = ((0, 1), (1, 0), (1, 1))


def gather_steps(spot, copies, own_ref, out_ref):
    half = out_ref.at[spot.c]

    def part(k, order, phase, position, piece=None):
        axis = order[phase]
        index = {}
        for n, name in enumerate(order):
            index[name] = slice(None) if n < phase else spot.at(name)
        index[axis] = position
        if piece is not None:
            index[order[0]] = pl.ds(*piece)
        return half.at[k, index["x"], index["y"], index["z"]]

    def ring(k, order, phase, position, piece, by):
        ref = part(k, order, phase, position, piece)
        return copies.start(ref, ref, spot.device(order[phase], by))

    def push(k, order, phase, position, piece):
        ref = part(k, order, phase, position, piece)
        return copies.start(ref, ref, spot.sibling())

    pushes = []
    for phase in range(3):
        if phase == 1:
            to_right, to_left = [(0, 2), (2, 2)], [(2, 2), (0, 2)]
            pass_right, pass_left = [(0, 2)], [(2, 2)]
        elif phase == 2:
            to_right, to_left = [(0, 1), (1, 1), (2, 1), (3, 1)], [(2, 1), (3, 1), (0, 1), (1, 1)]
            pass_right, pass_left = [(0, 1), (1, 1)], [(2, 1), (3, 1)]
        if phase == 0:
            straight = []
            for k, order in enumerate(ORDERS):
                for by in (2, 1, -1):
                    straight.append(copies.start(
                        own_ref.at[k], part(k, order, 0, spot.at(order[0])), spot.device(order[0], by)))
            yield
            for copy in straight:
                copy.wait_recv()
            continue
        first = {}
        for n in range(len(to_right)):
            for k, order in enumerate(ORDERS):
                me = spot.at(order[phase])
                first[k, "r", to_right[n]] = ring(k, order, phase, me, to_right[n], 1)
                first[k, "l", to_left[n]] = ring(k, order, phase, me, to_left[n], -1)
        if phase == 2:
            for k, order in enumerate(ORDERS):
                pushes.append(push(k, order, phase, spot.at(order[phase]), None))
        yield
        second = []
        for n in range(len(to_right)):
            for k, order in enumerate(ORDERS):
                axis = order[phase]
                before, after = spot.shifted(axis, -1), spot.shifted(axis, 1)
                first[k, "r", to_right[n]].wait_recv()
                if to_right[n] in pass_right:
                    second.append((k, to_right[n], ring(k, order, phase, before, to_right[n], 1)))
                first[k, "l", to_left[n]].wait_recv()
                if to_left[n] in pass_left:
                    second.append((k, to_left[n], ring(k, order, phase, after, to_left[n], -1)))
                if phase == 2:
                    pushes.append(push(k, order, phase, before, to_right[n]))
                    pushes.append(push(k, order, phase, after, to_left[n]))
            yield
        for k, piece, copy in second:
            copy.wait_recv()
            if phase == 2:
                order = ORDERS[k]
                pushes.append(push(k, order, phase, spot.shifted(order[phase], 2), piece))
    for copy in pushes:
        copy.wait_recv()
    copies.finish()


def place_own(spot, block_ref, out_ref, sems):
    return [pltpu.make_async_copy(block_ref.at[k], out_ref.at[spot.c, k, spot.x, spot.y, spot.z], sems.at[k]) for k in range(3)]


GATHERED = (2, 3, 4, 4, 4, 48, 768)


def gather_scratch():
    return [pltpu.SemaphoreType.DMA((112,)), pltpu.SemaphoreType.DMA((112,)), pltpu.SemaphoreType.DMA((3,))]


def start_kernel(order_ref, tokens_ref, cotangent_ref, vectors_ref, qv_ref, up_ref, shard_ref, w_ref, rows_ref, tokens_out, cotangent_out,
                 small_ref, x_ref, moved_ref, fourths, own, smalls, pair_sems, send_sems, recv_sems, own_sems, *move_refs):
    spot = Spot()
    move = Move(spot, order_ref, x_ref, moved_ref, *move_refs)
    copies = Copies(send_sems, recv_sems)
    greet(spot, move)
    micro = lax.rem(spot.s + spot.t, 2)
    small_ref[...] = jnp.zeros_like(small_ref)
    small_ref[0:6] = vectors_ref[0].astype(jnp.float32)
    small_ref[6:7, EARLY] = qv_ref[0, 0:1].astype(jnp.float32)
    small_ref[6:7, LATE] = qv_ref[0, 1:2].astype(jnp.float32)
    small_ref[7:8] = up_ref[:, 0:768].astype(jnp.float32)
    small_ref[8:9] = up_ref[:, 768:1536].astype(jnp.float32)
    pack_tiles(tokens_ref.at[micro], cotangent_ref.at[micro], x_ref)
    met()
    near = []
    for n, (section_by, core_by) in enumerate(FOURTHS):
        section, core = lax.rem(spot.s + section_by, 2), lax.rem(spot.c + core_by, 2)
        near.append(pltpu.make_async_remote_copy(
            src_ref=shard_ref.at[pl.ds((core * 2 + section) * 3, 3)], dst_ref=fourths.at[spot.s * 2 + spot.c],
            send_sem=pair_sems.at[n], recv_sem=pair_sems.at[n + 6],
            device_id=spot.fourth(section_by, core_by), device_id_type=MESH))
    for n, by in enumerate((1, -1, 2)):
        near.append(pltpu.make_async_remote_copy(
            src_ref=small_ref, dst_ref=smalls.at[spot.x], send_sem=pair_sems.at[n + 3], recv_sem=pair_sems.at[n + 9],
            device_id=spot.device("x", by), device_id_type=MESH))
    for copy in near:
        copy.start()
    fourths[spot.s * 2 + spot.c] = shard_ref[pl.ds((spot.c * 2 + spot.s) * 3, 3)]
    smalls[spot.x] = small_ref[...]
    for copy in near[:3]:
        copy.wait_recv()

    def both_cores(layer, k):
        return jnp.concatenate([fourths[layer * 2, k], fourths[layer * 2 + 1, k]], axis=0).astype(jnp.bfloat16)
    for k in range(3):
        own[k, :, EARLY] = both_cores(0, k)
        own[k, :, LATE] = both_cores(1, k)
    placed = place_own(spot, own, w_ref, own_sems)
    steps = gather_steps(spot, copies, own, w_ref)
    next(steps)
    for copy in placed:
        copy.start()
    move.begin()
    for copy in placed:
        copy.wait()
    for copy in near[3:]:
        copy.wait_recv()
    for layer in range(2):
        first, second = smalls[layer], smalls[layer + 2]
        rows_ref[layer, 0:6] = first[0:6]
        rows_ref[layer, 6:7] = jnp.concatenate([first[6:7, EARLY], second[6:7, EARLY]], axis=1)
        rows_ref[layer, 7:8] = jnp.concatenate([first[6:7, LATE], second[6:7, LATE]], axis=1)
        rows_ref[layer, 8:10] = first[7:9]
        rows_ref[layer, 10:12] = second[7:9]
    for _ in range(2):
        next(steps)
    move.turn()
    for _ in steps:
        pass
    move.end()
    unpack_tiles(moved_ref, tokens_out, cotangent_out)
    for copy in near:
        copy.wait_send()


def start(order, tokens, cotangent, vectors, qv_bias, up_bias, shard):
    vmem, any_place = pl.BlockSpec(memory_space=pltpu.VMEM), pl.BlockSpec(memory_space=pl.ANY)
    return pl.pallas_call(
        start_kernel,
        out_shape=shapes(jnp.bfloat16, GATHERED) + shapes(jnp.float32, (2, 12, 768)) + shapes(jnp.bfloat16, (128, 768), (128, 768)),
        in_specs=[pl.BlockSpec(memory_space=pltpu.SMEM)] + [vmem] * 6,
        out_specs=(any_place, vmem, vmem, vmem),
        scratch_shapes=[
            pltpu.VMEM((16, 768), jnp.float32), tiles(32, 48, 128), tiles(32, 48, 128),
            pltpu.VMEM((4, 3, 24, 384), jnp.float32), tiles(3, 48, 768), pltpu.VMEM((4, 16, 768), jnp.float32), pltpu.SemaphoreType.DMA((12,)),
        ] + gather_scratch() + move_scratch((32, 48, 128)),
        compiler_params=pltpu.CompilerParams(collective_id=1, has_side_effects=True, vmem_limit_bytes=32 * 2**20),
        name="start",
    )(order, tokens, cotangent, vectors, qv_bias, up_bias, shard)


SLOTS = (0, 0, 1, 2, 3, 3)


def reduce_steps(spot, copies, operands, out_ref, beside_steps,
                 g_ref, a0, b0, l0, r0, q0, a1, b1, l1, r1, q1, a2, b2, l2, r2):
    def make_part(k):
        for columns, (left_ref, right_ref) in zip((EARLY, LATE), operands):
            for section in range(2):
                @pl.loop(0, 2)
                def _(half):
                    unit = section * 3 + k
                    product = dot(left_ref[SLOTS[unit]], right_ref[unit, half])
                    g_ref[k, half * 2 + section, :, :, :, columns] = low(product).reshape(4, 4, 48, 384)
    first_in, second_in = [(a0, b0), (a1, b1), (a2, b2)], [(l0, r0), (l1, r1), (l2, r2)]
    quarters = [q0, q1]

    def source(k, phase, order, position, piece=None):
        axis = order[phase]
        rest = order[phase + 1:]
        if phase == 0:
            index = {axis: position}
            for n, name in enumerate(rest):
                index[name] = slice(None)
            if piece is not None:
                index[max(rest)] = pl.ds(2 * piece, 2)
            return g_ref.at[k, index["x"], index["y"], index["z"]]
        held = quarters[phase - 1].at[k]
        names = [n for n in "xyz" if n in order[phase:]]
        index = []
        for name in names:
            if name == axis:
                index.append(position)
            elif piece is not None and name == rest[0]:
                index.append(pl.ds(2 * piece, 2))
            else:
                index.append(slice(None))
        rows = slice(None)
        if phase == 2 and piece is not None:
            rows = pl.ds(0, 32) if piece == 0 else pl.ds(32, 16)
        return held.at[tuple(index) + (rows,)]

    def slot(buffer, k, phase, order, piece):
        held = buffer.at[k]
        if piece is None:
            return held
        if phase == 2:
            return held.at[pl.ds(0, 32) if piece == 0 else pl.ds(32, 16)]
        rest = order[phase + 1:]
        names = [n for n in "xyz" if n in rest]
        return held.at[tuple(pl.ds(2 * piece, 2) if n == max(rest) else slice(None) for n in names)]

    def each(shape, body):
        lead = shape[:-2]
        if not lead:
            body(())
        elif len(lead) == 1:
            @pl.loop(0, lead[0])
            def _(i):
                body((i,))
        else:
            @pl.loop(0, lead[0])
            def _(i):
                @pl.loop(0, lead[1])
                def _(j):
                    body((i, j))

    for phase in range(3):
        started = []
        if phase == 0:
            make_part(0)
            yield
        for k, gathered in enumerate(ORDERS):
            if phase == 0 and k > 0:
                make_part(k)
            order = gathered[::-1]
            axis = order[phase]
            right, left = spot.device(axis, 1), spot.device(axis, -1)
            a, b = first_in[phase]
            l, r = second_in[phase]
            far = spot.shifted(axis, 2)
            ca = copies.start(source(k, phase, order, far, 0), a.at[k], right)
            cb = copies.start(source(k, phase, order, far, 1), b.at[k], left)
            started.append([ca, cb])
            if phase == 0:
                yield
        for k, gathered in enumerate(ORDERS):
            order = gathered[::-1]
            axis = order[phase]
            right, left = spot.device(axis, 1), spot.device(axis, -1)
            l, r = second_in[phase]
            after, before = spot.shifted(axis, 1), spot.shifted(axis, -1)
            started[k].append(copies.start(source(k, phase, order, after, 1), slot(l, k, phase, order, 1), right))
            started[k].append(copies.start(source(k, phase, order, before, 0), slot(r, k, phase, order, 0), left))
        yield
        for k, gathered in enumerate(ORDERS):
            order = gathered[::-1]
            axis = order[phase]
            right, left = spot.device(axis, 1), spot.device(axis, -1)
            a, b = first_in[phase]
            l, r = second_in[phase]
            after, before = spot.shifted(axis, 1), spot.shifted(axis, -1)

            def join(buffer, own):
                def body(i):
                    buffer[i] = (buffer[i].astype(jnp.float32) + own[i].astype(jnp.float32)).astype(jnp.bfloat16)
                each(buffer.shape, body)

            started[k][0].wait_recv()
            join(a.at[k], source(k, phase, order, after, 0))
            started[k].append(copies.start(a.at[k], slot(l, k, phase, order, 0), right))
            started[k][1].wait_recv()
            join(b.at[k], source(k, phase, order, before, 1))
            started[k].append(copies.start(b.at[k], slot(r, k, phase, order, 1), left))
            yield
        beside_steps(phase)
        for k, gathered in enumerate(ORDERS):
            order = gathered[::-1]
            axis = order[phase]
            l, r = second_in[phase]
            for copy in started[k][2:]:
                copy.wait_recv()
            own = source(k, phase, order, spot.at(axis))
            left_in, right_in = l.at[k], r.at[k]
            target = out_ref.at[k] if phase == 2 else quarters[phase].at[k]

            def body(i):
                target[i] = (own[i].astype(jnp.float32) + left_in[i].astype(jnp.float32)
                             + right_in[i].astype(jnp.float32)).astype(target.dtype)
            each(target.shape, body)
            yield
    copies.finish()


def reduce_scratch():
    return [
        tiles(3, 4, 4, 4, 48, 768),
        tiles(3, 4, 2, 48, 768), tiles(3, 4, 2, 48, 768), tiles(3, 4, 4, 48, 768), tiles(3, 4, 4, 48, 768), tiles(3, 4, 4, 48, 768),
        tiles(3, 2, 48, 768), tiles(3, 2, 48, 768), tiles(3, 4, 48, 768), tiles(3, 4, 48, 768), tiles(3, 4, 48, 768),
        tiles(3, 32, 768), tiles(3, 16, 768), tiles(3, 48, 768), tiles(3, 48, 768),
    ]


REDUCED = 15


def end_kernel(order_ref, acts_0, acts_1, grads_0, grads_1, sums_0, sums_1, left_0, left_1, right_0, right_1,
               out_ref, acts_out, grads_out, vectors_out, qv_out, up_out, total_ref, leaving, moved_ref, turned_left, sums_ref, beside, slots, summed, both, mine, pair_sems, send_sems, recv_sems, *refs):
    spot = Spot()
    copies = Copies(send_sems, recv_sems)
    move = Move(spot, order_ref, mine, moved_ref, *refs[REDUCED:])
    greet(spot, move)
    micro = lax.rem(spot.s + spot.t, 2)
    for layer, ref in enumerate((left_0, left_1)):
        for n in range(4):
            turned_left[layer, n] = ref[n].T
    def spread(axis, n):
        me = spot.at(axis)
        return [copies.start(slots.at[n, me], slots.at[n, me], spot.device(axis, by)) for by in (1, -1, 2)]

    def gathered_sum(n):
        for copy in vector_copies.pop():
            copy.wait_recv()
        return (slots[n, 0] + slots[n, 1]) + (slots[n, 2] + slots[n, 3])

    def beside_steps(phase):
        if phase == 0:
            vector_copies.pop().wait_recv()
            slots[0, spot.x] = sums_ref[...] + beside[...]
            vector_copies.append(spread("x", 0))
            move.turn()
        else:
            slots[phase, spot.at("xyz"[phase])] = gathered_sum(phase - 1)
            vector_copies.append(spread("xyz"[phase], phase))

    steps = reduce_steps(
        spot, copies, ((turned_left.at[0], right_0), (turned_left.at[1], right_1)), summed, beside_steps, *refs[:REDUCED])
    next(steps)
    met()
    next(steps)
    layers = ((acts_0, grads_0), (acts_1, grads_1))
    for section in range(2):
        @pl.when(spot.s == section)
        def _():
            pack_tiles(*layers[section], mine.at[micro])
            pack_tiles(*layers[1 - section], leaving)
    exchange = pltpu.make_async_remote_copy(
        src_ref=leaving, dst_ref=mine.at[micro], send_sem=pair_sems.at[0], recv_sem=pair_sems.at[1],
        device_id=spot.fourth(1, 0), device_id_type=MESH)
    exchange.start()
    sums_ref[0:12] = sums_0[...]
    sums_ref[12:24] = sums_1[...]
    vector_copies = [copies.start(sums_ref, beside, spot.sibling())]

    for _ in range(3):
        next(steps)
    exchange.wait_recv()
    move.begin()
    for _ in steps:
        pass
    total_ref[...] = gathered_sum(2)
    for section in range(2):
        for half in range(2):
            @pl.when(jnp.logical_and(spot.s == section, spot.t == half))
            def _():
                row = section * 12
                vectors_out[...] = total_ref[row:row + 6, :]
                for n in range(2):
                    qv_out[n:n + 1, :] = total_ref[row + 6 + n:row + 7 + n, half * 384:half * 384 + 384]
                    place = row + 8 + half * 2 + n
                    up_out[:, n * 768:n * 768 + 768] = total_ref[place:place + 1, :]
    both[0] = summed[:, :, EARLY]
    both[1] = summed[:, :, LATE]
    near = []
    for n, (section_by, core_by) in enumerate(FOURTHS):
        section, core = lax.rem(spot.s + section_by, 2), lax.rem(spot.c + core_by, 2)
        near.append(pltpu.make_async_remote_copy(
            src_ref=both.at[section, :, pl.ds(pl.multiple_of(core * 24, 8), 24)],
            dst_ref=out_ref.at[pl.ds((spot.c * 2 + spot.s) * 3, 3)],
            send_sem=pair_sems.at[n + 2], recv_sem=pair_sems.at[n + 5],
            device_id=spot.fourth(section_by, core_by), device_id_type=MESH))
    for copy in near:
        copy.start()
    for core in range(2):
        @pl.when(spot.c == core)
        def _():
            out_ref[pl.ds((spot.c * 2 + spot.s) * 3, 3)] = both[spot.s, :, core * 24:core * 24 + 24]
    move.end()
    for n in range(2):
        unpack_tiles(moved_ref.at[n], acts_out.at[n], grads_out.at[n])
    exchange.wait_send()
    for copy in near:
        copy.wait()


def end(order, acts, grads, sums, lefts, rights):
    vmem = pl.BlockSpec(memory_space=pltpu.VMEM)
    return pl.pallas_call(
        end_kernel,
        out_shape=shapes(jnp.float32, (12, 24, 384)) + shapes(jnp.bfloat16, (2, 128, 768))
        + shapes(jnp.float32, (2, 128, 768), (6, 768), (2, 384), (1, 1536)),
        in_specs=[pl.BlockSpec(memory_space=pltpu.SMEM)] + [vmem] * 10,
        out_specs=(vmem,) * 6,
        scratch_shapes=[
            pltpu.VMEM((24, 768), jnp.float32), tiles(32, 48, 128), tiles(2, 32, 48, 128), tiles(2, 4, 768, 256),
            pltpu.VMEM((24, 768), jnp.float32), pltpu.VMEM((24, 768), jnp.float32), pltpu.VMEM((3, 4, 24, 768), jnp.float32),
            pltpu.VMEM((3, 48, 768), jnp.float32), pltpu.VMEM((2, 3, 48, 384), jnp.float32), tiles(2, 32, 48, 128), pltpu.SemaphoreType.DMA((8,)),
            pltpu.SemaphoreType.DMA((80,)), pltpu.SemaphoreType.DMA((80,)),
        ] + reduce_scratch() + move_scratch((2, 32, 48, 128)),
        compiler_params=pltpu.CompilerParams(collective_id=2, has_side_effects=True, vmem_limit_bytes=60 * 2**20),
        name="end",
    )(order, *acts, *grads, *sums, *lefts, *rights)


def lanes_swapped(tile):
    return pltpu.roll(tile, 64, 1)


def split_pair(tile):
    tile = tile.astype(jnp.float32)
    top, low = tile[0:64], tile[64:128]
    left = lax.broadcasted_iota(jnp.int32, (64, 128), 1) < 64
    first = jnp.where(left, top, lanes_swapped(low))
    second = jnp.where(left, lanes_swapped(top), low)
    return first.astype(jnp.bfloat16), second.astype(jnp.bfloat16)


def join_pair(first, second):
    first, second = first.astype(jnp.float32), second.astype(jnp.float32)
    left = lax.broadcasted_iota(jnp.int32, (64, 128), 1) < 64
    top = jnp.where(left, first, lanes_swapped(second))
    low = jnp.where(left, lanes_swapped(first), second)
    return top.astype(jnp.bfloat16), low.astype(jnp.bfloat16)


def pack_rows(block):
    return jnp.concatenate([block[0:64], block[64:128]], axis=1)


class Group:
    def __init__(self):
        self.known = False
        self.s, self.y, self.z, self.c, self.t = (lax.axis_index(a) for a in "syzct")
        self.micro = lax.rem(self.s + self.t, 2)
        y, z = lax.rem(self.y, 2), lax.rem(self.z, 2)
        self.me = y * 8 + z * 4 + self.c * 2 + self.t
        self.active = jnp.logical_or(self.c == 0, lax.rem(y + z + self.t, 2) == 0)
        self.head = jnp.where(self.c == 0, y * 4 + z * 2 + self.t, 8 + y * 2 + z)

    def member(self, index):
        t = lax.rem(index, 2)
        y = lax.div(self.y, 2) * 2 + lax.div(index, 8)
        z = lax.div(self.z, 2) * 2 + lax.rem(lax.div(index, 4), 2)
        return (lax.rem(self.micro + t, 2), y, z, lax.rem(lax.div(index, 2), 2), t)

    def holder(self, head):
        late = head - 8
        y, z = lax.div(late, 2), lax.rem(late, 2)
        return jnp.where(
            head < 8, lax.div(head, 4) * 8 + lax.rem(lax.div(head, 2), 2) * 4 + lax.rem(head, 2),
            y * 8 + z * 4 + 2 + lax.rem(y + z, 2))

    def greet(self):
        barrier = pltpu.get_barrier_semaphore()

        @pl.loop(1, 16)
        def _(n):
            pl.semaphore_signal(barrier, inc=1, device_id=self.member(lax.rem(self.me + n, 16)), device_id_type=MESH)

    def met(self):
        if self.known:
            return
        self.known = True
        pl.semaphore_wait(pltpu.get_barrier_semaphore(), 15)


def out_to_heads(group, packed, landed, send_sems, recv_sems):
    @pl.loop(0, 12)
    def _(n):
        head = lax.rem(group.me + n, 12)
        target = group.holder(head)

        @pl.when(target != group.me)
        def _():
            pltpu.make_async_remote_copy(
                src_ref=packed.at[head], dst_ref=landed.at[group.me], send_sem=send_sems.at[head],
                recv_sem=recv_sems.at[group.me], device_id=group.member(target), device_id_type=MESH).start()

    @pl.when(group.active)
    def _():
        landed[group.me] = packed[group.head]


def await_member(group, packed, landed, send_sems, recv_sems, index):
    @pl.when(group.me != index)
    def _():
        pltpu.make_async_remote_copy(
            src_ref=packed.at[0], dst_ref=landed.at[index], send_sem=send_sems.at[0],
            recv_sem=recv_sems.at[index], device_id=group.member(index), device_id_type=MESH).wait_recv()


def sent_to_heads(group, packed, landed, send_sems, recv_sems):
    @pl.loop(0, 12)
    def _(head):
        @pl.when(group.holder(head) != group.me)
        def _():
            pltpu.make_async_remote_copy(
                src_ref=packed.at[head], dst_ref=landed.at[group.me], send_sem=send_sems.at[head],
                recv_sem=recv_sems.at[group.me], device_id=group.member(group.holder(head)),
                device_id_type=MESH).wait_send()


def back_to_member(group, packed, landed, send_sems, recv_sems, index):
    @pl.when(group.me != index)
    def _():
        pltpu.make_async_remote_copy(
            src_ref=packed.at[index], dst_ref=landed.at[group.head], send_sem=send_sems.at[index],
            recv_sem=recv_sems.at[group.head], device_id=group.member(index), device_id_type=MESH).start()

    @pl.when(group.me == index)
    def _():
        landed[group.head] = packed[index]


def finish_back(group, packed, landed, send_sems, recv_sems):
    @pl.when(group.active)
    def _():
        @pl.loop(0, 16)
        def _(index):
            @pl.when(group.me != index)
            def _():
                pltpu.make_async_remote_copy(
                    src_ref=packed.at[index], dst_ref=landed.at[group.head], send_sem=send_sems.at[index],
                    recv_sem=recv_sems.at[group.head], device_id=group.member(index),
                    device_id_type=MESH).wait_send()

    @pl.loop(0, 12)
    def _(head):
        holder = group.holder(head)

        @pl.when(holder != group.me)
        def _():
            pltpu.make_async_remote_copy(
                src_ref=packed.at[0], dst_ref=landed.at[head], send_sem=send_sems.at[0],
                recv_sem=recv_sems.at[head], device_id=group.member(holder), device_id_type=MESH).wait_recv()


def dot_right(left, right):
    return lax.dot_general(left, right, (((1,), (1,)), ((), ())), preferred_element_type=jnp.float32)


def dot(left, right):
    return jnp.dot(left, right, preferred_element_type=jnp.float32)


def key_spans(block):
    own = slice(block * 256, block * 256 + 256)
    return ([(slice(0, block * 256), False)] if block else []) + [(own, True)]


def masked_scores(keys, query, masked):
    scores = dot_right(keys, query)
    if not masked:
        return scores
    key = lax.broadcasted_iota(jnp.int32, scores.shape, 0)
    return jnp.where(key <= lax.broadcasted_iota(jnp.int32, scores.shape, 1), scores, -1e30)


epsilon = 1e-05


def low(value):
    return value.astype(jnp.bfloat16)


def standard(values):
    centred = values - jnp.mean(values, axis=-1, keepdims=True)
    factor = lax.rsqrt(jnp.mean(centred * centred, axis=-1, keepdims=True) + epsilon)
    return centred * factor, factor


def norm_back(values, gain, grad):
    unit, factor = standard(values)
    scaled = grad * gain
    through = factor * (scaled - jnp.mean(scaled, axis=-1, keepdims=True)
                        - unit * jnp.mean(scaled * unit, axis=-1, keepdims=True))
    return through, jnp.sum(grad * unit, axis=0, keepdims=True), jnp.sum(grad, axis=0, keepdims=True)


def normal_share(values):
    return 0.5 * (1.0 + lax.erf(values * 0.7071067811865476))


class Weights:
    def __init__(self, source, held, sems):
        self.source, self.held, self.sems, self.copies = source, held, sems, {}

    def load(self, layer, part, half):
        if layer is None:
            return
        for unit in (2 * part, 2 * part + 1):
            copy = pltpu.make_async_copy(
                self.source.at[unit // 6, unit % 3, half * 2 + unit // 3 % 2, :, pl.ds(layer * 384, 384)],
                self.held.at[part, half, :, pl.ds(unit % 2 * 384, 384)], self.sems.at[unit * 2 + half])
            copy.start()
            self.copies[unit, half] = copy

    def ready(self, part, half):
        for unit in (2 * part, 2 * part + 1):
            copy = self.copies.pop((unit, half), None)
            if copy is not None:
                copy.wait()

    def __call__(self, part, half, columns=slice(0, 768)):
        self.ready(part, half)
        return self.held[part, half, :, columns]


def forward_layer(group, weights, following, x_ref, rows_ref, out_ref,
                  normed_ref, mixed_ref, heads_ref, total_ref, hidden_ref, normed_two_ref, pre_ref, active_ref,
                  packed, landed, back, home, value_turned, send_a, recv_a, send_b, recv_b):
    entering = x_ref[...].astype(jnp.float32)
    rows = [rows_ref[n:n + 1, :] for n in range(12)]
    normed = low(standard(entering)[0] * rows[0] + rows[1])
    normed_ref[...] = normed

    def pack(kind, half, values):
        for pair in range(3):
            first, second = split_pair(low(values[:, pair * 128:pair * 128 + 128]))
            packed[half * 6 + 2 * pair, kind * 64:kind * 64 + 64] = first
            packed[half * 6 + 2 * pair + 1, kind * 64:kind * 64 + 64] = second
    for half in range(2):
        both = dot(normed, weights(0, half))
        cut = slice(half * 384, half * 384 + 384)
        pack(0, half, (both[:, EARLY] + rows[6][:, cut]) * 0.125)
        pack(1, half, both[:, LATE])
        pack(2, half, dot(normed, weights(1, half, EARLY)) + rows[7][:, cut])
        weights.load(following, 0, half)
    group.met()
    out_to_heads(group, packed, landed, send_a, recv_a)

    for block in range(8):
        @pl.when(group.active)
        def _():
            for index in (2 * block, 2 * block + 1):
                await_member(group, packed, landed, send_a, recv_a, index)
                for n in range(3):
                    tile = landed[index, n * 64:n * 64 + 64]
                    heads_ref[n, index * 128:index * 128 + 64] = tile[:, 0:64]
                    heads_ref[n, index * 128 + 64:index * 128 + 128] = tile[:, 64:128]
            own = slice(block * 256, block * 256 + 256)
            value_turned[:, own] = heads_ref[2, own].T
            spans = key_spans(block)
            scores = [masked_scores(heads_ref[1, keys], heads_ref[0, own], masked) for keys, masked in spans]
            largest = functools.reduce(jnp.maximum, [jnp.max(part, axis=0, keepdims=True) for part in scores])
            shares = [jnp.exp(part - largest) for part in scores]
            total = sum(jnp.sum(part, axis=0, keepdims=True) for part in shares)
            total_ref[block:block + 1, :] = largest + jnp.log(total)
            mixed = sum(dot(value_turned[:, keys], low(part)) for (keys, _), part in zip(spans, shares)) / total
            mixed = mixed.T
            for n, index in enumerate((2 * block, 2 * block + 1)):
                back[index] = low(pack_rows(mixed[n * 128:n * 128 + 128]))
                back_to_member(group, back, home, send_b, recv_b, index)

    sent_to_heads(group, packed, landed, send_a, recv_a)
    finish_back(group, back, home, send_b, recv_b)
    for pair in range(6):
        mixed_ref[0:64, pair * 128:pair * 128 + 128], mixed_ref[64:128, pair * 128:pair * 128 + 128] = join_pair(
            home[2 * pair], home[2 * pair + 1])
    hidden = entering + rows[2]
    for half in range(2):
        hidden += dot_right(mixed_ref[:, half * 384:half * 384 + 384], weights(1, half, LATE))
        weights.load(following, 1, half)
    hidden_ref[...] = hidden
    normed_two = low(standard(hidden)[0] * rows[3] + rows[4])
    normed_two_ref[...] = normed_two
    leaving = hidden + rows[5]
    for half in range(2):
        for n in range(2):
            cut = slice((half * 2 + n) * 768, (half * 2 + n) * 768 + 768)
            pre = dot(normed_two, weights(2 + n, half)) + rows[8 + half * 2 + n]
            pre_ref[:, cut] = pre
            active = low(pre * normal_share(pre))
            active_ref[:, cut] = active
            leaving += dot_right(active, weights(4 + n, half))
            weights.load(following, 2 + n, half)
            weights.load(following, 4 + n, half)
    out_ref[...] = low(leaving)


def tiles(*shape):
    return pltpu.VMEM(shape, jnp.bfloat16)


def shapes(kind, *all_shapes):
    return tuple(jax.ShapeDtypeStruct(shape, kind) for shape in all_shapes)


def backward_layer(group, weights, following, arriving_ref, x_ref, rows_ref, out_ref, sums_ref, left_ref, right_ref,
                   normed_ref, mixed_ref, heads_ref, total_ref, hidden_ref, normed_two_ref, pre_ref, active_ref,
                   packed, landed, back, home, grad_heads, key_turned, key_sum, value_sum,
                   grad_pre, left_out, right_out, send_a, recv_a, send_b, recv_b, pair_sems):
    rows = [rows_ref[n:n + 1, :] for n in range(12)]

    def role(core, own, other, value):
        @pl.when(group.c == core)
        def _():
            own[...] = value

        @pl.when(group.c != core)
        def _():
            other[...] = value

    def left_role(core, n, value):
        role(core, left_ref.at[n, 0:128], left_out.at[n], value)

    def right_role(core, n, half, value):
        role(core, right_ref.at[n, half, 0:128], right_out.at[n, half], value)

    def to_sibling(n, source, target):
        return pltpu.make_async_remote_copy(
            src_ref=source, dst_ref=target, send_sem=pair_sems.at[n], recv_sem=pair_sems.at[n + 3],
            device_id=(group.s, group.y, group.z, 1 - group.c, group.t), device_id_type=MESH)

    arriving = arriving_ref[...]
    carried = arriving.astype(jnp.float32)
    sums_ref[5:6, :] = jnp.sum(carried, axis=0, keepdims=True)
    grad_normed_two = jnp.zeros((128, 768), jnp.float32)
    for half in range(2):
        for n in range(2):
            place = half * 2 + n
            cut = slice(place * 768, place * 768 + 768)
            pre = pre_ref[:, cut]
            slope = normal_share(pre) + pre * (jnp.exp(pre * pre * -0.5) * 0.3989422804014327)
            grad = low(dot(arriving, weights(4 + n, half)) * slope)
            grad_pre[:, cut] = grad
            sums_ref[8 + place:9 + place, :] = jnp.sum(grad.astype(jnp.float32), axis=0, keepdims=True)
            grad_normed_two += dot_right(grad, weights(2 + n, half))
            weights.load(following, 4 + n, half)
            weights.load(following, 2 + n, half)
    hidden = hidden_ref[...]
    through, gain, shift = norm_back(hidden, rows[3], grad_normed_two)
    sums_ref[3:4, :], sums_ref[4:5, :] = gain, shift
    grad_hidden = carried + through
    hidden_low = low(grad_hidden)
    sums_ref[2:3, :] = jnp.sum(hidden_low.astype(jnp.float32), axis=0, keepdims=True)
    for half in range(2):
        grad_mixed = low(dot(hidden_low, weights(1, half, LATE)))
        for pair in range(3):
            packed[half * 6 + 2 * pair], packed[half * 6 + 2 * pair + 1] = split_pair(
                grad_mixed[:, pair * 128:pair * 128 + 128])
    out_to_heads(group, packed, landed, send_a, recv_a)

    normed, normed_two = normed_ref[...], normed_two_ref[...]
    for n, value in enumerate((normed, normed, hidden_low, normed_two)):
        left_role(0, n, value)
    for n, value in enumerate((normed_two, arriving, arriving, arriving)):
        left_role(1, n, value)
    left_copy = to_sibling(0, left_out, left_ref.at[:, 128:256])
    left_copy.start()
    for half in range(2):
        def columns(n):
            return slice(half * 1536 + n * 384, half * 1536 + n * 384 + 384)
        right_role(0, 3, half, mixed_ref[:, half * 384:half * 384 + 384])
        for n in range(2):
            right_role(0, 4 + n, half, grad_pre[:, columns(n)])
            right_role(1, n, half, grad_pre[:, columns(2 + n)])
        for n in range(4):
            right_role(1, 2 + n, half, active_ref[:, columns(n)])

    early_copy = to_sibling(2, right_out.at[3:6], right_ref.at[3:6, :, 128:256])
    early_copy.start()

    @pl.when(group.active)
    def _():
        key_turned[...] = heads_ref[1].T

    for block in reversed(range(8)):
        @pl.when(group.active)
        def _():
            for index in (2 * block, 2 * block + 1):
                await_member(group, packed, landed, send_a, recv_a, index)
                tile = landed[index]
                grad_heads[index * 128:index * 128 + 64] = tile[:, 0:64]
                grad_heads[index * 128 + 64:index * 128 + 128] = tile[:, 64:128]
            own = slice(block * 256, block * 256 + 256)
            query, grad = heads_ref[0, own], grad_heads[own]
            spans, shares, softs = key_spans(block), [], []
            for keys, masked in spans:
                shares.append(jnp.exp(masked_scores(heads_ref[1, keys], query, masked) - total_ref[block:block + 1, :]))
                softs.append(dot_right(heads_ref[2, keys], grad))
            dots = sum(jnp.sum(share * soft, axis=0, keepdims=True) for share, soft in zip(shares, softs))
            for_query = 0.0
            for (keys, _), share, soft in zip(spans, shares, softs):
                moved = low(share * (soft - dots))
                for_key, for_value = dot(moved, query), dot(low(share), grad)
                if block == 7:
                    key_sum[keys] = for_key
                    value_sum[keys] = for_value
                else:
                    key_sum[keys] = key_sum[keys] + for_key
                    value_sum[keys] = value_sum[keys] + for_value
                for_query += dot(key_turned[:, keys], moved)
            for_query = low(for_query.T).astype(jnp.float32) * 0.125
            for n, index in enumerate((2 * block, 2 * block + 1)):
                part = slice(index * 128, index * 128 + 128)
                back[index, 0:64] = low(pack_rows(for_query[n * 128:n * 128 + 128]))
                back[index, 64:128] = low(pack_rows(key_sum[part]))
                back[index, 128:192] = low(pack_rows(value_sum[part]))
                back_to_member(group, back, home, send_b, recv_b, index)

    sent_to_heads(group, packed, landed, send_a, recv_a)
    finish_back(group, back, home, send_b, recv_b)
    grad_normed = jnp.zeros((128, 768), jnp.float32)
    for half in range(2):
        def joined(kind):
            whole = []
            for pair in range(3):
                head = half * 6 + 2 * pair
                top, bottom = join_pair(home[head, kind * 64:kind * 64 + 64], home[head + 1, kind * 64:kind * 64 + 64])
                whole.append(jnp.concatenate([top, bottom], axis=0))
            return jnp.concatenate(whole, axis=1)
        grad_q, grad_k, grad_v = joined(0), joined(1), joined(2)
        cut = slice(half * 384, half * 384 + 384)
        sums_ref[6:7, cut] = jnp.sum(grad_q.astype(jnp.float32), axis=0, keepdims=True)
        sums_ref[7:8, cut] = jnp.sum(grad_v.astype(jnp.float32), axis=0, keepdims=True)
        for n, value in enumerate((grad_q, grad_k, grad_v)):
            right_role(0, n, half, value)
        grad_normed += dot_right(grad_q, weights(0, half, EARLY)) + dot_right(grad_k, weights(0, half, LATE))
        grad_normed += dot_right(grad_v, weights(1, half, EARLY))
        weights.load(following, 1, half)
        weights.load(following, 0, half)
    right_copy = to_sibling(1, right_out.at[0:3], right_ref.at[0:3, :, 128:256])
    right_copy.start()
    through, gain, shift = norm_back(x_ref[...].astype(jnp.float32), rows[0], grad_normed)
    sums_ref[0:1, :], sums_ref[1:2, :] = gain, shift
    out_ref[...] = low(grad_hidden + through)
    left_copy.wait()
    early_copy.wait()
    right_copy.wait()


def layers_kernel(tokens_ref, cotangent_ref, rows_ref, w_ref,
                  acts_0, acts_1, grads_0, grads_1, sums_0, sums_1, left_0, left_1, right_0, right_1,
                  held, w_sems, *refs):
    group = Group()
    group.greet()
    weights = Weights(w_ref, held, w_sems)
    for part in range(6):
        for half in range(2):
            weights.load(0, part, half)
    states, forward, backward, pair_sems = (refs[0:8], refs[8:16]), refs[16:25], refs[25:-1], refs[-1]
    forward_layer(group, weights, 1, tokens_ref, rows_ref.at[0], acts_0, *states[0], *forward)
    forward_layer(group, weights, None, acts_0, rows_ref.at[1], acts_1, *states[1], *forward)
    backward_layer(group, weights, 0, cotangent_ref, acts_0, rows_ref.at[1], grads_1, sums_1, left_1, right_1,
                   *states[1], *backward, pair_sems.at[1])
    backward_layer(group, weights, None, grads_1, tokens_ref, rows_ref.at[0], grads_0, sums_0, left_0, right_0,
                   *states[0], *backward, pair_sems.at[0])


def layers(tokens, cotangent, rows, gathered):
    vmem = pl.BlockSpec(memory_space=pltpu.VMEM)
    block = (128, 768)
    wide = lambda *shape: pltpu.VMEM(shape, jnp.float32)
    state = [
        tiles(*block), tiles(*block), tiles(3, 2048, 64), wide(8, 256), wide(*block), tiles(*block), wide(128, 3072),
        tiles(128, 3072)]
    sems = [pltpu.SemaphoreType.DMA((count,)) for count in (12, 16, 16, 12)]
    return pl.pallas_call(
        layers_kernel,
        out_shape=shapes(jnp.bfloat16, block, block, block, block) + shapes(jnp.float32, (12, 768), (12, 768))
        + shapes(jnp.bfloat16, (4, 256, 768), (4, 256, 768), (6, 2, 256, 384), (6, 2, 256, 384)),
        in_specs=[vmem, vmem, vmem, pl.BlockSpec(memory_space=pl.ANY)],
        out_specs=(vmem,) * 10,
        scratch_shapes=[tiles(6, 2, 768, 768), pltpu.SemaphoreType.DMA((24,))] + state + state + [
            tiles(12, 192, 128), tiles(16, 192, 128), tiles(16, 64, 128), tiles(12, 64, 128), tiles(64, 2048),
        ] + sems + [
            tiles(12, 64, 128), tiles(16, 64, 128), tiles(16, 192, 128), tiles(12, 192, 128), tiles(2048, 64), tiles(64, 2048),
            wide(2048, 64), wide(2048, 64), tiles(128, 3072), tiles(4, 128, 768), tiles(6, 2, 128, 384),
        ] + sems + [pltpu.SemaphoreType.DMA((2, 6))],
        compiler_params=pltpu.CompilerParams(collective_id=3, has_side_effects=True, vmem_limit_bytes=62 * 2**20),
        name="layers",
    )(tokens, cotangent, rows, gathered)


def on_device(tokens_in, cotangent, place, w_qkv, w_out, w_up, w_down, qv_bias, up_bias, vectors):
    shard = jnp.concatenate([
        w_qkv[0], w_out[0].T[None], w_up[0].reshape(24, 4, 384).transpose(1, 0, 2),
        w_down[0].reshape(4, 384, 24).transpose(0, 2, 1)]).astype(jnp.float32)
    device = jnp.arange(32, dtype=jnp.int32)
    y, z = device // 8, device // 2 % 4
    seat = ((y // 2) * 2 + z // 2) * 8 + (y % 2) * 4 + (z % 2) * 2 + device % 2
    order = jnp.sum(jnp.where(place[None, :] == seat[:, None], device[None, :], 0), axis=1)
    gathered, rows, tokens, arriving = start(order, tokens_in, cotangent, vectors, qv_bias, up_bias, shard)
    gathered = gathered.reshape(2, 3, 4, 768, 768)

    acts_zero, acts_one, grads_zero, grads_one, sums_zero, sums_one, *operands = layers(tokens, arriving, rows, gathered)
    left_zero, left_one, right_zero, right_one = operands
    seq, part = place // 8, place % 8
    holder = (seq // 2 * 2 + part // 4) * 8 + (seq % 2 * 2 + part // 2 % 2) * 2 + part % 2
    full, acts_out, grads_out, grad_vectors, grad_qv, grad_up_bias = end(
        holder, (acts_zero, acts_one), (grads_zero, grads_one), (sums_zero, sums_one), (left_zero, left_one), (right_zero, right_one))
    acts_out, grads_out = acts_out[None], grads_out[None]
    grad_qkv = full[None, 0:3]
    grad_out = full[3].T[None]
    grad_up = full[4:8].transpose(1, 0, 2).reshape(1, 24, 1536)
    grad_down = full[8:12].transpose(0, 2, 1).reshape(1, 1536, 24)

    grad_vectors, grad_qv = grad_vectors[None], grad_qv[None]
    return acts_out, grads_out, grad_qkv, grad_out, grad_up, grad_down, grad_qv, grad_up_bias, grad_vectors


def solution(mesh):
    fine = Mesh(mesh.devices.reshape(2, 4, 4, 2, 2), ("s", "y", "z", "c", "t"))
    dp = ("y", "z", "c")
    blocks = P(None, dp + ("t",), None)
    weights = (P("s", None, dp, "t"), P("s", "t", dp), P("s", dp, "t"), P("s", "t", dp))
    small = (P("s", None, "t"), P("s", "t"), P("s", None, None))
    rows = P("s", None, dp + ("t",), None)
    return jax.shard_map(
        on_device, mesh=fine,
        in_specs=(blocks, blocks, P()) + weights + small,
        out_specs=(rows, rows) + weights + small,
        check_vma=False)
```
